32 devices in a mesh: seq: 4 (over y, x), fsdp: 8 (over z, core).
Axes of the slice: x: 2, y: 2, z: 4, core: 2. Of those that a mesh axis runs over, the one named last changes fastest.
Arguments:
- tokens: bfloat16 [8, 2048, 1024], P('fsdp', 'seq'), may hold values from -17 to 17
- segments: int32 [8, 2048], P('fsdp'), may hold values from 0 to 10, as said below
- valid_mask: int32 [8, 2048], P('fsdp', 'seq'), may hold values 0 or 1
- norm_gains: float32 [2, 2, 1024], replicated, may hold values from 0.5 to 1.5
- head_gain: float32 [2, 128], replicated, may hold values from 0.5 to 1.5
- conv_weight: float32 [2, 4, 3072], replicated, may hold values from -3 to 3
- beta_weight: bfloat16 [2, 1024, 8], replicated, may hold values from -0.1875 to 0.1875
- qkv_weight: bfloat16 [2, 1024, 3072], P(None, 'fsdp'), may hold values from -0.1875 to 0.1875
- out_weight: bfloat16 [2, 1024, 1024], P(None, 'fsdp'), may hold values from -0.1875 to 0.1875
- gate_up_weight: bfloat16 [2, 1024, 5632], P(None, 'fsdp'), may hold values from -0.1875 to 0.1875
- down_weight: bfloat16 [2, 2816, 1024], P(None, 'fsdp'), may hold values from -0.109375 to 0.109375
- cotangent: bfloat16 [8, 2048, 1024], P('fsdp', 'seq'), may hold values from -17 to 17
Outputs:
- mixed: bfloat16 [8, 2048, 1024], P('fsdp', 'seq')
- d_tokens: float32 [8, 2048, 1024], P('fsdp', 'seq')
- d_norm_gains: float32 [2, 2, 1024], replicated
- d_head_gain: float32 [2, 128], replicated
- d_conv_weight: float32 [2, 4, 3072], replicated
- d_beta_weight: float32 [2, 1024, 8], replicated
- d_qkv_weight: float32 [2, 1024, 3072], P(None, 'fsdp')
- d_out_weight: float32 [2, 1024, 1024], P(None, 'fsdp')
- d_gate_up_weight: float32 [2, 1024, 5632], P(None, 'fsdp')
- d_down_weight: float32 [2, 2816, 1024], P(None, 'fsdp')
- rms_stats: float32 [2, 3], replicated
The draws below stay inside these ranges and needn't reach their ends.
Inputs may be any that keep to these rules, and one draw needn't show every extreme that they name: `segments`: segment numbers start at 0 and rise by one at each document boundary; documents run 200 to 1024 tokens, except the last of a sequence, which may be cut shorter.
All inputs are finite; a program needn't handle non-finite values. No bound on the sum of `valid_mask` on one device may be relied on, other than what follows from the above.
Results may differ from the reference program's by a relative error of at most 0.025.
Values may be sent and summed in bfloat16 or wider, within the bound.
No kernel may reach another device: no remote copies, remote signals or barrier semaphores. Data moves between devices by JAX's collectives and lax.ppermute only.
A program may use at most 384 MiB of HBM per device.

```python
from functools import partial
import jax
import jax.numpy as jnp
from jax import lax

D = 1024
H = 8
HD = 128
FF = 2816
KW = 4
STRETCH = 64
LAYERS = 2
SEQ_LEN = 2048
SEQS = 8


def row_scale(rise):
    place = (jnp.arange(SEQS)[:, None] * SEQ_LEN + jnp.arange(SEQ_LEN)[None, :]).astype(jnp.float32) / (SEQS * SEQ_LEN)
    return jnp.exp(jnp.log(rise) * place)[:, :, None]


def draw_tokens(key, part):
    key = jax.random.fold_in(key, 11)
    own_key = jax.random.fold_in(key, 0)
    base = jnp.clip(jax.random.normal(own_key, (SEQS, SEQ_LEN, D), jnp.float32), -4.0, 4.0)
    return (base * row_scale(3.0)).astype(jnp.bfloat16)


def draw_cotangent(key, part):
    key = jax.random.fold_in(key, 17)
    own_key = jax.random.fold_in(key, 0)
    base = jnp.clip(jax.random.normal(own_key, (SEQS, SEQ_LEN, D), jnp.float32), -4.0, 4.0)
    return (base * row_scale(3.0)).astype(jnp.bfloat16)


def draw_segments(key, part):
    key = jax.random.fold_in(key, 13)
    length_key, pick_key = jax.random.split(key)
    shortest = min(200, max(2, SEQ_LEN // 8))
    longest = min(2000, SEQ_LEN // 2)
    count_docs = SEQ_LEN // shortest + 1
    doc_lengths = jax.random.randint(length_key, (SEQS, count_docs), shortest, longest + 1)
    chosen = jax.random.randint(pick_key, (), 0, SEQS)
    picked_row = (jnp.arange(SEQS, dtype=jnp.int32) == chosen)[:, None]
    doc_lengths = jnp.where(picked_row, jnp.full_like(doc_lengths, shortest), doc_lengths)
    bounds = jnp.cumsum(doc_lengths, axis=1)
    place = jnp.arange(SEQ_LEN, dtype=jnp.int32)[None, :, None]
    return jnp.sum((place >= bounds[:, None, :]).astype(jnp.int32), axis=2)


def place_ends(drawn, rng, low, largest):
    longest = drawn.shape.index(max(drawn.shape))
    spots = []
    for shift in (0, 1):
        where = [jax.random.randint(jax.random.fold_in(rng, axis), (), 0, length) for axis, length in enumerate(drawn.shape)]
        where[longest] = (where[longest] + shift) % drawn.shape[longest]
        spots.append(tuple(where))
    return drawn.at[spots[0]].set(low).at[spots[1]].set(largest)


def block_levels(stream_key, dims, shards, low, largest):
    def one(axis_at, shards_of):
        heights = jax.random.uniform(jax.random.fold_in(jax.random.fold_in(stream_key, 6), axis_at), (shards_of,), jnp.float32, low / len(shards), largest / len(shards))
        return jnp.repeat(jnp.exp(heights), dims[axis_at] // shards_of).reshape((-1,) + (1,) * (len(dims) - axis_at - 1))

    factor_of = one(*shards[0])
    for cut in shards[1:]:
        factor_of = factor_of * one(*cut)
    return factor_of


def bell_draw(stream_key, dims, deviation, limit, shards=(), held_as=jnp.bfloat16):
    loudness = block_levels(stream_key, dims, shards, -0.22, 0.18) if shards else 1.0
    array = jax.random.normal(stream_key, dims, jnp.float32) * deviation * loudness
    return jnp.minimum(jnp.maximum(array, -limit), limit).astype(held_as)


def setup_inputs(seed: int = 0) -> dict:
    key_of = jax.random.split(jax.random.key(seed), 13)
    return {
        "tokens": draw_tokens(jax.random.fold_in(key_of[12], 71), 0),
        "segments": draw_segments(jax.random.fold_in(key_of[12], 71), 0),
        "valid_mask": place_ends((jax.random.randint(key_of[2], (SEQS, SEQ_LEN), 0, 4) < 3).astype(jnp.int32), jax.random.fold_in(key_of[2], 1), 0, 1),
        "norm_gains": jnp.clip(1.0 + 0.1 * jax.random.normal(key_of[3], (LAYERS, 2, D), jnp.float32), 0.5, 1.5),
        "head_gain": jnp.clip(1.0 + 0.1 * jax.random.normal(key_of[4], (LAYERS, HD), jnp.float32), 0.5, 1.5),
        "conv_weight": bell_draw(key_of[5], (LAYERS, KW, 3 * D), KW ** -0.5, 3.0, (), jnp.float32),
        "beta_weight": bell_draw(key_of[6], (LAYERS, D, H), D ** -0.5, 0.1875),
        "qkv_weight": bell_draw(key_of[7], (LAYERS, D, 3 * D), D ** -0.5, 0.1875, ((1, 8),)),
        "out_weight": bell_draw(key_of[8], (LAYERS, D, D), D ** -0.5, 0.1875, ((1, 8),)),
        "gate_up_weight": bell_draw(key_of[9], (LAYERS, D, 2 * FF), D ** -0.5, 0.1875, ((1, 8),)),
        "down_weight": bell_draw(key_of[10], (LAYERS, FF, D), FF ** -0.5, 0.109375, ((1, 8),)),
        "cotangent": draw_cotangent(jax.random.fold_in(key_of[12], 71), 0),
    }


highest = lax.Precision.HIGHEST
epsilon_norm = 1e-05
epsilon_unit = 1e-06

@jax.custom_vjp
def low(v):
    return lax.optimization_barrier(v.astype(jnp.bfloat16)).astype(jnp.float32)

@jax.custom_vjp
def low_back(v):
    return v

def low_keep(v):
    return (low(v), None)

def low_pass(kept, grad):
    return (grad,)

def back_keep(v):
    return (v, None)

def back_low(kept, grad):
    return (low(grad),)
low.defvjp(low_keep, low_pass)
low_back.defvjp(back_keep, back_low)

def matmul(left, right):
    return jnp.dot(left.astype(jnp.float32), right.astype(jnp.float32), precision=highest, preferred_element_type=jnp.float32)

def root_norm(values, gain):
    return values * lax.rsqrt(lax.optimization_barrier(jnp.mean(values * values, axis=-1, keepdims=True)) + epsilon_norm) * gain

def short_filter(extended, doc_ext, filt):
    taps = filt.shape[0]
    row_count = extended.shape[0] - taps + 1
    current = doc_ext[taps - 1:]
    summed = jnp.zeros((row_count, extended.shape[1]), jnp.float32)
    for offset in range(taps):
        same_doc = (doc_ext[offset:offset + row_count] == current).astype(jnp.float32)
        summed = summed + filt[offset] * extended[offset:offset + row_count] * same_doc[:, None]
    return jax.nn.silu(summed)

def delta_head(query, keys, values, strength, doc_ids, block_size):
    length, head_width = query.shape
    query = query * lax.rsqrt(lax.optimization_barrier(jnp.sum(query * query, axis=-1, keepdims=True)) + epsilon_unit) * head_width ** (-0.5)
    keys = keys * lax.rsqrt(lax.optimization_barrier(jnp.sum(keys * keys, axis=-1, keepdims=True)) + epsilon_unit)
    blocks = length // block_size
    ends = doc_ids[block_size - 1::block_size]
    before = jnp.concatenate([jnp.full((1,), -1, jnp.int32), ends[:blocks - 1]])
    row_index = lax.broadcasted_iota(jnp.int32, (block_size, block_size), 0)
    col_index = lax.broadcasted_iota(jnp.int32, (block_size, block_size), 1)
    identity = jnp.eye(block_size, dtype=jnp.float32)

    def advance(memory, block_items):
        query_b, keys_b, values_b, strength_b, doc_b, prior_doc = block_items
        same_doc = doc_b[:, None] == doc_b[None, :]
        lower_mask = (same_doc & (col_index < row_index)).astype(jnp.float32)
        upto_mask = (same_doc & (col_index <= row_index)).astype(jnp.float32)
        carry_on = (doc_b == prior_doc).astype(jnp.float32)
        tail_doc = (doc_b == doc_b[block_size - 1]).astype(jnp.float32)
        keys_scaled = keys_b * strength_b[:, None]
        system = identity + matmul(keys_scaled, keys_b.T) * lower_mask
        solved = jax.scipy.linalg.solve_triangular(system, jnp.concatenate([keys_scaled, values_b * strength_b[:, None]], axis=1), lower=True)
        key_mix = solved[:, :head_width]
        value_mix = solved[:, head_width:]
        deltas = value_mix - carry_on[:, None] * matmul(key_mix, memory)
        output = carry_on[:, None] * matmul(query_b, memory) + matmul(matmul(query_b, keys_b.T) * upto_mask, deltas)
        memory = carry_on[block_size - 1] * memory + matmul(keys_b.T, tail_doc[:, None] * deltas)
        return (memory, output)
    block_items = (query.reshape(blocks, block_size, head_width), keys.reshape(blocks, block_size, head_width), values.reshape(blocks, block_size, head_width), strength.reshape(blocks, block_size), doc_ids.reshape(blocks, block_size), before)
    last_memory, outputs = lax.scan(jax.checkpoint(advance), jnp.zeros((head_width, head_width), jnp.float32), block_items)
    return outputs.reshape(length, head_width)

def sequence_forward(stream, doc_ids, valid_rows, weights_all):
    norm_gains, head_gain, conv_weight, beta_weight, qkv_weight, out_weight, gate_up_weight, down_weight = weights_all
    doc_ext = jnp.concatenate([jnp.full((KW - 1,), -1, jnp.int32), doc_ids])
    square_sums = []
    for layer_at in range(LAYERS):
        square_sums.append(jnp.sum(lax.optimization_barrier(jnp.sum(stream * stream, axis=-1)) * valid_rows))
        normed = low(root_norm(stream, norm_gains[layer_at, 0]))
        projected = low_back(low(matmul(normed, qkv_weight[layer_at])))
        logits = low_back(low(matmul(normed, beta_weight[layer_at])))
        extended = jnp.concatenate([jnp.zeros((KW - 1, 3 * D), jnp.float32), projected], axis=0)
        filtered = low_back(low(short_filter(extended, doc_ext, conv_weight[layer_at])))
        split_heads = filtered.reshape(SEQ_LEN, 3, H, HD)
        mixed_heads = jax.vmap(partial(delta_head, doc_ids=doc_ids, block_size=STRETCH), in_axes=1, out_axes=1)(split_heads[:, 0], split_heads[:, 1], split_heads[:, 2], jax.nn.sigmoid(logits))
        head_out = low_back(low(root_norm(mixed_heads, head_gain[layer_at]))).reshape(SEQ_LEN, D)
        branch = low_back(matmul(head_out, out_weight[layer_at]))
        square_sums.append(jnp.sum(lax.optimization_barrier(jnp.sum(branch * branch, axis=-1)) * valid_rows))
        stream = stream + branch
        normed = low(root_norm(stream, norm_gains[layer_at, 1]))
        gate_up = low_back(matmul(normed, gate_up_weight[layer_at]))
        activated = low(jax.nn.silu(gate_up[:, :FF]) * gate_up[:, FF:])
        branch = low_back(matmul(activated, down_weight[layer_at]))
        square_sums.append(jnp.sum(lax.optimization_barrier(jnp.sum(branch * branch, axis=-1)) * valid_rows))
        stream = stream + branch
    return (stream, jnp.stack(square_sums))

def reference(tokens, segments, valid_mask, norm_gains, head_gain, conv_weight, beta_weight, qkv_weight, out_weight, gate_up_weight, down_weight, cotangent):
    valid_rows = valid_mask.astype(jnp.float32)
    weights_all = tuple((member.astype(jnp.float32) for member in (norm_gains, head_gain, conv_weight, beta_weight, qkv_weight, out_weight, gate_up_weight, down_weight)))

    def forward(inputs, weights_now):

        def one_sequence(block_items):
            stream, doc_ids, valid_one = block_items
            return jax.checkpoint(sequence_forward)(stream, doc_ids, valid_one, weights_now)
        streams, square_sums = lax.map(one_sequence, (inputs, segments, valid_rows))
        return (streams, lax.optimization_barrier(jnp.sum(square_sums, axis=0)))
    result, pullback, square_sums = jax.vjp(forward, tokens.astype(jnp.float32), weights_all, has_aux=True)
    gradient_in, gradients = pullback(cotangent.astype(jnp.float32) * valid_rows[:, :, None])
    valid_total = jnp.maximum(jnp.sum(valid_rows), 1.0)
    rms_stats = jnp.sqrt(square_sums / (valid_total * D)).reshape(LAYERS, 3)
    return (result.astype(jnp.bfloat16), gradient_in, gradients[0], gradients[1], gradients[2], gradients[3], gradients[4], gradients[5], gradients[6], gradients[7], rms_stats)
```

```python
from functools import partial
import jax
import jax.numpy as jnp
from jax import lax
from jax.experimental import pallas as pl
from jax.experimental.pallas import tpu as pltpu
from jax.sharding import PartitionSpec as P

D = 1024
H = 8
HD = 128
KW = 4
CHUNK = 128
HALO = 8
f32 = jnp.float32
bf16 = jnp.bfloat16
EPS_NORM = 1e-05
EPS_UNIT = 1e-06
VMEM_LIMIT = 48 * 1024 * 1024


def dot_nn(a, b):
    return lax.dot_general(a.astype(bf16), b.astype(bf16), (((1,), (0,)), ((), ())), preferred_element_type=f32)


def dot_nt(a, b):
    return lax.dot_general(a.astype(bf16), b.astype(bf16), (((1,), (1,)), ((), ())), preferred_element_type=f32)


def dot_tn(a, b):
    return lax.dot_general(a.astype(bf16), b.astype(bf16), (((0,), (0,)), ((), ())), preferred_element_type=f32)


def sigmoid(x):
    return 1.0 / (1.0 + jnp.exp(-x))


def conv_masks(dcol_ref, rows):
    here = dcol_ref[pl.ds(HALO, rows), :]
    return [
        jnp.broadcast_to((dcol_ref[pl.ds(HALO - KW + 1 + i, rows), :] == here).astype(f32), (rows, HD))
        for i in range(KW - 1)
    ]


def conv_sum(x_ref, halo_ref, taps_ref, masks, ext):
    rows = x_ref.shape[0]
    ext[pl.ds(0, HALO), :] = halo_ref[...].astype(f32)
    ext[pl.ds(HALO, rows), :] = x_ref[...].astype(f32)
    total = taps_ref[pl.ds(KW - 1, 1), :] * ext[pl.ds(HALO, rows), :]
    for i in range(KW - 1):
        total = total + taps_ref[pl.ds(i, 1), :] * ext[pl.ds(HALO - KW + 1 + i, rows), :] * masks[i]
    return total


def low(x):
    return x.astype(bf16).astype(f32)


def unit_scale(x):
    return lax.rsqrt(jnp.sum(x * x, axis=-1, keepdims=True) + EPS_UNIT)


def head_column(table, head):
    lane = lax.broadcasted_iota(jnp.int32, table.shape, 1)
    return jnp.sum(jnp.where(lane == head, table, 0.0), axis=1, keepdims=True)


def chunk_marks(dcol_ref, c):
    at = HALO + c * CHUNK
    docs = dcol_ref[pl.ds(at, CHUNK), :]
    prior = dcol_ref[pl.ds(at - 1, 1), :]
    last = dcol_ref[pl.ds(at + CHUNK - 1, 1), :]
    carry = (docs == prior).astype(f32)
    tail = (docs == last).astype(f32)
    carry_last = (last == prior).astype(f32)
    return docs, carry, tail, carry_last


def tri_index():
    row = lax.broadcasted_iota(jnp.int32, (CHUNK, CHUNK), 0)
    col = lax.broadcasted_iota(jnp.int32, (CHUNK, CHUNK), 1)
    return row, col


def inverses(systems, differ):
    row, col = tri_index()
    eye = (row == col).astype(f32)
    found = [eye - jnp.where(differ == 1, low_part, 0.0) for low_part in systems]
    step = 2
    while step < CHUNK:
        side = (differ >= step) & (differ < 2 * step)
        lows = [x.astype(bf16) for x in found]
        inner = [dot_nn(jnp.where(side, s, 0.0), x) for s, x in zip(systems, lows)]
        outer = [dot_nn(x, y) for x, y in zip(lows, inner)]
        found = [x - y for x, y in zip(found, outer)]
        step *= 2
    return found


def fwd_local_kernel(
    q_ref, k_ref, v_ref, hq_ref, hk_ref, hv_ref, tq_ref, tk_ref, tv_ref, lg_ref, dcol_ref, drow_ref,
    qn_ref, kn_ref, tinv_ref, wu_ref, gain_ref, pre_ref, total_ref, ext,
):
    head = pl.program_id(0)
    rows = q_ref.shape[0]
    chunks = rows // CHUNK
    masks = conv_masks(dcol_ref, rows)

    def filtered(x, halo, taps):
        s = conv_sum(x, halo, taps, masks, ext)
        return low(s * sigmoid(s))

    query = filtered(q_ref, hq_ref, tq_ref)
    qn_ref[...] = (query * (unit_scale(query) * HD**-0.5)).astype(bf16)
    keys = filtered(k_ref, hk_ref, tk_ref)
    kn = keys * unit_scale(keys)
    kn_ref[...] = kn.astype(bf16)
    values = filtered(v_ref, hv_ref, tv_ref)
    beta = sigmoid(head_column(lg_ref[...].astype(f32), head))
    kb = beta * kn
    vb = beta * values
    row, col = tri_index()
    differ = row ^ col
    marks = [chunk_marks(dcol_ref, c) for c in range(chunks)]
    cut = lambda x, c: x[c * CHUNK : (c + 1) * CHUNK]
    systems = []
    for c in range(chunks):
        docs = marks[c][0]
        keep = (docs == drow_ref[pl.ds(c, 1), :]) & (col < row)
        systems.append(jnp.where(keep, dot_nt(cut(kb, c), cut(kn, c)), 0.0))
    found = inverses(systems, differ)
    both = [
        dot_nn(found[c], jnp.concatenate([cut(kb, c), cut(vb, c)], axis=1)) for c in range(chunks)
    ]
    state = None
    eye = (row == col).astype(f32)
    for c in range(chunks):
        tinv_ref[0, pl.ds(c * CHUNK, CHUNK), :] = found[c].astype(bf16)
        _, carry, tail, carry_last = marks[c]
        w, u = both[c][:, :HD], both[c][:, HD:]
        wu_ref[0, pl.ds(c * CHUNK, CHUNK), :] = both[c].astype(bf16)
        step = dot_tn(cut(kn, c) * tail, jnp.concatenate([w * carry, u], axis=1))
        gain_ref[0, pl.ds(c * CHUNK, CHUNK), :] = step[:, :HD].astype(bf16)
        if c == 0:
            state = jnp.concatenate([eye, jnp.zeros_like(eye)], axis=1)
        pre_ref[0, pl.ds(c * CHUNK, CHUNK), :] = state.astype(bf16)
        moved = carry_last * state - dot_nn(step[:, :HD], state)
        state = jnp.concatenate([moved[:, :HD], moved[:, HD:] + step[:, HD:]], axis=1)
    total_ref[0] = state.astype(bf16)


def col_spec(rows, base):
    return pl.BlockSpec((rows, HD), lambda h: (0, base + h))


def full_spec(shape):
    return pl.BlockSpec(shape, lambda h: (0,) * len(shape))


def head_spec(shape):
    return pl.BlockSpec((1,) + shape, lambda h: (h,) + (0,) * len(shape))


def params():
    return pltpu.CompilerParams(vmem_limit_bytes=VMEM_LIMIT, dimension_semantics=("arbitrary",))


def cost(units, rows, traffic):
    return pl.CostEstimate(flops=2 * units * HD * HD * HD * H * (rows // CHUNK), bytes_accessed=traffic, transcendentals=0)


def fwd_local(projected, halo, taps, logits, dcol, drow):
    rows = projected.shape[0]
    chunks = rows // CHUNK
    sds = jax.ShapeDtypeStruct
    return pl.pallas_call(
        fwd_local_kernel,
        grid=(H,),
        in_specs=[col_spec(rows, 0), col_spec(rows, H), col_spec(rows, 2 * H)]
        + [col_spec(HALO, 0), col_spec(HALO, H), col_spec(HALO, 2 * H)]
        + [col_spec(KW, 0), col_spec(KW, H), col_spec(KW, 2 * H)]
        + [full_spec((rows, H)), full_spec((rows + HALO, 1)), full_spec((chunks, CHUNK))],
        out_specs=[
            col_spec(rows, 0),
            col_spec(rows, 0),
            head_spec((rows, CHUNK)),
            head_spec((rows, 2 * HD)),
            head_spec((rows, HD)),
            head_spec((rows, 2 * HD)),
            head_spec((HD, 2 * HD)),
        ],
        out_shape=[
            sds((rows, D), bf16),
            sds((rows, D), bf16),
            sds((H, rows, CHUNK), bf16),
            sds((H, rows, 2 * HD), bf16),
            sds((H, rows, HD), bf16),
            sds((H, rows, 2 * HD), bf16),
            sds((H, HD, 2 * HD), bf16),
        ],
        scratch_shapes=[pltpu.VMEM((rows + HALO, HD), f32)],
        compiler_params=params(),
        cost_estimate=cost(60, rows, rows * D * 24),
        name="delta_local",
    )(*([projected] * 3 + [halo] * 3 + [taps] * 3 + [logits, dcol, drow]))


def fwd_read_kernel(qn_ref, kn_ref, wu_ref, dcol_ref, drow_ref, r_ref, o_ref):
    rows = qn_ref.shape[0]
    row, col = tri_index()
    for c in range(rows // CHUNK):
        at = pl.ds(c * CHUNK, CHUNK)
        docs, carry, _, _ = chunk_marks(dcol_ref, c)
        keep = (docs == drow_ref[pl.ds(c, 1), :]) & (col <= row)
        part = jnp.where(keep, dot_nt(qn_ref[at, :], kn_ref[at, :]), 0.0)
        w = wu_ref[0, at, :HD].astype(f32) * carry
        both = dot_nn(part, jnp.concatenate([w.astype(bf16), wu_ref[0, at, HD:]], axis=1))
        r_ref[at, :] = (qn_ref[at, :].astype(f32) * carry - both[:, :HD]).astype(bf16)
        o_ref[at, :] = both[:, HD:]


def fwd_read(qn, kn, wu, dcol, drow):
    rows = qn.shape[0]
    chunks = rows // CHUNK
    sds = jax.ShapeDtypeStruct
    return pl.pallas_call(
        fwd_read_kernel,
        grid=(H,),
        in_specs=[col_spec(rows, 0), col_spec(rows, 0), head_spec((rows, 2 * HD)), full_spec((rows + HALO, 1)), full_spec((chunks, CHUNK))],
        out_specs=[col_spec(rows, 0), col_spec(rows, 0)],
        out_shape=[sds((rows, D), bf16), sds((rows, D), f32)],
        compiler_params=params(),
        cost_estimate=cost(20, rows, rows * D * 14),
        name="delta_read",
    )(qn, kn, wu, dcol, drow)


def fwd_state_kernel(*refs):
    *near_refs, far_ref, pre_ref, r_ref, o_ref, gain_ref, state_ref, out_ref, head_ref = refs
    rows = r_ref.shape[0]
    state = far_ref[0].astype(f32)
    for near_ref in reversed(near_refs):
        state = dot_nn(near_ref[0, :, :HD], state) + near_ref[0, :, HD:].astype(f32)
    for c in range(rows // CHUNK):
        at = pl.ds(c * CHUNK, CHUNK)
        now = dot_nn(pre_ref[0, at, :HD], state) + pre_ref[0, at, HD:].astype(f32)
        state_ref[0, at, :] = now.astype(bf16)
        o = o_ref[at, :] + dot_nn(r_ref[at, :], now)
        out_ref[at, :] = o
        scale = lax.rsqrt(jnp.mean(o * o, axis=-1, keepdims=True) + EPS_NORM)
        head_ref[at, :] = (o * scale * gain_ref[...]).astype(bf16)


def fwd_state(nears, far, pre, r, o, gain):
    rows = r.shape[0]
    sds = jax.ShapeDtypeStruct
    return pl.pallas_call(
        fwd_state_kernel,
        grid=(H,),
        in_specs=[
            *[head_spec((HD, 2 * HD)) for _ in nears],
            head_spec((HD, HD)),
            head_spec((rows, 2 * HD)),
            col_spec(rows, 0),
            col_spec(rows, 0),
            full_spec((1, HD)),
        ],
        out_specs=[head_spec((rows, HD)), col_spec(rows, 0), col_spec(rows, 0)],
        out_shape=[sds((H, rows, HD), bf16), sds((rows, D), f32), sds((rows, D), bf16)],
        compiler_params=params(),
        cost_estimate=cost(10, rows, rows * D * 14),
        name="delta_state",
    )(*nears, far, pre, r, o, gain)


def bwd_local_kernel(dhead_ref, o_ref, r_ref, gain_ref, step_ref, dcol_ref, do_ref, dgain_ref, total_ref):
    rows = o_ref.shape[0]
    chunks = rows // CHUNK

    @pl.when(pl.program_id(0) == 0)
    def _():
        dgain_ref[...] = jnp.zeros_like(dgain_ref)

    o = o_ref[...]
    dy = dhead_ref[...].astype(f32)
    scale = lax.rsqrt(jnp.mean(o * o, axis=-1, keepdims=True) + EPS_NORM)
    x = o * scale
    dgain_ref[...] += jnp.sum(dy * x, axis=0, keepdims=True)
    dx = dy * gain_ref[...]
    do = scale * (dx - x * jnp.mean(dx * x, axis=-1, keepdims=True))
    do_ref[...] = do.astype(bf16)
    gives = [dot_tn(r_ref[pl.ds(c * CHUNK, CHUNK), :], do[c * CHUNK : (c + 1) * CHUNK]) for c in range(chunks)]
    state = jnp.zeros((HD, HD), f32)
    for c in reversed(range(chunks)):
        carry_last = chunk_marks(dcol_ref, c)[3]
        if c == chunks - 1:
            state = gives[c]
        else:
            state = carry_last * state - dot_tn(step_ref[0, pl.ds(c * CHUNK, CHUNK), :], state) + gives[c]
    total_ref[0] = state.astype(bf16)


def bwd_local(dhead, o, r, gain, step, dcol):
    rows = o.shape[0]
    sds = jax.ShapeDtypeStruct
    return pl.pallas_call(
        bwd_local_kernel,
        grid=(H,),
        in_specs=[col_spec(rows, 0), col_spec(rows, 0), col_spec(rows, 0), full_spec((1, HD)), head_spec((rows, HD)), full_spec((rows + HALO, 1))],
        out_specs=[col_spec(rows, 0), full_spec((1, HD)), head_spec((HD, HD))],
        out_shape=[sds((rows, D), bf16), sds((1, HD), f32), sds((H, HD, HD), bf16)],
        compiler_params=params(),
        cost_estimate=cost(12, rows, rows * D * 12),
        name="delta_back_local",
    )(dhead, o, r, gain, step, dcol)


def bwd_main_kernel(moves, *refs):
    later, refs = refs[: 2 * moves + 1], refs[2 * moves + 1 :]
    bwd_main_body(later, *refs)


def bwd_main_body(
    later, q_ref, k_ref, v_ref, hq_ref, hk_ref, hv_ref, tq_ref, tk_ref, tv_ref, lg_ref, dcol_ref, drow_ref,
    tinv_ref, wu_ref, step_ref, state_ref, r_ref, do_ref,
    dq_ref, dk_ref, dv_ref, rq_ref, rk_ref, rv_ref, cq_ref, ck_ref, cv_ref, dl_ref, ext, grad,
):
    head = pl.program_id(0)
    rows = q_ref.shape[0]
    chunks = rows // CHUNK
    masks = conv_masks(dcol_ref, rows)
    row, col = tri_index()
    cut = lambda x, c: x[c * CHUNK : (c + 1) * CHUNK]

    def filtered(x, halo, taps):
        s = conv_sum(x, halo, taps, masks, ext)
        gate = sigmoid(s)
        return low(s * gate), gate * (1.0 + s * (1.0 - gate))

    query, slope_q = filtered(q_ref, hq_ref, tq_ref)
    scale_q = unit_scale(query)
    qn = query * scale_q * HD**-0.5
    keys, slope_k = filtered(k_ref, hk_ref, tk_ref)
    scale_k = unit_scale(keys)
    kn = keys * scale_k
    values, slope_v = filtered(v_ref, hv_ref, tv_ref)
    beta = sigmoid(head_column(lg_ref[...].astype(f32), head))
    kb = beta * kn

    moves = len(later) // 2
    ds = later[-1][0].astype(f32)
    for i in reversed(range(moves)):
        ds = dot_tn(later[i][0], ds) + later[moves + i][0].astype(f32)
    marks = [chunk_marks(dcol_ref, c) for c in range(chunks)]
    leaving = [None] * chunks
    gives = [dot_tn(r_ref[pl.ds(c * CHUNK, CHUNK), :], do_ref[pl.ds(c * CHUNK, CHUNK), :]) for c in range(chunks)]
    for c in reversed(range(chunks)):
        leaving[c] = ds.astype(bf16)
        if c:
            ds = marks[c][3] * ds - dot_tn(step_ref[0, pl.ds(c * CHUNK, CHUNK), :], ds) + gives[c]

    dqs, dks, dvs, dbs = [], [], [], []
    for c in range(chunks):
        at = pl.ds(c * CHUNK, CHUNK)
        docs, carry, tail, _ = marks[c]
        same = docs == drow_ref[pl.ds(c, 1), :]
        q_c, k_c, kb_c = cut(qn, c).astype(bf16), cut(kn, c).astype(bf16), cut(kb, c).astype(bf16)
        do = do_ref[at, :]
        wu = wu_ref[0, at, :]
        state = state_ref[0, at, :]
        deltas = (wu[:, HD:].astype(f32) - carry * dot_nn(wu[:, :HD], state)).astype(bf16)
        part = jnp.where(same & (col <= row), dot_nt(q_c, k_c), 0.0)
        dd = dot_tn(part, do) + tail * dot_nn(k_c, leaving[c])
        dpart = jnp.where(same & (col <= row), dot_nt(do, deltas), 0.0)
        through = dot_nt(jnp.concatenate([do, dd.astype(bf16)], axis=0), state)
        dkf = dot_nt(deltas, leaving[c])
        dwu = dot_tn(tinv_ref[0, at, :], jnp.concatenate([-(carry * through[CHUNK:]), dd], axis=1))
        dlow = jnp.where(same & (col < row), -dot_nt(dwu, wu), 0.0)
        pair = jnp.concatenate([dpart.astype(bf16), dlow.astype(bf16)], axis=0)
        onto = dot_nn(pair, k_c)
        dqs.append(carry * through[:CHUNK] + onto[:CHUNK])
        dkb = dwu[:, :HD] + onto[CHUNK:]
        dvb = dwu[:, HD:]
        b_c = cut(beta, c)
        dks.append(dot_tn(pair, jnp.concatenate([q_c, kb_c], axis=0)) + tail * dkf + b_c * dkb)
        dvs.append(b_c * dvb)
        dbs.append(jnp.sum(dkb * cut(kn, c) + dvb * cut(values, c), axis=1, keepdims=True))

    join = lambda parts: jnp.concatenate(parts, axis=0)
    dqn = join(dqs) * HD**-0.5
    unit = query * scale_q
    dquery = scale_q * (dqn - unit * jnp.sum(dqn * unit, axis=-1, keepdims=True))
    dkn = join(dks)
    dkeys = scale_k * (dkn - kn * jnp.sum(dkn * kn, axis=-1, keepdims=True))
    dlogit = join(dbs) * beta * (1.0 - beta)
    lane = lax.broadcasted_iota(jnp.int32, (rows, H), 1)

    @pl.when(head == 0)
    def _():
        dl_ref[...] = jnp.zeros_like(dl_ref)

    dl_ref[...] = jnp.where(lane == head, dlogit, dl_ref[...].astype(f32)).astype(bf16)

    def conv_back(dfilt, slope, x_ref, halo_ref, taps_ref, out_ref, rim_ref, dtap_ref):
        ds_ = low(dfilt) * slope
        ext[pl.ds(0, HALO), :] = halo_ref[...].astype(f32)
        ext[pl.ds(HALO, rows), :] = x_ref[...].astype(f32)
        grad[...] = jnp.zeros_like(grad)
        dtap_ref[pl.ds(KW - 1, 1), :] = jnp.sum(ds_ * ext[pl.ds(HALO, rows), :], axis=0, keepdims=True)
        grad[pl.ds(HALO, rows), :] = ds_ * taps_ref[pl.ds(KW - 1, 1), :]
        for i in range(KW - 1):
            masked = ds_ * masks[i]
            place_i = pl.ds(HALO - KW + 1 + i, rows)
            dtap_ref[pl.ds(i, 1), :] = jnp.sum(masked * ext[place_i, :], axis=0, keepdims=True)
            grad[place_i, :] = grad[place_i, :] + masked * taps_ref[pl.ds(i, 1), :]
        rim_ref[...] = grad[pl.ds(0, HALO), :].astype(bf16)
        out_ref[...] = grad[pl.ds(HALO, rows), :].astype(out_ref.dtype)

    conv_back(dquery, slope_q, q_ref, hq_ref, tq_ref, dq_ref, rq_ref, cq_ref)
    conv_back(dkeys, slope_k, k_ref, hk_ref, tk_ref, dk_ref, rk_ref, ck_ref)
    conv_back(join(dvs), slope_v, v_ref, hv_ref, tv_ref, dv_ref, rv_ref, cv_ref)


def bwd_main(moves, gives, projected, halo, taps, logits, dcol, drow, tinv, wu, step, state, r, do):
    rows = projected.shape[0]
    chunks = rows // CHUNK
    sds = jax.ShapeDtypeStruct
    return pl.pallas_call(
        partial(bwd_main_kernel, len(moves)),
        grid=(H,),
        in_specs=[head_spec((HD, HD)) for _ in (*moves, *gives)]
        + [col_spec(rows, 0), col_spec(rows, H), col_spec(rows, 2 * H)]
        + [col_spec(HALO, 0), col_spec(HALO, H), col_spec(HALO, 2 * H)]
        + [col_spec(KW, 0), col_spec(KW, H), col_spec(KW, 2 * H)]
        + [full_spec((rows, H)), full_spec((rows + HALO, 1)), full_spec((chunks, CHUNK))]
        + [head_spec((rows, CHUNK)), head_spec((rows, 2 * HD)), head_spec((rows, HD)), head_spec((rows, HD))]
        + [col_spec(rows, 0), col_spec(rows, 0)],
        out_specs=[col_spec(rows, 0)] * 3 + [col_spec(HALO, 0)] * 3 + [col_spec(KW, 0)] * 3 + [full_spec((rows, H))],
        out_shape=[sds((rows, D), f32)] * 3 + [sds((HALO, D), bf16)] * 3 + [sds((KW, D), f32)] * 3 + [sds((rows, H), bf16)],
        scratch_shapes=[pltpu.VMEM((rows + HALO, HD), f32), pltpu.VMEM((rows + HALO, HD), f32)],
        compiler_params=params(),
        cost_estimate=cost(90, rows, rows * D * 40),
        name="delta_back",
    )(*moves, *gives, *([projected] * 3 + [halo] * 3 + [taps] * 3), logits, dcol, drow, tinv, wu, step, state, r, do)


epsilon_norm = EPS_NORM
LAYERS = 2


def shifted(block, axis, distance):
    devices = range(lax.axis_size(axis))
    route = [(i - distance, i) for i in devices if i - distance in devices]
    return lax.ppermute(block, axis, route)


def root_norm(values, gain):
    return (
        values * lax.rsqrt(jnp.mean(values * values, axis=-1, keepdims=True) + epsilon_norm) * gain
    )


def swiglu_act(gate_up):
    half_width = gate_up.shape[1] // 2
    return jax.nn.silu(gate_up[:, :half_width]) * gate_up[:, half_width:]


def contract_last(left, right):
    return lax.dot_general(
        left, right, (((1,), (1,)), ((), ())), preferred_element_type=jnp.float32
    )


def contract_first(left, right):
    return lax.dot_general(
        left, right, (((0,), (0,)), ((), ())), preferred_element_type=jnp.float32
    )


def fetch_rows(weights):
    return lax.all_gather(weights, "fsdp", axis=0, tiled=True)


def reduce_rows(left, right):
    return lax.psum_scatter(
        contract_first(left, right).astype(jnp.bfloat16), "fsdp", scatter_dimension=0, tiled=True
    )


def on_device(
    tokens,
    segments,
    valid_mask,
    norm_gains,
    head_gain,
    conv_weight,
    beta_weight,
    qkv_weight,
    out_weight,
    gate_up_weight,
    down_weight,
    cotangent,
):
    rows = tokens.shape[1]
    pieces = lax.axis_size("seq")
    doc_ids = segments[0]
    doc_pad = jnp.concatenate([jnp.full((HALO,), -1, jnp.int32), doc_ids])
    piece_start = lax.axis_index("seq") * rows
    dcol = lax.dynamic_slice_in_dim(doc_pad, piece_start, rows + HALO)
    drow = dcol[HALO:].reshape(rows // CHUNK, CHUNK)
    dcol = dcol[:, None]
    valid_rows = valid_mask[0].astype(jnp.float32)
    stream = tokens[0].astype(jnp.float32)
    square_sums = []
    stored = []
    for at in range(LAYERS):
        qkv_full = fetch_rows(qkv_weight[at])
        out_full = fetch_rows(out_weight[at])
        gate_up_full = fetch_rows(gate_up_weight[at])
        down_full = fetch_rows(down_weight[at])
        square_sums.append(jnp.sum(jnp.sum(stream * stream, axis=1) * valid_rows))
        normed_one, pull_one = jax.vjp(root_norm, stream, norm_gains[at, 0])
        normed_one = normed_one.astype(jnp.bfloat16)
        projected = jnp.dot(normed_one, qkv_full, preferred_element_type=jnp.float32).astype(bf16)
        logits = jnp.dot(normed_one, beta_weight[at], preferred_element_type=jnp.float32).astype(bf16)
        halo = shifted(projected[rows - HALO :], "seq", 1)
        qn, kn, tinv, wu, step, pre, total = fwd_local(
            projected, halo, conv_weight[at], logits, dcol, drow
        )
        nears = [shifted(total, "seq", d) for d in range(1, pieces - 1)]
        far = shifted(total[:, :, HD:], "seq", pieces - 1)
        moves = [shifted(total[:, :, :HD], "seq", -d) for d in range(1, pieces - 1)]
        reads, local_out = fwd_read(qn, kn, wu, dcol, drow)
        state, mixed, attended = fwd_state(nears, far, pre, reads, local_out, head_gain[at][None])
        branch = jnp.dot(attended, out_full, preferred_element_type=jnp.float32)
        square_sums.append(jnp.sum(jnp.sum(branch * branch, axis=1) * valid_rows))
        stream = stream + branch
        normed_two, pull_two = jax.vjp(root_norm, stream, norm_gains[at, 1])
        normed_two = normed_two.astype(jnp.bfloat16)
        gate_up = jnp.dot(normed_two, gate_up_full, preferred_element_type=jnp.float32)
        activated, pull_act = jax.vjp(swiglu_act, gate_up)
        activated = activated.astype(jnp.bfloat16)
        branch = jnp.dot(activated, down_full, preferred_element_type=jnp.float32)
        square_sums.append(jnp.sum(jnp.sum(branch * branch, axis=1) * valid_rows))
        stream = stream + branch
        stored.append(
            (
                qkv_full, out_full, gate_up_full, down_full, pull_one, normed_one, attended, pull_two, normed_two,
                pull_act, activated, moves, mixed,
                (projected, halo, conv_weight[at], logits, dcol, drow, tinv, wu, step, state, reads),
            )
        )
    stream_grad = cotangent[0].astype(jnp.float32) * valid_rows[:, None]
    gain_list = []
    head_list = []
    filter_list = []
    beta_list = []
    weight_list = []
    for at in reversed(range(LAYERS)):
        (
            qkv_full, out_full, gate_up_full, down_full, pull_one, normed_one, attended, pull_two, normed_two,
            pull_act, activated, moves, mixed, kept,
        ) = stored[at]
        step, reads = kept[8], kept[10]
        branch_low = stream_grad.astype(jnp.bfloat16)
        grad_down = reduce_rows(activated, branch_low)
        (grad_gate_up,) = pull_act(contract_last(branch_low, down_full))
        grad_gate_up = grad_gate_up.astype(jnp.bfloat16)
        grad_gate = reduce_rows(normed_two, grad_gate_up)
        grad_state, gain_two = pull_two(contract_last(grad_gate_up, gate_up_full))
        stream_grad = stream_grad + grad_state
        branch_low = stream_grad.astype(jnp.bfloat16)
        grad_out = reduce_rows(attended, branch_low)
        grad_heads = contract_last(branch_low, out_full).astype(jnp.bfloat16)
        grad_mixed, gain_head, total = bwd_local(
            grad_heads, mixed, reads, head_gain[at][None], step, dcol
        )
        gives = [shifted(total, "seq", -d) for d in range(1, pieces)]
        *parts, grad_logits = bwd_main(moves, gives, *kept, grad_mixed)
        rim = shifted(jnp.concatenate(parts[3:6], axis=1), "seq", -1).astype(f32)
        grad_filter = jnp.concatenate(parts[6:9], axis=1)
        grad_proj = jnp.concatenate(parts[:3], axis=1)
        grad_proj = jnp.concatenate(
            [grad_proj[: rows - HALO], grad_proj[rows - HALO :] + rim], axis=0
        ).astype(bf16)
        grad_qkv = reduce_rows(normed_one, grad_proj)
        grad_beta = contract_first(normed_one, grad_logits)
        grad_normed = contract_last(grad_proj, qkv_full) + contract_last(grad_logits, beta_weight[at])
        grad_state, gain_one = pull_one(grad_normed)
        stream_grad = stream_grad + grad_state
        weight_list.append(
            [lax.psum(grad, "seq").astype(f32) for grad in (grad_qkv, grad_out, grad_gate, grad_down)]
        )
        gain_list.append(jnp.stack([gain_one, gain_two]))
        head_list.append(gain_head[0])
        filter_list.append(grad_filter)
        beta_list.append(grad_beta)
    stats_sum, valid_count, gains_sum, head_sum, filter_sum, beta_sum = lax.psum(
        (
            jnp.stack(square_sums),
            jnp.sum(valid_rows),
            jnp.stack(gain_list[::-1]),
            jnp.stack(head_list[::-1]),
            jnp.stack(filter_list[::-1]),
            jnp.stack(beta_list[::-1]),
        ),
        ("seq", "fsdp"),
    )
    rms_stats = jnp.sqrt(stats_sum / (jnp.maximum(valid_count, 1.0) * D)).reshape(LAYERS, 3)
    return (
        stream.astype(jnp.bfloat16)[None],
        stream_grad[None],
        gains_sum,
        head_sum,
        filter_sum,
        beta_sum,
        *[jnp.stack(pair[::-1]) for pair in zip(*weight_list)],
        rms_stats,
    )


def solution(mesh):
    return jax.shard_map(
        on_device,
        mesh=mesh,
        in_specs=(
            P("fsdp", "seq", None),
            P("fsdp", None),
            P("fsdp", "seq"),
            P(),
            P(),
            P(),
            P(),
            P(None, "fsdp", None),
            P(None, "fsdp", None),
            P(None, "fsdp", None),
            P(None, "fsdp", None),
            P("fsdp", "seq", None),
        ),
        out_specs=(
            P("fsdp", "seq", None),
            P("fsdp", "seq", None),
            P(),
            P(),
            P(),
            P(),
            P(None, "fsdp", None),
            P(None, "fsdp", None),
            P(None, "fsdp", None),
            P(None, "fsdp", None),
            P(),
        ),
        check_vma=False,
    )
```

```python
from functools import partial
import jax
import jax.numpy as jnp
from jax import lax
from jax.experimental import pallas as pl
from jax.experimental.pallas import tpu as pltpu
from jax.sharding import PartitionSpec as P

D = 1024
H = 8
HD = 128
KW = 4
LAYERS = 2
CHUNK = 128
TOGETHER = 4
TOGETHER_BACK = 2
HALO = 16
f32 = jnp.float32
bf16 = jnp.bfloat16
EPS_NORM = 1e-05
EPS_UNIT = 1e-06
VMEM_LIMIT = 60 * 1024 * 1024


def dot_nn(a, b):
    return lax.dot_general(a.astype(bf16), b.astype(bf16), (((1,), (0,)), ((), ())), preferred_element_type=f32)


def dot_nt(a, b):
    return lax.dot_general(a.astype(bf16), b.astype(bf16), (((1,), (1,)), ((), ())), preferred_element_type=f32)


def dot_tn(a, b):
    return lax.dot_general(a.astype(bf16), b.astype(bf16), (((0,), (0,)), ((), ())), preferred_element_type=f32)


def sigmoid(x):
    return 1.0 / (1.0 + jnp.exp(-x))


def conv_masks(dcol_ref, rows):
    here = dcol_ref[pl.ds(HALO, rows), :]
    return [
        jnp.broadcast_to((dcol_ref[pl.ds(HALO - KW + 1 + i, rows), :] == here).astype(f32), (rows, HD))
        for i in range(KW - 1)
    ]


def conv_sum(x_ref, taps_ref, masks, ext, h):
    rows = x_ref.shape[0] - HALO
    lanes = pl.ds(h * HD, HD)
    ext[...] = x_ref[:, lanes].astype(f32)
    total = taps_ref[pl.ds(KW - 1, 1), lanes] * ext[pl.ds(HALO, rows), :]
    for i in range(KW - 1):
        total = total + taps_ref[pl.ds(i, 1), lanes] * ext[pl.ds(HALO - KW + 1 + i, rows), :] * masks[i]
    return total


def low(x):
    return x.astype(bf16).astype(f32)


def unit_scale(x):
    return lax.rsqrt(jnp.sum(x * x, axis=-1, keepdims=True) + EPS_UNIT)


def head_column(table, head):
    lane = lax.broadcasted_iota(jnp.int32, table.shape, 1)
    return jnp.sum(jnp.where(lane == head, table, 0.0), axis=1, keepdims=True)


def chunk_marks(dcol_ref, c):
    at = HALO + c * CHUNK
    docs = dcol_ref[pl.ds(at, CHUNK), :]
    prior = dcol_ref[pl.ds(at - 1, 1), :]
    last = dcol_ref[pl.ds(at + CHUNK - 1, 1), :]
    carry = (docs == prior).astype(f32)
    tail = (docs == last).astype(f32)
    carry_last = (last == prior).astype(f32)
    return docs, carry, tail, carry_last


def tri_index():
    row = lax.broadcasted_iota(jnp.int32, (CHUNK, CHUNK), 0)
    col = lax.broadcasted_iota(jnp.int32, (CHUNK, CHUNK), 1)
    return row, col


def inverses(systems, differ):
    row, col = tri_index()
    eye = (row == col).astype(f32)
    found = [eye - jnp.where(differ == 1, low_part, 0.0) for low_part in systems]
    step = 2
    while step < CHUNK:
        side = (differ >= step) & (differ < 2 * step)
        lows = [x.astype(bf16) for x in found]
        inner = [dot_nn(jnp.where(side, s, 0.0), x) for s, x in zip(systems, lows)]
        outer = [dot_nn(x, y) for x, y in zip(lows, inner)]
        found = [x - y for x, y in zip(found, outer)]
        step *= 2
    return found


def fwd_local_kernel(
    q_ref, k_ref, v_ref, tq_ref, tk_ref, tv_ref, lg_ref, dcol_ref, drow_ref, *refs,
):
    qn_ref, kn_ref, tinv_ref, wu_ref, gain_ref, pre_ref, total_ref, ext = refs[-8:]
    group = pl.program_id(0)
    rows = q_ref.shape[0] - HALO
    chunks = rows // CHUNK
    masks = conv_masks(dcol_ref, rows)
    heads = range(q_ref.shape[1] // HD)

    def filtered(x, taps, h):
        s = conv_sum(x, taps, masks, ext.at[h], h)
        return low(s * sigmoid(s))

    queries = [filtered(q_ref, tq_ref, h) for h in heads]
    keys = [filtered(k_ref, tk_ref, h) for h in heads]
    values = [filtered(v_ref, tv_ref, h) for h in heads]
    kns, kbs, vbs = [], [], []
    for h in heads:
        lanes = pl.ds(h * HD, HD)
        qn_ref[:, lanes] = (queries[h] * (unit_scale(queries[h]) * HD**-0.5)).astype(bf16)
        kn = keys[h] * unit_scale(keys[h])
        kn_ref[:, lanes] = kn.astype(bf16)
        beta = sigmoid(head_column(lg_ref[...].astype(f32), group * len(heads) + h))
        kns.append(kn.astype(bf16))
        kbs.append((beta * kn).astype(bf16))
        vbs.append((beta * values[h]).astype(bf16))
    row, col = tri_index()
    differ = row ^ col
    marks = [chunk_marks(dcol_ref, c) for c in range(chunks)]
    cut = lambda x, c: x[c * CHUNK : (c + 1) * CHUNK]
    items = [(h, c) for h in heads for c in range(chunks)]
    keeps = [(marks[c][0] == drow_ref[pl.ds(c, 1), :]) & (col < row) for c in range(chunks)]
    systems = [dot_nt(cut(kbs[h], c), cut(kns[h], c)) for h, c in items]
    systems = [jnp.where(keeps[c], s, 0.0) for s, (h, c) in zip(systems, items)]
    found = [x.astype(bf16) for x in inverses(systems, differ)]
    both = [
        dot_nn(x, jnp.concatenate([cut(kbs[h], c), cut(vbs[h], c)], axis=1)) for x, (h, c) in zip(found, items)
    ]
    tails = [(cut(kns[h], c).astype(f32) * marks[c][2]).astype(bf16) for h, c in items]
    moved = [
        jnp.concatenate([(b[:, :HD] * marks[c][1]).astype(bf16), b[:, HD:].astype(bf16)], axis=1)
        for b, (h, c) in zip(both, items)
    ]
    steps = [dot_tn(t, m) for t, m in zip(tails, moved)]
    for i, (h, c) in enumerate(items):
        at = pl.ds(c * CHUNK, CHUNK)
        tinv_ref[h, at, :] = found[i]
        wu_ref[h, at, :] = both[i].astype(bf16)
        gain_ref[h, at, :] = steps[i][:, :HD].astype(bf16)
    eye = (row == col).astype(f32)
    states = [jnp.concatenate([eye, jnp.zeros_like(eye)], axis=1) for _ in heads]
    for c in range(chunks):
        lows = [state.astype(bf16) for state in states]
        for h in heads:
            pre_ref[h, pl.ds(c * CHUNK, CHUNK), :] = lows[h]
        gone = [dot_nn(steps[h * chunks + c][:, :HD], lows[h]) for h in heads]
        states = [
            marks[c][3] * states[h]
            - gone[h]
            + jnp.concatenate([jnp.zeros_like(eye), steps[h * chunks + c][:, HD:]], axis=1)
            for h in heads
        ]
    for h in heads:
        total_ref[h] = states[h].astype(bf16)


def col_spec(rows, base, count=1):
    return pl.BlockSpec((rows, count * HD), lambda h: (0, base // count + h))


def full_spec(shape):
    return pl.BlockSpec(shape, lambda h: (0,) * len(shape))


def head_spec(shape, count=1):
    return pl.BlockSpec((count,) + shape, lambda h: (h,) + (0,) * len(shape))


def params():
    return pltpu.CompilerParams(vmem_limit_bytes=VMEM_LIMIT, dimension_semantics=("arbitrary",))


def cost(micros, rows):
    return pl.CostEstimate(flops=0, bytes_accessed=int(micros * 3.69e6 * rows / 512), transcendentals=0)


def fwd_local(projected, taps, logits, dcol, drow, after):
    rows = projected.shape[0] - HALO
    chunks = rows // CHUNK
    sds = jax.ShapeDtypeStruct
    return pl.pallas_call(
        fwd_local_kernel,
        grid=(H // TOGETHER,),
        in_specs=[col_spec(rows + HALO, i * H, TOGETHER) for i in range(3)]
        + [col_spec(KW, 0, TOGETHER), col_spec(KW, H, TOGETHER), col_spec(KW, 2 * H, TOGETHER)]
        + [full_spec((rows, HD)), full_spec((rows + HALO, 1)), full_spec((chunks, CHUNK))]
        + [pl.BlockSpec(memory_space=pl.ANY) for _ in after],
        out_specs=[
            col_spec(rows, 0, TOGETHER),
            col_spec(rows, 0, TOGETHER),
            head_spec((rows, CHUNK), TOGETHER),
            head_spec((rows, 2 * HD), TOGETHER),
            head_spec((rows, HD), TOGETHER),
            head_spec((rows, 2 * HD), TOGETHER),
            head_spec((HD, 2 * HD), TOGETHER),
        ],
        out_shape=[
            sds((rows, D), bf16),
            sds((rows, D), bf16),
            sds((H, rows, CHUNK), bf16),
            sds((H, rows, 2 * HD), bf16),
            sds((H, rows, HD), bf16),
            sds((H, rows, 2 * HD), bf16),
            sds((H, HD, 2 * HD), bf16),
        ],
        scratch_shapes=[pltpu.VMEM((TOGETHER, rows + HALO, HD), f32)],
        compiler_params=params(),
        cost_estimate=cost(14.5, rows),
        name="delta_local",
    )(*([projected] * 3 + [taps] * 3 + [logits, dcol, drow]), *after)


def fwd_read_kernel(qn_ref, kn_ref, wu_ref, dcol_ref, drow_ref, r_ref, o_ref):
    rows = qn_ref.shape[0]
    row, col = tri_index()
    chunks = range(rows // CHUNK)
    ats = [pl.ds(c * CHUNK, CHUNK) for c in chunks]
    marks = [chunk_marks(dcol_ref, c) for c in chunks]
    keeps = [(marks[c][0] == drow_ref[pl.ds(c, 1), :]) & (col <= row) for c in chunks]
    items = [(h, c) for h in range(qn_ref.shape[1] // HD) for c in chunks]
    lanes = [pl.ds(h * HD, HD) for h, _ in items]
    parts = [dot_nt(qn_ref[ats[c], lane], kn_ref[ats[c], lane]) for lane, (h, c) in zip(lanes, items)]
    parts = [jnp.where(keeps[c], part, 0.0).astype(bf16) for part, (h, c) in zip(parts, items)]
    ws = [(wu_ref[h, ats[c], :HD].astype(f32) * marks[c][1]).astype(bf16) for h, c in items]
    both = [
        dot_nn(part, jnp.concatenate([w, wu_ref[h, ats[c], HD:]], axis=1)) for part, w, (h, c) in zip(parts, ws, items)
    ]
    for lane, b, (h, c) in zip(lanes, both, items):
        r_ref[ats[c], lane] = (qn_ref[ats[c], lane].astype(f32) * marks[c][1] - b[:, :HD]).astype(bf16)
        o_ref[ats[c], lane] = b[:, HD:]


def fwd_read(qn, kn, wu, dcol, drow):
    rows = qn.shape[0]
    chunks = rows // CHUNK
    sds = jax.ShapeDtypeStruct
    return pl.pallas_call(
        fwd_read_kernel,
        grid=(H // TOGETHER,),
        in_specs=[col_spec(rows, 0, TOGETHER), col_spec(rows, 0, TOGETHER), head_spec((rows, 2 * HD), TOGETHER), full_spec((rows + HALO, 1)), full_spec((chunks, CHUNK))],
        out_specs=[col_spec(rows, 0, TOGETHER), col_spec(rows, 0, TOGETHER)],
        out_shape=[sds((rows, D), bf16), sds((rows, D), f32)],
        compiler_params=params(),
        cost_estimate=cost(3.2, rows),
        name="delta_read",
    )(qn, kn, wu, dcol, drow)


def fwd_state_kernel(moves, paired, place_ref, *refs):
    ins, (state_ref, out_ref, head_ref) = refs[: moves + 5], refs[-3:]
    *near_refs, far_ref, pre_ref, r_ref, o_ref, gain_ref = ins
    rows = r_ref.shape[0]
    heads = range(r_ref.shape[1] // HD)
    states = [far_ref[h].astype(f32) for h in heads]
    if paired:
        states = [jnp.where(place_ref[0] >= 2, state, 0.0) for state in states]
    for near_ref in reversed(near_refs):
        moved = [dot_nn(near_ref[h, :, :HD], states[h]) + near_ref[h, :, HD:].astype(f32) for h in heads]
        states = [jnp.where(place_ref[0] % 2 == 1, m, s) if paired else m for m, s in zip(moved, states)]
    lows = [state.astype(bf16) for state in states]
    items = [(h, c) for h in heads for c in range(rows // CHUNK)]
    ats = [pl.ds(c * CHUNK, CHUNK) for _, c in items]
    lanes = [pl.ds(h * HD, HD) for h, _ in items]
    nows = [dot_nn(pre_ref[h, at, :HD], lows[h]) for at, (h, c) in zip(ats, items)]
    nows = [(now + pre_ref[h, at, HD:].astype(f32)).astype(bf16) for now, at, (h, c) in zip(nows, ats, items)]
    outs = [dot_nn(r_ref[at, lane], now) for at, lane, now in zip(ats, lanes, nows)]
    for out, now, at, lane, (h, c) in zip(outs, nows, ats, lanes, items):
        state_ref[h, at, :] = now
        o = o_ref[at, lane] + out
        out_ref[at, lane] = o
        scale = lax.rsqrt(jnp.mean(o * o, axis=-1, keepdims=True) + EPS_NORM)
        head_ref[at, lane] = (o * scale * gain_ref[...]).astype(bf16)


def fwd_state(place, paired, nears, far, pre, r, o, gain, after):
    rows = r.shape[0]
    sds = jax.ShapeDtypeStruct
    return pl.pallas_call(
        partial(fwd_state_kernel, len(nears), paired),
        grid=(H // TOGETHER,),
        in_specs=[
            pl.BlockSpec(memory_space=pltpu.SMEM),
            *[head_spec((HD, 2 * HD), TOGETHER) for _ in nears],
            head_spec((HD, HD), TOGETHER),
            head_spec((rows, 2 * HD), TOGETHER),
            col_spec(rows, 0, TOGETHER),
            col_spec(rows, 0, TOGETHER),
            full_spec((1, HD)),
            *[pl.BlockSpec(memory_space=pl.ANY) for _ in after],
        ],
        out_specs=[head_spec((rows, HD), TOGETHER), col_spec(rows, 0, TOGETHER), col_spec(rows, 0, TOGETHER)],
        out_shape=[sds((H, rows, HD), bf16), sds((rows, D), f32), sds((rows, D), bf16)],
        compiler_params=params(),
        cost_estimate=cost(4.3, rows),
        name="delta_state",
    )(place, *nears, far, pre, r, o, gain, *after)


def bwd_local_kernel(dhead_ref, o_ref, r_ref, gain_ref, step_ref, dcol_ref, *refs):
    do_ref, dgain_ref, total_ref = refs[-3:]
    rows = o_ref.shape[0]
    chunks = rows // CHUNK

    @pl.when(pl.program_id(0) == 0)
    def _():
        dgain_ref[...] = jnp.zeros_like(dgain_ref)

    heads = range(o_ref.shape[1] // HD)
    ats = [pl.ds(c * CHUNK, CHUNK) for c in range(chunks)]
    marks = [chunk_marks(dcol_ref, c)[3] for c in range(chunks)]
    dos = []
    for h in heads:
        lanes = pl.ds(h * HD, HD)
        o = o_ref[:, lanes]
        dy = dhead_ref[:, lanes].astype(f32)
        scale = lax.rsqrt(jnp.mean(o * o, axis=-1, keepdims=True) + EPS_NORM)
        x = o * scale
        dgain_ref[...] += jnp.sum(dy * x, axis=0, keepdims=True)
        dx = dy * gain_ref[...]
        do = (scale * (dx - x * jnp.mean(dx * x, axis=-1, keepdims=True))).astype(bf16)
        do_ref[:, lanes] = do
        dos.append(do)
    gives = [
        [dot_tn(r_ref[ats[c], pl.ds(h * HD, HD)], dos[h][c * CHUNK : (c + 1) * CHUNK]) for c in range(chunks)] for h in heads
    ]
    states = [gives[h][chunks - 1] for h in heads]
    for c in reversed(range(chunks - 1)):
        gone = [dot_tn(step_ref[h, ats[c], :], states[h]) for h in heads]
        states = [marks[c] * states[h] - gone[h] + gives[h][c] for h in heads]
    for h in heads:
        total_ref[h] = states[h].astype(bf16)


def bwd_local(dhead, o, r, gain, step, dcol, after):
    rows = o.shape[0]
    sds = jax.ShapeDtypeStruct
    return pl.pallas_call(
        bwd_local_kernel,
        grid=(H // TOGETHER,),
        in_specs=[col_spec(rows, 0, TOGETHER), col_spec(rows, 0, TOGETHER), col_spec(rows, 0, TOGETHER), full_spec((1, HD)), head_spec((rows, HD), TOGETHER), full_spec((rows + HALO, 1))]
        + [pl.BlockSpec(memory_space=pl.ANY) for _ in after],
        out_specs=[col_spec(rows, 0, TOGETHER), full_spec((1, HD)), head_spec((HD, HD), TOGETHER)],
        out_shape=[sds((rows, D), bf16), sds((1, HD), f32), sds((H, HD, HD), bf16)],
        compiler_params=params(),
        cost_estimate=cost(3.8, rows),
        name="delta_back_local",
    )(dhead, o, r, gain, step, dcol, *after)


def bwd_main_kernel(moves, paired, place_ref, *refs):
    later, refs = refs[: 2 * moves + 1], refs[2 * moves + 1 :]
    ins, outs = refs[:15], refs[-12:]
    bwd_main_body(place_ref if paired else None, later, *ins, *outs)


def bwd_main_body(
    place_ref, later, q_ref, k_ref, v_ref, tq_ref, tk_ref, tv_ref, lg_ref, dcol_ref, drow_ref,
    tinv_ref, wu_ref, step_ref, state_ref, r_ref, do_ref,
    dproj_ref, rq_ref, rk_ref, rv_ref, cq_ref, ck_ref, cv_ref, dl_ref, ext, grad, held, sems,
):
    group = pl.program_id(0)
    rows = q_ref.shape[0] - HALO
    chunks = range(rows // CHUNK)
    heads = range(q_ref.shape[1] // HD)
    masks = conv_masks(dcol_ref, rows)
    row, col = tri_index()
    cut = lambda x, c: x[c * CHUNK : (c + 1) * CHUNK]

    def filtered(x, taps, h, which):
        s = conv_sum(x, taps, masks, ext.at[which + 3 * h], h)
        gate = sigmoid(s)
        return low(s * gate), gate * (1.0 + s * (1.0 - gate))

    queries, slope_q, scale_q, qns = [], [], [], []
    keys, slope_k, scale_k, kns = [], [], [], []
    values, slope_v, betas, kbs = [], [], [], []
    for h in heads:
        query, slope = filtered(q_ref, tq_ref, h, 0)
        queries.append(query)
        slope_q.append(slope)
        scale_q.append(unit_scale(query))
        qns.append((query * scale_q[h] * HD**-0.5).astype(bf16))
        key, slope = filtered(k_ref, tk_ref, h, 1)
        slope_k.append(slope)
        scale_k.append(unit_scale(key))
        kns.append(key * scale_k[h])
        value, slope = filtered(v_ref, tv_ref, h, 2)
        values.append(value)
        slope_v.append(slope)
        betas.append(sigmoid(head_column(lg_ref[...].astype(f32), group * len(heads) + h)))
        kbs.append((betas[h] * kns[h]).astype(bf16))

    moves = len(later) // 2
    marks = [chunk_marks(dcol_ref, c) for c in chunks]
    ats = [pl.ds(c * CHUNK, CHUNK) for c in chunks]
    items = [(h, c) for h in heads for c in chunks]
    lanes = [pl.ds(h * HD, HD) for h in heads]
    dss = [later[-1][h].astype(f32) for h in heads]
    if place_ref is not None:
        dss = [jnp.where(place_ref[0] < 2, ds, 0.0) for ds in dss]
    for i in reversed(range(moves)):
        moved = [dot_tn(later[i][h], dss[h]) + later[moves + i][h].astype(f32) for h in heads]
        dss = [m if place_ref is None else jnp.where(place_ref[0] % 2 == 0, m, ds) for m, ds in zip(moved, dss)]
    gives = [dot_tn(r_ref[ats[c], lanes[h]], do_ref[ats[c], lanes[h]]) for h, c in items]
    leaving = {}
    for c in reversed(chunks):
        for h in heads:
            leaving[h, c] = dss[h].astype(bf16)
        if c:
            gone = [dot_tn(step_ref[h, ats[c], :], leaving[h, c]) for h in heads]
            dss = [marks[c][3] * dss[h] - gone[h] + gives[h * len(chunks) + c] for h in heads]

    each = range(len(items))
    carries = [marks[c][1] for _, c in items]
    tails = [marks[c][2] for _, c in items]
    sames = [marks[c][0] == drow_ref[pl.ds(c, 1), :] for c in chunks]
    uptos = [sames[c] & (col <= row) for _, c in items]
    belows = [sames[c] & (col < row) for _, c in items]
    q_cs = [cut(qns[h], c) for h, c in items]
    k_cs = [cut(kns[h], c).astype(bf16) for h, c in items]
    kb_cs = [cut(kbs[h], c) for h, c in items]
    dos = [do_ref[ats[c], lanes[h]] for h, c in items]
    wus = [wu_ref[h, ats[c], :] for h, c in items]
    states = [state_ref[h, ats[c], :] for h, c in items]
    leave = [leaving[item] for item in items]
    parts = [dot_nt(q_cs[i], k_cs[i]) for i in each]
    reads = [dot_nn(wus[i][:, :HD], states[i]) for i in each]
    kds = [dot_nn(k_cs[i], leave[i]) for i in each]
    parts = [jnp.where(uptos[i], parts[i], 0.0).astype(bf16) for i in each]
    deltas = [(wus[i][:, HD:].astype(f32) - carries[i] * reads[i]).astype(bf16) for i in each]
    pds = [dot_tn(parts[i], dos[i]) for i in each]
    dparts = [dot_nt(dos[i], deltas[i]) for i in each]
    dkfs = [dot_nt(deltas[i], leave[i]) for i in each]
    dds = [pds[i] + tails[i] * kds[i] for i in each]
    throughs = [dot_nt(jnp.concatenate([dos[i], dds[i].astype(bf16)], axis=0), states[i]) for i in each]
    inner = [
        jnp.concatenate([(-(carries[i] * throughs[i][CHUNK:])).astype(bf16), dds[i].astype(bf16)], axis=1) for i in each
    ]
    dwus = [dot_tn(tinv_ref[h, ats[c], :], x) for x, (h, c) in zip(inner, items)]
    dlows = [dot_nt(dwus[i], wus[i]) for i in each]
    pairs = [
        jnp.concatenate(
            [jnp.where(uptos[i], dparts[i], 0.0).astype(bf16), jnp.where(belows[i], -dlows[i], 0.0).astype(bf16)], axis=0
        )
        for i in each
    ]
    ontos = [dot_nn(pairs[i], k_cs[i]) for i in each]
    backs = [dot_tn(pairs[i], jnp.concatenate([q_cs[i], kb_cs[i]], axis=0)) for i in each]
    b_cs = [cut(betas[h], c) for h, c in items]
    dqs = [carries[i] * throughs[i][:CHUNK] + ontos[i][:CHUNK] for i in each]
    dkbs = [dwus[i][:, :HD] + ontos[i][CHUNK:] for i in each]
    dks = [backs[i] + tails[i] * dkfs[i] + b_cs[i] * dkbs[i] for i in each]
    dvs = [b_cs[i] * dwus[i][:, HD:] for i in each]
    dbs = [
        jnp.sum(dkbs[i] * cut(kns[h], c) + dwus[i][:, HD:] * cut(values[h], c), axis=1, keepdims=True)
        for i, (h, c) in zip(each, items)
    ]

    @pl.when(group == 0)
    def _():
        dl_ref[...] = jnp.zeros_like(dl_ref)

    slot = lax.rem(group, 2)
    width = len(heads) * HD

    def sent(step, which):
        start = pl.multiple_of(which * D + step * width, 128)
        return pltpu.make_async_copy(
            held.at[lax.rem(step, 2), which], dproj_ref.at[:, pl.ds(start, width)], sems.at[lax.rem(step, 2), which]
        )

    @pl.when(group >= 2)
    def _():
        for which in range(3):
            sent(group - 2, which).wait()

    for i in range(KW - 1):
        grad[i, pl.ds(0, HALO), :] = jnp.zeros((HALO, HD), f32)
        grad[i, pl.ds(HALO + rows, 8), :] = jnp.zeros((8, HD), f32)

    def conv_back(dfilt, slope, taps_ref, rim_ref, dtap_ref, h, which):
        ds_ = low(dfilt) * slope
        lane = lanes[h]
        x = ext.at[which + 3 * h]
        dtap_ref[pl.ds(KW - 1, 1), lane] = jnp.sum(ds_ * x[pl.ds(HALO, rows), :], axis=0, keepdims=True)
        total = ds_ * taps_ref[pl.ds(KW - 1, 1), lane]
        rim = jnp.zeros((HALO, HD), f32)
        for i in range(KW - 1):
            masked = ds_ * masks[i]
            grad[i, pl.ds(HALO, rows), :] = masked
            place_i = pl.ds(HALO - KW + 1 + i, rows)
            dtap_ref[pl.ds(i, 1), lane] = jnp.sum(masked * x[place_i, :], axis=0, keepdims=True)
            tap = taps_ref[pl.ds(i, 1), lane]
            total = total + tap * grad[i, pl.ds(HALO + KW - 1 - i, rows), :]
            rim = rim + tap * grad[i, pl.ds(KW - 1 - i, HALO), :]
        rim_ref[:, lane] = rim.astype(bf16)
        held[slot, which, :, lane] = total.astype(bf16)

    lane_index = lax.broadcasted_iota(jnp.int32, (rows, HD), 1)
    for h in heads:
        join = lambda parts: jnp.concatenate(parts[h * len(chunks) : (h + 1) * len(chunks)], axis=0)
        dqn = join(dqs) * HD**-0.5
        unit = queries[h] * scale_q[h]
        dquery = scale_q[h] * (dqn - unit * jnp.sum(dqn * unit, axis=-1, keepdims=True))
        dkn = join(dks)
        dkeys = scale_k[h] * (dkn - kns[h] * jnp.sum(dkn * kns[h], axis=-1, keepdims=True))
        dlogit = join(dbs) * betas[h] * (1.0 - betas[h])
        dl_ref[...] = jnp.where(
            lane_index == group * len(heads) + h, dlogit, dl_ref[...].astype(f32)
        ).astype(bf16)
        conv_back(dquery, slope_q[h], tq_ref, rq_ref, cq_ref, h, 0)
        conv_back(dkeys, slope_k[h], tk_ref, rk_ref, ck_ref, h, 1)
        conv_back(join(dvs), slope_v[h], tv_ref, rv_ref, cv_ref, h, 2)
    for which in range(3):
        sent(group, which).start()

    @pl.when(group == pl.num_programs(0) - 1)
    def _():
        for which in range(3):
            sent(group - 1, which).wait()
            sent(group, which).wait()


def bwd_main(place, paired, moves, gives, projected, taps, logits, dcol, drow, tinv, wu, step, state, r, do, after):
    rows = projected.shape[0] - HALO
    chunks = rows // CHUNK
    sds = jax.ShapeDtypeStruct
    return pl.pallas_call(
        partial(bwd_main_kernel, len(moves), paired),
        grid=(H // TOGETHER_BACK,),
        in_specs=[pl.BlockSpec(memory_space=pltpu.SMEM)]
        + [head_spec((HD, HD), TOGETHER_BACK) for _ in (*moves, *gives)]
        + [col_spec(rows + HALO, i * H, TOGETHER_BACK) for i in range(3)]
        + [col_spec(KW, 0, TOGETHER_BACK), col_spec(KW, H, TOGETHER_BACK), col_spec(KW, 2 * H, TOGETHER_BACK)]
        + [full_spec((rows, HD)), full_spec((rows + HALO, 1)), full_spec((chunks, CHUNK))]
        + [head_spec((rows, CHUNK), TOGETHER_BACK), head_spec((rows, 2 * HD), TOGETHER_BACK), head_spec((rows, HD), TOGETHER_BACK), head_spec((rows, HD), TOGETHER_BACK)]
        + [col_spec(rows, 0, TOGETHER_BACK), col_spec(rows, 0, TOGETHER_BACK)]
        + [pl.BlockSpec(memory_space=pl.ANY) for _ in after],
        out_specs=[pl.BlockSpec(memory_space=pl.ANY)] + [col_spec(HALO, 0, TOGETHER_BACK)] * 3 + [col_spec(KW, 0, TOGETHER_BACK)] * 3 + [full_spec((rows, HD))],
        out_shape=[sds((rows, 3 * D), bf16)] + [sds((HALO, D), bf16)] * 3 + [sds((KW, D), f32)] * 3 + [sds((rows, HD), bf16)],
        scratch_shapes=[
            pltpu.VMEM((3 * TOGETHER_BACK, rows + HALO, HD), f32),
            pltpu.VMEM((KW - 1, rows + HALO + 8, HD), f32),
            pltpu.VMEM((2, 3, rows, TOGETHER_BACK * HD), bf16),
            pltpu.SemaphoreType.DMA((2, 3)),
        ],
        compiler_params=params(),
        cost_estimate=cost(24, rows),
        name="delta_back",
    )(place, *moves, *gives, *([projected] * 3 + [taps] * 3), logits, dcol, drow, tinv, wu, step, state, r, do, *after)


def pair_forward_kernel(place_ref, own_ref, other_ref, out_ref):
    late = place_ref[0] % 2 == 1
    for h in range(H):
        own, partner = own_ref[h].astype(f32), other_ref[h].astype(f32)
        first, second = jnp.where(late, partner, own), jnp.where(late, own, partner)
        out_ref[h] = (dot_nn(second[:, :HD], first[:, HD:]) + second[:, HD:]).astype(bf16)


def pair_backward_kernel(place_ref, own_a_ref, other_a_ref, own_ref, other_ref, out_ref):
    late = place_ref[0] % 2 == 1
    for h in range(H):
        own, partner = own_ref[h].astype(f32), other_ref[h].astype(f32)
        first, second = jnp.where(late, partner, own), jnp.where(late, own, partner)
        passed = jnp.where(late, other_a_ref[h, :, :HD].astype(f32), own_a_ref[h, :, :HD].astype(f32))
        out_ref[h] = (first + dot_tn(passed, second)).astype(bf16)


def pair_state(kernel, place, *arrays, after=()):
    count = len(arrays) + 1
    return pl.pallas_call(
        lambda *refs: kernel(*refs[:count], refs[-1]),
        in_specs=[pl.BlockSpec(memory_space=pltpu.SMEM)]
        + [pl.BlockSpec(memory_space=pltpu.VMEM)] * len(arrays)
        + [pl.BlockSpec(memory_space=pl.ANY)] * len(after),
        out_specs=pl.BlockSpec(memory_space=pltpu.VMEM),
        out_shape=jax.ShapeDtypeStruct((H, HD, HD), bf16),
        cost_estimate=cost(3, 512),
        name="pair_state",
        compiler_params=pltpu.CompilerParams(vmem_limit_bytes=VMEM_LIMIT),
    )(place, *arrays, *after)


def project_kernel(tail_ref, gain_ref, normed_ref, weight_ref, beta_ref, out_ref, logits_ref, low_tail):
    @pl.when(pl.program_id(0) == 0)
    def _():
        tail = tail_ref[...]
        scale = lax.rsqrt(jnp.mean(tail * tail, axis=-1, keepdims=True) + EPS_NORM)
        low_tail[...] = (tail * scale * gain_ref[...]).astype(bf16)
        logits_ref[...] = dot_nn(normed_ref[...], beta_ref[...]).astype(bf16)

    out_ref[pl.ds(0, HALO), :] = dot_nn(low_tail[...], weight_ref[...]).astype(bf16)
    out_ref[pl.ds(HALO, normed_ref.shape[0]), :] = dot_nn(normed_ref[...], weight_ref[...]).astype(bf16)


def project(tail, gain, normed, weight, beta, after, steps=4):
    rows, width = normed.shape[0], weight.shape[1]
    sds = jax.ShapeDtypeStruct
    return pl.pallas_call(
        lambda *refs: project_kernel(*refs[:5], *refs[-3:]),
        grid=(steps,),
        in_specs=[
            full_spec(tail.shape),
            full_spec((1, D)),
            full_spec(normed.shape),
            pl.BlockSpec((D, width // steps), lambda j: (0, j)),
            full_spec(beta.shape),
        ]
        + [pl.BlockSpec(memory_space=pl.ANY) for _ in after],
        out_specs=[pl.BlockSpec((rows + HALO, width // steps), lambda j: (0, j)), full_spec((rows, beta.shape[1]))],
        out_shape=[sds((rows + HALO, width), bf16), sds((rows, beta.shape[1]), bf16)],
        scratch_shapes=[pltpu.VMEM((HALO, D), bf16)],
        compiler_params=params(),
        cost_estimate=cost(5, rows),
        name="project",
    )(tail, gain, normed, weight, beta, *after)


def branch_kernel(x_ref, weight_ref, stream_ref, valid_ref, gain_ref, out_ref, normed_ref, sums_ref, total, *, last):
    step = pl.program_id(0)

    @pl.when(step == 0)
    def _():
        total[...] = jnp.zeros_like(total)

    total[...] += dot_nn(x_ref[...], weight_ref[...])

    @pl.when(step == pl.num_programs(0) - 1)
    def _():
        branch = total[...]
        stream = stream_ref[...] + branch
        out_ref[...] = stream
        sums_ref[pl.ds(0, 1), :] = jnp.sum(branch * branch * valid_ref[...], axis=0, keepdims=True)
        square = stream * stream
        sums_ref[pl.ds(1, 1), :] = jnp.sum(square * valid_ref[...], axis=0, keepdims=True)
        if last:
            normed_ref[...] = stream.astype(bf16)
        else:
            scale = lax.rsqrt(jnp.mean(square, axis=-1, keepdims=True) + EPS_NORM)
            normed_ref[...] = (stream * scale * gain_ref[...]).astype(bf16)


def branch(x, weight, stream, valid, gain, last, after, steps):
    rows, depth = x.shape
    sds = jax.ShapeDtypeStruct
    return pl.pallas_call(
        lambda *refs: branch_kernel(*refs[:5], *refs[-4:], last=last),
        grid=(steps,),
        in_specs=[
            pl.BlockSpec((rows, depth // steps), lambda j: (0, j)),
            pl.BlockSpec((depth // steps, D), lambda j: (j, 0)),
            full_spec((rows, D)),
            full_spec((rows, 1)),
            full_spec((1, D)),
        ]
        + [pl.BlockSpec(memory_space=pl.ANY) for _ in after],
        out_specs=[full_spec((rows, D)), full_spec((rows, D)), full_spec((2, D))],
        out_shape=[sds((rows, D), f32), sds((rows, D), bf16), sds((2, D), f32)],
        scratch_shapes=[pltpu.VMEM((rows, D), f32)],
        compiler_params=params(),
        cost_estimate=cost(5, rows),
        name="branch",
    )(x, weight, stream, valid, gain, *after)


def act_kernel(x_ref, gate_ref, up_ref, act_ref, both_ref):
    gate = dot_nn(x_ref[...], gate_ref[...])
    up = dot_nn(x_ref[...], up_ref[...])
    act_ref[...] = (gate * sigmoid(gate) * up).astype(bf16)
    both_ref[0] = gate.astype(bf16)
    both_ref[1] = up.astype(bf16)


def gated(x, weight, after, steps=11):
    rows, half = x.shape[0], weight.shape[1] // 2
    size = half // steps
    sds = jax.ShapeDtypeStruct
    return pl.pallas_call(
        lambda *refs: act_kernel(*refs[:3], *refs[-2:]),
        grid=(steps,),
        in_specs=[
            full_spec(x.shape),
            pl.BlockSpec((D, size), lambda j: (0, j)),
            pl.BlockSpec((D, size), lambda j: (0, steps + j)),
        ]
        + [pl.BlockSpec(memory_space=pl.ANY) for _ in after],
        out_specs=[pl.BlockSpec((rows, size), lambda j: (0, j)), pl.BlockSpec((2, rows, size), lambda j: (0, 0, j))],
        out_shape=[sds((rows, half), bf16), sds((2, rows, half), bf16)],
        compiler_params=params(),
        cost_estimate=cost(9, rows),
        name="gated",
    )(x, weight, weight, *after)


def act_back_kernel(g_ref, down_ref, both_ref, out_ref):
    dact = dot_nt(g_ref[...], down_ref[...])
    gate, up = both_ref[0].astype(f32), both_ref[1].astype(f32)
    part = sigmoid(gate)
    silu = gate * part
    out_ref[0] = (dact * up * (part + silu * (1.0 - part))).astype(bf16)
    out_ref[1] = (dact * silu).astype(bf16)


def gated_back(g, down, both, after, steps=11):
    rows, half = g.shape[0], down.shape[0]
    size = half // steps
    block = pl.BlockSpec((2, rows, size), lambda j: (0, 0, j))
    return pl.pallas_call(
        lambda *refs: act_back_kernel(*refs[:3], refs[-1]),
        grid=(steps,),
        in_specs=[full_spec(g.shape), pl.BlockSpec((size, D), lambda j: (j, 0)), block]
        + [pl.BlockSpec(memory_space=pl.ANY) for _ in after],
        out_specs=block,
        out_shape=jax.ShapeDtypeStruct((2, rows, half), bf16),
        compiler_params=params(),
        cost_estimate=cost(8, rows),
        name="gated_back",
    )(g, down, both, *after)


def norm_back_kernel(d_ref, weight_ref, extra_ref, extra_weight_ref, stream_ref, g_ref, gain_ref, out_ref, low_ref, dgain_ref, total):
    step = pl.program_id(0)

    @pl.when(step == 0)
    def _():
        if extra_ref is None:
            total[...] = jnp.zeros_like(total)
        else:
            total[...] = dot_nt(extra_ref[...], extra_weight_ref[...])

    block = d_ref[0] if len(d_ref.shape) == 3 else d_ref[...]
    total[...] += dot_nt(block, weight_ref[...])

    @pl.when(step == pl.num_programs(0) - 1)
    def _():
        dn = total[...]
        stream = stream_ref[...]
        scale = lax.rsqrt(jnp.mean(stream * stream, axis=-1, keepdims=True) + EPS_NORM)
        x = stream * scale
        dgain_ref[...] = jnp.sum(dn * x, axis=0, keepdims=True)
        dx = dn * gain_ref[...]
        g = g_ref[...] + scale * (dx - x * jnp.mean(dx * x, axis=-1, keepdims=True))
        out_ref[...] = g
        low_ref[...] = g.astype(bf16)


def norm_back(d, weight, extra, stream, g, gain, after):
    rows = stream.shape[0]
    steps = 4
    size = weight.shape[1] // steps
    sds = jax.ShapeDtypeStruct
    if d.ndim == 3:
        d_spec = pl.BlockSpec((1, rows, size), lambda k: (k // 2, 0, k % 2))
    else:
        d_spec = pl.BlockSpec((rows, size), lambda k: (0, k))
    count = 5 + len(extra)

    def kernel(*refs):
        ins, outs = refs[:count], refs[-4:]
        more = ins[2 : 2 + len(extra)] if extra else (None, None)
        norm_back_kernel(*ins[:2], *more, *ins[2 + len(extra) :], *outs)

    return pl.pallas_call(
        kernel,
        grid=(steps,),
        in_specs=[d_spec, pl.BlockSpec((D, size), lambda k: (0, k))]
        + [full_spec(array.shape) for array in extra]
        + [full_spec((rows, D)), full_spec((rows, D)), full_spec((1, D))]
        + [pl.BlockSpec(memory_space=pl.ANY) for _ in after],
        out_specs=[full_spec((rows, D)), full_spec((rows, D)), full_spec((1, D))],
        out_shape=[sds((rows, D), f32), sds((rows, D), bf16), sds((1, D), f32)],
        scratch_shapes=[pltpu.VMEM((rows, D), f32)],
        compiler_params=params(),
        cost_estimate=cost(9, rows),
        name="norm_back",
    )(d, weight, *extra, stream, g, gain, *after)


def other(block, axis, mask):
    return lax.ppermute(block, axis, [(i, i ^ mask) for i in range(lax.axis_size(axis))])


def sum_over(block, axis):
    mask = 1
    while mask < lax.axis_size(axis):
        block = block + other(block, axis, mask)
        mask *= 2
    return block


ANY = pl.BlockSpec(memory_space=pl.ANY)
SMEM = pl.BlockSpec(memory_space=pltpu.SMEM)
VMEM = pl.BlockSpec(memory_space=pltpu.VMEM)


def run_copies(pairs, sems):
    copies = [pltpu.make_async_copy(src, dst, sems.at[i]) for i, (src, dst) in enumerate(pairs)]
    for copy in copies:
        copy.start()
    for copy in copies:
        copy.wait()


def aligned(index, size):
    return pl.ds(pl.multiple_of(index * size, 128), size)


def offsets(sizes):
    return [sum(sizes[:i]) for i in range(len(sizes))]


def pack_kernel(place_ref, *refs, plan):
    count = sum(len(sizes) for _, sizes in plan)
    ins, outs, sems = list(refs[:count]), refs[-len(plan) - 1 : -1], refs[-1]
    quarter = place_ref[0]
    pairs = []
    for (layer, sizes), out_ref in zip(plan, outs):
        for at, size in zip(offsets(sizes), sizes):
            pairs.append((ins.pop(0).at[layer, :, aligned(quarter, size)], out_ref.at[:, pl.ds(at, size)]))
    run_copies(pairs, sems)


def pack(place, groups, after):
    plan = [(layer, [weight.shape[2] // 4 for weight in weights]) for weights, layer in groups]
    weights = [weight for group, _ in groups for weight in group]
    return pl.pallas_call(
        partial(pack_kernel, plan=plan),
        in_specs=[SMEM] + [ANY] * (len(weights) + len(after)),
        out_specs=[VMEM] * len(groups),
        out_shape=[jax.ShapeDtypeStruct((128, sum(sizes)), bf16) for _, sizes in plan],
        scratch_shapes=[pltpu.SemaphoreType.DMA((len(weights),))],
        cost_estimate=cost(2 * len(groups), 512),
        name="pack_quarters",
        compiler_params=pltpu.CompilerParams(vmem_limit_bytes=VMEM_LIMIT),
    )(place, *weights, *after)


def spread_kernel(place_ref, *refs, sizes):
    pieces, outs, sems = refs[:10], refs[-len(sizes) - 1 : -1], refs[-1]
    seq, core = place_ref[0], place_ref[1]
    chips = outs[0].shape[0]
    pairs = []
    for own, (h, x, y, a, b) in ((core, pieces[:5]), (1 - core, pieces[5:])):
        for piece, mask, at in ((h, 0, 0), (x, 1, 0), (y, 2, 0), (a, 3, 0), (b, 3, chips // 2)):
            here = pl.ds(at, piece.shape[0])
            for out_ref, start, size in zip(outs, offsets(sizes), sizes):
                pairs.append((piece.at[:, :, pl.ds(start, size)], out_ref.at[here, own, :, aligned(seq ^ mask, size)]))
    run_copies(pairs, sems)


def spread(place, pieces, sizes, after):
    chips = pieces[0].shape[0] // 128
    pieces = [piece.reshape(-1, 128, piece.shape[1]) for piece in pieces]
    weights = pl.pallas_call(
        partial(spread_kernel, sizes=sizes),
        in_specs=[SMEM] + [ANY] * (len(pieces) + len(after)),
        out_specs=[VMEM] * len(sizes),
        out_shape=[jax.ShapeDtypeStruct((chips, 2, 128, size * 4), bf16) for size in sizes],
        scratch_shapes=[pltpu.SemaphoreType.DMA((len(pieces) * len(sizes),))],
        compiler_params=pltpu.CompilerParams(vmem_limit_bytes=VMEM_LIMIT),
        cost_estimate=cost(7, 512),
        name="spread_weights",
    )(place, *pieces, *after)
    return [weight.reshape(-1, weight.shape[3]) for weight in weights]


def gate(array, after):
    return pl.pallas_call(
        lambda *refs: None,
        in_specs=[ANY] * (1 + len(after)),
        out_specs=ANY,
        out_shape=jax.ShapeDtypeStruct(array.shape, array.dtype),
        input_output_aliases={0: 0},
        cost_estimate=cost(0.5, 512),
        name="gate",
        compiler_params=pltpu.CompilerParams(vmem_limit_bytes=VMEM_LIMIT),
    )(array, *after)


def relay_kernel(x_ref, y_ref, *refs):
    a_ref, b_ref, _, _, sems = refs[-5:]
    half = a_ref.shape[0]
    run_copies([(x_ref.at[pl.ds(0, half)], a_ref), (y_ref.at[pl.ds(half, half)], b_ref)], sems)


def relay(over_x, over_y, after):
    half = jax.ShapeDtypeStruct((over_x.shape[0] // 2, over_x.shape[1]), over_x.dtype)
    whole = jax.ShapeDtypeStruct(over_x.shape, over_x.dtype)
    a, b, over_x, over_y = pl.pallas_call(
        relay_kernel,
        in_specs=[ANY] * (2 + len(after)),
        out_specs=[VMEM] * 2 + [ANY] * 2,
        out_shape=[half] * 2 + [whole] * 2,
        input_output_aliases={0: 2, 1: 3},
        scratch_shapes=[pltpu.SemaphoreType.DMA((2,))],
        cost_estimate=cost(2.5, 512),
        name="relay",
        compiler_params=pltpu.CompilerParams(vmem_limit_bytes=VMEM_LIMIT),
    )(over_x, over_y, *after)
    return (a, b), (over_x, over_y)


def core_groups():
    return [list(range(core, lax.axis_size("fsdp"), 2)) for core in range(2)]


def gather_chips(packed):
    return lax.all_gather(packed, "fsdp", axis=0, axis_index_groups=core_groups(), tiled=True)


def scatter_chips(total):
    return lax.psum_scatter(total, "fsdp", scatter_dimension=0, axis_index_groups=core_groups(), tiled=True)


def first_round(block):
    return other(block, "seq", 1), other(block, "seq", 2)


def second_round(passed):
    return other(passed[0], "seq", 2), other(passed[1], "seq", 1)


def interleaved(ref, core):
    blocks = ref.shape[1] // 256
    return jnp.concatenate([ref[:, aligned(2 * z + core, 128)] for z in range(blocks)], axis=1)


def grad_pieces_kernel(place_ref, *refs, count):
    ins, (o0_ref, o1_ref, o2_ref, oa_ref, ob_ref), scratch = refs[: 4 * count], refs[-6 - count : -1 - count], refs[-1 - count :]
    lefts, rights, turned, total = ins[: 2 * count], ins[2 * count :], scratch[:count], scratch[count]
    step = pl.program_id(0)
    tokens = lefts[0].shape[0]

    @pl.when(step == 0)
    def _():
        for i in range(2 * count):
            turned[i // 2][:, pl.ds((i % 2) * tokens, tokens)] = interleaved(lefts[i], place_ref[1]).T

    start = 0
    for i in range(count):
        a_ref, b_ref = rights[2 * i : 2 * i + 2]
        size = a_ref.shape[-1]
        a, b = [ref[0] if len(ref.shape) == 3 else ref[...] for ref in (a_ref, b_ref)]
        total[:, pl.ds(start, size)] = (
            dot_nn(turned[i][:, pl.ds(0, tokens)], a) + dot_nn(turned[i][:, pl.ds(tokens, tokens)], b)
        ).astype(bf16)
        start += size
    half = total.shape[0] // 2
    for i, out in enumerate((o0_ref, o1_ref, o2_ref)):

        @pl.when(step == i)
        def _(out=out):
            out[...] = total[...]

    @pl.when(step == 3)
    def _():
        oa_ref[...] = total[pl.ds(0, half), :]
        ob_ref[...] = total[pl.ds(half, half), :]


def grad_pieces(place, pairs, after):
    lefts = [left for pair in pairs for left in pair[0]]
    rights = [right for pair in pairs for right in pair[1]]
    tokens, rows = lefts[0].shape[0], lefts[0].shape[1] // 2
    sizes = [right.size // tokens // 4 for right in rights]
    width = sum(sizes[::2])
    whole = lambda array: pl.BlockSpec(array.shape, lambda j, place_ref: (0, 0))

    def quarter(right, size):
        if right.ndim == 2:
            return pl.BlockSpec((tokens, size), lambda j, place_ref: (0, place_ref[0] ^ j))
        return pl.BlockSpec(
            (1, tokens, size), lambda j, place_ref: ((place_ref[0] ^ j) // 2, 0, lax.rem(place_ref[0] ^ j, 2))
        )

    shapes = [(rows, width)] * 3 + [(rows // 2, width)] * 2
    return pl.pallas_call(
        partial(grad_pieces_kernel, count=len(pairs)),
        grid_spec=pltpu.PrefetchScalarGridSpec(
            num_scalar_prefetch=1,
            grid=(4,),
            in_specs=[whole(left) for left in lefts] + [quarter(right, size) for right, size in zip(rights, sizes)] + [ANY] * len(after),
            out_specs=[pl.BlockSpec(shape, lambda j, place_ref: (0, 0)) for shape in shapes],
            scratch_shapes=[pltpu.VMEM((rows, 2 * tokens), bf16) for _ in pairs] + [pltpu.VMEM((rows, width), bf16)],
        ),
        out_shape=[jax.ShapeDtypeStruct(shape, bf16) for shape in shapes],
        compiler_params=pltpu.CompilerParams(vmem_limit_bytes=VMEM_LIMIT),
        cost_estimate=cost(12, 512),
        name="grad_pieces",
    )(place, *lefts, *rights, *after)


def settle_kernel(place_ref, *refs, sizes):
    pieces, outs = refs[:5], refs[-len(sizes) :]
    rows = pieces[0].shape[0]
    masks = ((0, 0, rows), (1, 0, rows), (2, 0, rows), (3, 0, rows // 2), (3, rows // 2, rows // 2))
    for piece, (mask, at, count) in zip(pieces, masks):
        for out_ref, start, size in zip(outs, offsets(sizes), sizes):
            out_ref[0, pl.ds(at, count), aligned(place_ref[0] ^ mask, size)] = piece[:, pl.ds(start, size)].astype(f32)


def settle(place, pieces, sizes, layer, so_far):
    rows = pieces[0].shape[0]
    whole = lambda array: pl.BlockSpec(array.shape, lambda i: (0, 0))
    return pl.pallas_call(
        partial(settle_kernel, sizes=sizes),
        grid=(1,),
        in_specs=[SMEM] + [whole(piece) for piece in pieces] + [ANY] * len(so_far),
        out_specs=[pl.BlockSpec((1, rows, 4 * size), lambda i: (layer, 0, 0)) for size in sizes],
        out_shape=[jax.ShapeDtypeStruct((LAYERS, rows, 4 * size), f32) for size in sizes],
        input_output_aliases={6 + i: i for i in range(len(so_far))},
        compiler_params=pltpu.CompilerParams(vmem_limit_bytes=VMEM_LIMIT),
        cost_estimate=cost(3, 512),
        name="settle_gradient",
    )(place, *pieces, *so_far)


def merge_kernel(x_ref, y_ref, a_ref, b_ref, *refs):
    ox_ref, oy_ref = refs[-2:]
    ox_ref[...] = (x_ref[...].astype(f32) + b_ref[...].astype(f32)).astype(bf16)
    oy_ref[...] = (y_ref[...].astype(f32) + a_ref[...].astype(f32)).astype(bf16)


def merge(over_x, over_y, diag_a, diag_b, after):
    half, width = diag_a.shape
    rows = half // 4
    lower = pl.BlockSpec((rows, width), lambda i: (i, 0))
    upper = pl.BlockSpec((rows, width), lambda i: (i + 4, 0))
    whole = jax.ShapeDtypeStruct(over_x.shape, bf16)
    return pl.pallas_call(
        merge_kernel,
        grid=(4,),
        in_specs=[upper, lower, lower, lower] + [ANY] * len(after),
        out_specs=[upper, lower],
        out_shape=[whole, whole],
        input_output_aliases={0: 0, 1: 1},
        compiler_params=pltpu.CompilerParams(vmem_limit_bytes=VMEM_LIMIT),
        cost_estimate=cost(3.5, 512),
        name="merge",
    )(over_x, over_y, diag_a, diag_b, *after)


def total_kernel(own_ref, x_ref, y_ref, *refs):
    refs[-1][...] = (own_ref[...].astype(f32) + x_ref[...].astype(f32) + y_ref[...].astype(f32)).astype(bf16)


def total_of(own, from_x, from_y, after):
    rows, width = own.shape
    block = pl.BlockSpec((rows // 4, width), lambda i: (i, 0))
    return pl.pallas_call(
        total_kernel,
        grid=(4,),
        in_specs=[block] * 3 + [ANY] * len(after),
        out_specs=block,
        out_shape=jax.ShapeDtypeStruct(own.shape, bf16),
        compiler_params=pltpu.CompilerParams(vmem_limit_bytes=VMEM_LIMIT),
        cost_estimate=cost(4, 512),
        name="total",
    )(own, from_x, from_y, *after)


def gather_start(scattered, after):
    block = gate(scattered, after) if after else scattered
    return block, first_round(block)


def gather_settle(place, block, over, sizes, layer, so_far, after):
    passed, over = relay(*over, after)
    pieces = [block, *over, *second_round(passed)]
    return settle(place, pieces, sizes, layer, so_far), passed


def small_kernel(*refs):
    ins, out_ref = refs[:-1], refs[-1]
    at = 0
    out_ref[...] = jnp.zeros_like(out_ref)
    for ref in ins:
        for start in range(0, ref.shape[1], D):
            size = min(D, ref.shape[1] - start)
            out_ref[pl.ds(at, ref.shape[0]), pl.ds(0, size)] = ref[:, pl.ds(start, size)]
            at += ref.shape[0]


def small_rows(arrays):
    counts = [array.shape[0] * -(-array.shape[1] // D) for array in arrays]
    packed = pl.pallas_call(
        small_kernel,
        in_specs=[VMEM] * len(arrays),
        out_specs=VMEM,
        out_shape=jax.ShapeDtypeStruct((-(-sum(counts) // 8) * 8, D), f32),
        cost_estimate=cost(2, 512),
        name="small_rows",
        compiler_params=pltpu.CompilerParams(vmem_limit_bytes=VMEM_LIMIT),
    )(*arrays)
    return packed, offsets(counts)


def small_part(packed, start, shape):
    parts = -(-shape[1] // D)
    rows = [packed[start + i * shape[0] : start + (i + 1) * shape[0], : min(D, shape[1])] for i in range(parts)]
    return jnp.concatenate(rows, axis=1)


epsilon_norm = EPS_NORM


def shifted(block, axis, distance):
    devices = range(lax.axis_size(axis))
    route = [(i - distance, i) for i in devices if i - distance in devices]
    return lax.ppermute(block, axis, route)


def root_norm(values, gain):
    return (
        values * lax.rsqrt(jnp.mean(values * values, axis=-1, keepdims=True) + epsilon_norm) * gain
    )


def swiglu_act(gate_up):
    half_width = gate_up.shape[1] // 2
    return jax.nn.silu(gate_up[:, :half_width]) * gate_up[:, half_width:]


def contract_last(left, right):
    return lax.dot_general(
        left, right, (((1,), (1,)), ((), ())), preferred_element_type=jnp.float32
    )


def contract_first(left, right):
    return lax.dot_general(
        left, right, (((0,), (0,)), ((), ())), preferred_element_type=jnp.float32
    )


def fetch_rows(weights):
    return lax.all_gather(weights, "fsdp", axis=0, tiled=True)


def reduce_rows(left, right):
    return lax.psum_scatter(
        contract_first(left, right).astype(jnp.bfloat16), "fsdp", scatter_dimension=0, tiled=True
    )


def documents(segments, rows):
    doc_pad = jnp.concatenate([jnp.full((HALO,), -1, jnp.int32), segments])
    dcol = lax.dynamic_slice_in_dim(doc_pad, lax.axis_index("seq") * rows, rows + HALO)
    return dcol[:, None], dcol[HALO:].reshape(rows // CHUNK, CHUNK)


def on_device(
    tokens,
    segments,
    valid_mask,
    norm_gains,
    head_gain,
    conv_weight,
    beta_weight,
    qkv_weight,
    out_weight,
    gate_up_weight,
    down_weight,
    cotangent,
):
    rows = tokens.shape[1]
    pieces = lax.axis_size("seq")
    dcol, drow = documents(segments[0], rows)
    place = jnp.stack([lax.axis_index("seq"), lax.axis_index("fsdp") % 2]).astype(jnp.int32)
    valid_rows = valid_mask[0].astype(jnp.float32)
    stream = tokens[0].astype(jnp.float32)
    square_sums = []
    stored = []
    for at in range(LAYERS):
        qkv_full = fetch_rows(qkv_weight[at])
        out_full = fetch_rows(out_weight[at])
        gate_up_full = fetch_rows(gate_up_weight[at])
        down_full = fetch_rows(down_weight[at])
        square_sums.append(jnp.sum(jnp.sum(stream * stream, axis=1) * valid_rows))
        normed_one, pull_one = jax.vjp(root_norm, stream, norm_gains[at, 0])
        normed_one = normed_one.astype(jnp.bfloat16)
        projected = jnp.dot(normed_one, qkv_full, preferred_element_type=jnp.float32).astype(bf16)
        logits = jnp.dot(normed_one, beta_weight[at], preferred_element_type=jnp.float32).astype(bf16)
        logits = jnp.pad(logits, ((0, 0), (0, HD - H)))
        projected = jnp.concatenate([shifted(projected[rows - HALO :], "seq", 1), projected], axis=0)
        qn, kn, tinv, wu, step, pre, total = fwd_local(
            projected, conv_weight[at], logits, dcol, drow, []
        )
        nears = [shifted(total, "seq", d) for d in range(1, pieces - 1)]
        far = shifted(total[:, :, HD:], "seq", pieces - 1)
        moves = [shifted(total[:, :, :HD], "seq", -d) for d in range(1, pieces - 1)]
        reads, local_out = fwd_read(qn, kn, wu, dcol, drow)
        state, mixed, attended = fwd_state(
            place, False, nears, far, pre, reads, local_out, head_gain[at][None], []
        )
        branch = jnp.dot(attended, out_full, preferred_element_type=jnp.float32)
        square_sums.append(jnp.sum(jnp.sum(branch * branch, axis=1) * valid_rows))
        stream = stream + branch
        normed_two, pull_two = jax.vjp(root_norm, stream, norm_gains[at, 1])
        normed_two = normed_two.astype(jnp.bfloat16)
        gate_up = jnp.dot(normed_two, gate_up_full, preferred_element_type=jnp.float32)
        activated, pull_act = jax.vjp(swiglu_act, gate_up)
        activated = activated.astype(jnp.bfloat16)
        branch = jnp.dot(activated, down_full, preferred_element_type=jnp.float32)
        square_sums.append(jnp.sum(jnp.sum(branch * branch, axis=1) * valid_rows))
        stream = stream + branch
        stored.append(
            (
                qkv_full, out_full, gate_up_full, down_full, pull_one, normed_one, attended, pull_two, normed_two,
                pull_act, activated, moves, mixed,
                (projected, conv_weight[at], logits, dcol, drow, tinv, wu, step, state, reads),
            )
        )
    stream_grad = cotangent[0].astype(jnp.float32) * valid_rows[:, None]
    gain_list = []
    head_list = []
    filter_list = []
    beta_list = []
    weight_list = []
    for at in reversed(range(LAYERS)):
        (
            qkv_full, out_full, gate_up_full, down_full, pull_one, normed_one, attended, pull_two, normed_two,
            pull_act, activated, moves, mixed, kept,
        ) = stored[at]
        step, reads = kept[7], kept[9]
        branch_low = stream_grad.astype(jnp.bfloat16)
        grad_down = reduce_rows(activated, branch_low)
        (grad_gate_up,) = pull_act(contract_last(branch_low, down_full))
        grad_gate_up = grad_gate_up.astype(jnp.bfloat16)
        grad_gate = reduce_rows(normed_two, grad_gate_up)
        grad_state, gain_two = pull_two(contract_last(grad_gate_up, gate_up_full))
        stream_grad = stream_grad + grad_state
        branch_low = stream_grad.astype(jnp.bfloat16)
        grad_out = reduce_rows(attended, branch_low)
        grad_heads = contract_last(branch_low, out_full).astype(jnp.bfloat16)
        grad_mixed, gain_head, total = bwd_local(
            grad_heads, mixed, reads, head_gain[at][None], step, dcol, []
        )
        gives = [shifted(total, "seq", -d) for d in range(1, pieces)]
        grad_proj, *parts, grad_logits = bwd_main(place, False, moves, gives, *kept, grad_mixed, [])
        grad_logits = grad_logits[:, :H]
        rim = shifted(jnp.concatenate(parts[:3], axis=1), "seq", -1)
        grad_filter = jnp.concatenate(parts[3:6], axis=1)
        grad_proj = grad_proj.at[rows - HALO :].add(rim)
        grad_qkv = reduce_rows(normed_one, grad_proj)
        grad_beta = contract_first(normed_one, grad_logits)
        grad_normed = contract_last(grad_proj, qkv_full) + contract_last(grad_logits, beta_weight[at])
        grad_state, gain_one = pull_one(grad_normed)
        stream_grad = stream_grad + grad_state
        weight_list.append(
            [lax.psum(grad, "seq").astype(f32) for grad in (grad_qkv, grad_out, grad_gate, grad_down)]
        )
        gain_list.append(jnp.stack([gain_one, gain_two]))
        head_list.append(gain_head[0])
        filter_list.append(grad_filter)
        beta_list.append(grad_beta)
    stats_sum, valid_count, gains_sum, head_sum, filter_sum, beta_sum = lax.psum(
        (
            jnp.stack(square_sums),
            jnp.sum(valid_rows),
            jnp.stack(gain_list[::-1]),
            jnp.stack(head_list[::-1]),
            jnp.stack(filter_list[::-1]),
            jnp.stack(beta_list[::-1]),
        ),
        ("seq", "fsdp"),
    )
    rms_stats = jnp.sqrt(stats_sum / (jnp.maximum(valid_count, 1.0) * D)).reshape(LAYERS, 3)
    return (
        stream.astype(jnp.bfloat16)[None],
        stream_grad[None],
        gains_sum,
        head_sum,
        filter_sum,
        beta_sum,
        *[jnp.stack(pair[::-1]) for pair in zip(*weight_list)],
        rms_stats,
    )


def on_device_axes(
    tokens,
    segments,
    valid_mask,
    norm_gains,
    head_gain,
    conv_weight,
    beta_weight,
    qkv_weight,
    out_weight,
    gate_up_weight,
    down_weight,
    cotangent,
):
    rows = tokens.shape[1]
    dcol, drow = documents(segments[0], rows)
    place = jnp.stack([lax.axis_index("seq"), lax.axis_index("fsdp") % 2]).astype(jnp.int32)
    valid_rows = valid_mask[0].astype(f32)
    near = lambda array: (array, other(array, "fsdp", 1))
    size_qkv, size_out, size_gate = [weight.shape[2] // 4 for weight in (qkv_weight, out_weight, gate_up_weight)]
    sizes_one, sizes_two = (size_qkv, size_out), (size_gate,)
    groups = []
    for at in range(LAYERS):
        groups += [((qkv_weight, out_weight), at), ((gate_up_weight,), at)]
    packs = pack(place, groups[:1], [])
    packs += pack(place, groups[1:], packs)
    blocks, downs = [], []
    for at in range(LAYERS):
        blocks += [gather_chips(packed) for packed in packs[2 * at : 2 * at + 2]]
        downs.append(lax.all_gather(down_weight[at], "fsdp", axis=0, tiled=True))

    def launch(block, after):
        block = gate(block, after) if after else block
        return block, first_round(block)

    def finish(block, over, after):
        near_block = other(block, "fsdp", 1)
        passed, over = relay(*over, [near_block, *after])
        near_over = [other(piece, "fsdp", 1) for piece in over]
        return [block, *over], [near_block, *near_over], second_round(passed), passed

    def complete(came, after):
        own, near_own, passed, _ = came
        passed = [gate(piece, after) if after else piece for piece in passed]
        return [*own, *passed, *near_own, *[other(piece, "fsdp", 1) for piece in passed]]

    stream = tokens[0].astype(f32)
    tail = shifted(tokens[0, rows - HALO :], "seq", 1).astype(f32)
    valid = valid_rows[:, None]
    betas = jnp.pad(beta_weight, ((0, 0), (0, 0), (0, HD - H)))
    gains = lambda at, which: norm_gains[at, which][None]
    square_sums = [jnp.sum(stream * stream * valid, axis=0)[None]]
    normed = root_norm(stream, gains(0, 0)).astype(bf16)
    ready = [tail, betas, normed, dcol, drow, valid, stream, *square_sums]
    parts_one = complete(finish(*launch(blocks[0], []), ready), [])
    coming = launch(blocks[1], parts_one[-2:])
    stored = []
    for at in range(LAYERS):
        normed_one = near(normed)
        qkv_full, out_full = spread(place, parts_one, sizes_one, [])
        projected, logits = project(tail, gains(at, 0), normed, qkv_full, betas[at], [])
        qn, kn, tinv, wu, step, pre, total = fwd_local(
            projected, conv_weight[at], logits, dcol, drow, normed_one[1:]
        )
        partner = other(total, "seq", 1)
        reads, local_out = fwd_read(qn, kn, wu, dcol, drow)
        pair = pair_state(pair_forward_kernel, place, total, partner)
        far = other(pair, "seq", 2)
        came = finish(*coming, [far, reads])
        state, mixed, attended = fwd_state(
            place, True, [partner], far, pre, reads, local_out, head_gain[at][None], [*came[1], *came[3]]
        )
        parts_two = complete(came, [attended])
        attended = near(attended)
        after_mix, normed, sums = branch(attended[0], out_full, stream, valid, gains(at, 1), False, [], 1)
        normed_two = near(normed)
        (gate_up_full,) = spread(place, parts_two, sizes_two, [*attended, normed])
        more = at + 1 < LAYERS
        if more:
            coming = launch(blocks[2 * at + 2], parts_two[3:5])
        activated, both = gated(normed, gate_up_full, [], 2)
        passed = []
        if more:
            came = finish(*coming, [activated, *normed_two])
            passed = came[3]
        new_stream, normed, more_sums = branch(
            activated, downs[at], after_mix, valid, gains((at + 1) % LAYERS, 0), not more, passed, 2
        )
        if more:
            parts_one = complete(came, [new_stream])
            tail = shifted(new_stream[rows - HALO :], "seq", 1)
            coming = launch(blocks[2 * at + 3], [*parts_one[-2:], tail])
        square_sums += [sums[:1], more_sums[:1], more_sums[1:]]
        stored.append(
            (
                qkv_full, out_full, gate_up_full, downs[at], stream, normed_one, attended, after_mix,
                normed_two, both, activated, (total, partner), mixed,
                (projected, conv_weight[at], logits, dcol, drow, tinv, wu, step, state, reads),
            )
        )
        stream = new_stream
    result = normed
    g = cotangent[0].astype(f32) * valid
    g_low = g.astype(bf16)
    small = []
    waiting = []
    downs = []
    result_qkv, result_out, result_gate = [], [], []
    for at in reversed(range(LAYERS)):
        (
            qkv_full, out_full, gate_up_full, down_full, stream, normed_one, attended, after_mix,
            normed_two, both, activated, states, mixed, kept,
        ) = stored[at]
        step, reads = kept[7], kept[9]
        started = []
        last_low = g_low
        if waiting:
            grad_down = contract_first(gate(activated, [scattered, waiting[0]]), g_low).astype(bf16)
            own, over_x, over_y, diag_a, diag_b = waiting
            over_x, over_y = merge(over_x, over_y, diag_a, diag_b, [grad_down])
            above = (own, other(over_x, "seq", 1), other(over_y, "seq", 2))
            block, over = gather_start(scattered, [over_x])
            started = [block]
        grad_gate_up = gated_back(g_low, down_full, both, [over_x, downs[-1]] if waiting else [], 2)
        grad_gate_up = near(grad_gate_up)
        g, g_low, gain_two = norm_back(
            grad_gate_up[0], gate_up_full, (), after_mix, g, gains(at, 1), started
        )
        branch_low = near(g_low)
        pairs_one = [(normed_two, grad_gate_up)]
        out_pair = (attended, branch_low)
        if waiting:
            pairs_one.append(out_pair)
        own, over_x, over_y, diag_a, diag_b = grad_pieces(place, pairs_one, [gain_two])
        diag_a, diag_b = other(diag_a, "seq", 1), other(diag_b, "seq", 2)
        done = [own]
        if waiting:
            reduced = total_of(*above, [own])
            above = scatter_chips(reduced)
            result_gate, passed = gather_settle(place, block, over, (size_gate,), at + 1, [], [own])
            done = [own, reduced, *passed]
        grad_heads = contract_last(branch_low[0], out_full).astype(bf16)
        grad_mixed, gain_head, total = bwd_local(
            grad_heads, mixed, reads, head_gain[at][None], step, dcol, done
        )
        partner = other(total, "seq", 1)
        if not waiting:
            grad_down = contract_first(gate(activated, [total]), last_low).astype(bf16)
        ordered = grad_down
        grad_down = lax.psum_scatter(grad_down, "fsdp", scatter_dimension=0, tiled=True)
        pair = pair_state(pair_backward_kernel, place, *states, total, partner, after=[ordered])
        gives = [partner, other(pair, "seq", 2)]
        over_x, over_y = merge(over_x, over_y, diag_a, diag_b, [gives[1], *result_gate])
        from_x, from_y = other(over_x, "seq", 1), other(over_y, "seq", 2)
        grad_proj, *parts, grad_logits = bwd_main(
            place, True, states[1:], gives, *kept, grad_mixed,
            [over_x, *branch_low[1:], *([above] if waiting else [])],
        )
        rim = shifted(jnp.concatenate(parts[:3], axis=1), "seq", -1)
        reduced = total_of(own, from_x, from_y, [grad_proj])
        scattered = scatter_chips(reduced)
        grad_proj = near(gate(grad_proj, [reduced]).at[rows - HALO :].add(rim))
        grad_beta = contract_first(grad_logits[:, :H], normed_one[0])
        grad_down = gate(grad_down, [reduced])
        grad_down = grad_down + other(grad_down, "seq", 1)
        g, g_low, gain_one = norm_back(
            grad_proj[0], qkv_full, (grad_logits, betas[at]), stream, g, gains(at, 0), [reduced]
        )
        pairs_two = [(normed_one, grad_proj)]
        started = [gain_one, grad_down]
        if waiting:
            block, over = gather_start(above, [reduced])
            started += [block]
        else:
            pairs_two.append(out_pair)
        grad_down = gate(grad_down, [gain_one])
        taken = other(grad_down, "seq", 2)
        own, over_x, over_y, diag_a, diag_b = grad_pieces(place, pairs_two, started)
        if waiting:
            (result_qkv, result_out), passed = gather_settle(
                place, block, over, (size_qkv, size_out), at + 1, [], [own]
            )
        downs.append(grad_down + gate(taken, [own]))
        waiting = own, over_x, over_y, other(diag_a, "seq", 1), other(diag_b, "seq", 2)
        small += [gain_one, gain_two, gain_head, *parts[3:6], grad_beta]
    small += [*square_sums[: 3 * LAYERS], jnp.broadcast_to(jnp.sum(valid_rows), (1, D))]
    packed, starts = small_rows(small)
    own, over_x, over_y, diag_a, diag_b = waiting
    over_x, over_y = merge(over_x, over_y, diag_a, diag_b, [packed, downs[-1], *passed])
    from_x, from_y = other(over_x, "seq", 1), other(over_y, "seq", 2)
    packed = sum_over(gate(packed, [over_x]), "fsdp")
    reduced = total_of(own, from_x, from_y, [packed, result_out])
    last = scatter_chips(reduced)
    packed = sum_over(gate(packed, [reduced]), "seq")
    block, over = gather_start(scattered, [reduced])
    (result_gate, result_out), _ = gather_settle(
        place, block, over, (size_gate, size_out), 0, [*result_gate, result_out], []
    )
    block, over = gather_start(last, [packed, result_gate])
    (result_qkv,), _ = gather_settle(place, block, over, (size_qkv,), 0, [result_qkv], [])
    summed = [small_part(packed, start, array.shape) for start, array in zip(starts, small)]
    of_layer = lambda at: summed[7 * (LAYERS - 1 - at) : 7 * (LAYERS - at)]
    by_layer = lambda pick: jnp.stack([pick(of_layer(at)) for at in range(LAYERS)])
    stats = jnp.concatenate(summed[7 * LAYERS : -1], axis=0)
    count = summed[-1][0, 0]
    rms_stats = jnp.sqrt(jnp.sum(stats, axis=1) / (jnp.maximum(count, 1.0) * D)).reshape(LAYERS, 3)
    return (
        result[None],
        g[None],
        by_layer(lambda arrays: jnp.concatenate(arrays[:2], axis=0)),
        by_layer(lambda arrays: arrays[2][0]),
        by_layer(lambda arrays: jnp.concatenate(arrays[3:6], axis=1)),
        by_layer(lambda arrays: arrays[6].T),
        result_qkv,
        result_out,
        result_gate,
        jnp.stack(downs[::-1]).astype(f32),
        rms_stats,
    )


def solution(mesh):
    axes = mesh.shape["seq"] == 4 and mesh.shape["fsdp"] == 8
    return jax.shard_map(
        on_device_axes if axes else on_device,
        mesh=mesh,
        in_specs=(
            P("fsdp", "seq", None),
            P("fsdp", None),
            P("fsdp", "seq"),
            P(),
            P(),
            P(),
            P(),
            P(None, "fsdp", None),
            P(None, "fsdp", None),
            P(None, "fsdp", None),
            P(None, "fsdp", None),
            P("fsdp", "seq", None),
        ),
        out_specs=(
            P("fsdp", "seq", None),
            P("fsdp", "seq", None),
            P(),
            P(),
            P(),
            P(),
            P(None, "fsdp", None),
            P(None, "fsdp", None),
            P(None, "fsdp", None),
            P(None, "fsdp", None),
            P(),
        ),
        check_vma=False,
    )
```

```python
from functools import partial
import jax
import jax.numpy as jnp
from jax import lax
from jax.experimental import pallas as pl
from jax.experimental.pallas import tpu as pltpu
from jax.sharding import PartitionSpec as P

D = 1024
H = 8
HD = 128
KW = 4
LAYERS = 2
CHUNK = 128
TOGETHER = 4
TOGETHER_BACK = 2
HALO = 16
f32 = jnp.float32
bf16 = jnp.bfloat16
EPS_NORM = 1e-05
EPS_UNIT = 1e-06
VMEM_LIMIT = 60 * 1024 * 1024


def dot_nn(a, b):
    return lax.dot_general(a.astype(bf16), b.astype(bf16), (((1,), (0,)), ((), ())), preferred_element_type=f32)


def dot_nt(a, b):
    return lax.dot_general(a.astype(bf16), b.astype(bf16), (((1,), (1,)), ((), ())), preferred_element_type=f32)


def dot_tn(a, b):
    return lax.dot_general(a.astype(bf16), b.astype(bf16), (((0,), (0,)), ((), ())), preferred_element_type=f32)


def sigmoid(x):
    return 1.0 / (1.0 + jnp.exp(-x))


def conv_masks(dcol_ref, rows):
    here = dcol_ref[pl.ds(HALO, rows), :]
    return [
        jnp.broadcast_to((dcol_ref[pl.ds(HALO - KW + 1 + i, rows), :] == here).astype(f32), (rows, HD))
        for i in range(KW - 1)
    ]


def conv_sum(x_ref, taps_ref, masks, ext, h):
    rows = x_ref.shape[0] - HALO
    lanes = pl.ds(h * HD, HD)
    ext[...] = x_ref[:, lanes].astype(f32)
    total = taps_ref[pl.ds(KW - 1, 1), lanes] * ext[pl.ds(HALO, rows), :]
    for i in range(KW - 1):
        total = total + taps_ref[pl.ds(i, 1), lanes] * ext[pl.ds(HALO - KW + 1 + i, rows), :] * masks[i]
    return total


def low(x):
    return x.astype(bf16).astype(f32)


def unit_scale(x):
    return lax.rsqrt(jnp.sum(x * x, axis=-1, keepdims=True) + EPS_UNIT)


def head_column(table, head):
    lane = lax.broadcasted_iota(jnp.int32, table.shape, 1)
    return jnp.sum(jnp.where(lane == head, table, 0.0), axis=1, keepdims=True)


def chunk_marks(dcol_ref, c):
    at = HALO + c * CHUNK
    docs = dcol_ref[pl.ds(at, CHUNK), :]
    prior = dcol_ref[pl.ds(at - 1, 1), :]
    last = dcol_ref[pl.ds(at + CHUNK - 1, 1), :]
    carry = (docs == prior).astype(f32)
    tail = (docs == last).astype(f32)
    carry_last = (last == prior).astype(f32)
    return docs, carry, tail, carry_last


def tri_index():
    row = lax.broadcasted_iota(jnp.int32, (CHUNK, CHUNK), 0)
    col = lax.broadcasted_iota(jnp.int32, (CHUNK, CHUNK), 1)
    return row, col


def inverses(systems, differ):
    row, col = tri_index()
    eye = (row == col).astype(f32)
    found = [eye - jnp.where(differ == 1, low_part, 0.0) for low_part in systems]
    step = 2
    while step < CHUNK:
        side = (differ >= step) & (differ < 2 * step)
        lows = [x.astype(bf16) for x in found]
        inner = [dot_nn(jnp.where(side, s, 0.0), x) for s, x in zip(systems, lows)]
        outer = [dot_nn(x, y) for x, y in zip(lows, inner)]
        found = [x - y for x, y in zip(found, outer)]
        step *= 2
    return found


def fwd_local_kernel(
    q_ref, k_ref, v_ref, tq_ref, tk_ref, tv_ref, lg_ref, dcol_ref, drow_ref, *refs,
):
    qn_ref, kn_ref, tinv_ref, wu_ref, gain_ref, pre_ref, total_ref, ext = refs[-8:]
    group = pl.program_id(0)
    rows = q_ref.shape[0] - HALO
    chunks = rows // CHUNK
    masks = conv_masks(dcol_ref, rows)
    heads = range(q_ref.shape[1] // HD)

    def filtered(x, taps, h):
        s = conv_sum(x, taps, masks, ext.at[h], h)
        return low(s * sigmoid(s))

    queries = [filtered(q_ref, tq_ref, h) for h in heads]
    keys = [filtered(k_ref, tk_ref, h) for h in heads]
    values = [filtered(v_ref, tv_ref, h) for h in heads]
    kns, kbs, vbs = [], [], []
    for h in heads:
        lanes = pl.ds(h * HD, HD)
        qn_ref[:, lanes] = (queries[h] * (unit_scale(queries[h]) * HD**-0.5)).astype(bf16)
        kn = keys[h] * unit_scale(keys[h])
        kn_ref[:, lanes] = kn.astype(bf16)
        beta = sigmoid(head_column(lg_ref[...].astype(f32), group * len(heads) + h))
        kns.append(kn.astype(bf16))
        kbs.append((beta * kn).astype(bf16))
        vbs.append((beta * values[h]).astype(bf16))
    row, col = tri_index()
    differ = row ^ col
    marks = [chunk_marks(dcol_ref, c) for c in range(chunks)]
    cut = lambda x, c: x[c * CHUNK : (c + 1) * CHUNK]
    items = [(h, c) for h in heads for c in range(chunks)]
    keeps = [(marks[c][0] == drow_ref[pl.ds(c, 1), :]) & (col < row) for c in range(chunks)]
    systems = [dot_nt(cut(kbs[h], c), cut(kns[h], c)) for h, c in items]
    systems = [jnp.where(keeps[c], s, 0.0) for s, (h, c) in zip(systems, items)]
    found = [x.astype(bf16) for x in inverses(systems, differ)]
    both = [
        dot_nn(x, jnp.concatenate([cut(kbs[h], c), cut(vbs[h], c)], axis=1)) for x, (h, c) in zip(found, items)
    ]
    tails = [(cut(kns[h], c).astype(f32) * marks[c][2]).astype(bf16) for h, c in items]
    moved = [
        jnp.concatenate([(b[:, :HD] * marks[c][1]).astype(bf16), b[:, HD:].astype(bf16)], axis=1)
        for b, (h, c) in zip(both, items)
    ]
    steps = [dot_tn(t, m) for t, m in zip(tails, moved)]
    for i, (h, c) in enumerate(items):
        at = pl.ds(c * CHUNK, CHUNK)
        tinv_ref[h, at, :] = found[i]
        wu_ref[h, at, :] = both[i].astype(bf16)
        gain_ref[h, at, :] = steps[i][:, :HD].astype(bf16)
    eye = (row == col).astype(f32)
    states = [jnp.concatenate([eye, jnp.zeros_like(eye)], axis=1) for _ in heads]
    for c in range(chunks):
        lows = [state.astype(bf16) for state in states]
        for h in heads:
            pre_ref[h, pl.ds(c * CHUNK, CHUNK), :] = lows[h]
        gone = [dot_nn(steps[h * chunks + c][:, :HD], lows[h]) for h in heads]
        states = [
            marks[c][3] * states[h]
            - gone[h]
            + jnp.concatenate([jnp.zeros_like(eye), steps[h * chunks + c][:, HD:]], axis=1)
            for h in heads
        ]
    for h in heads:
        total_ref[h] = states[h].astype(bf16)


def col_spec(rows, base, count=1):
    return pl.BlockSpec((rows, count * HD), lambda h: (0, base // count + h))


def full_spec(shape):
    return pl.BlockSpec(shape, lambda h: (0,) * len(shape))


def head_spec(shape, count=1):
    return pl.BlockSpec((count,) + shape, lambda h: (h,) + (0,) * len(shape))


def params():
    return pltpu.CompilerParams(vmem_limit_bytes=VMEM_LIMIT, dimension_semantics=("arbitrary",))


def cost(micros, rows):
    return pl.CostEstimate(flops=0, bytes_accessed=int(micros * 3.69e6 * rows / 512), transcendentals=0)


def fwd_local(projected, taps, logits, dcol, drow, after):
    rows = projected.shape[0] - HALO
    chunks = rows // CHUNK
    sds = jax.ShapeDtypeStruct
    return pl.pallas_call(
        fwd_local_kernel,
        grid=(H // TOGETHER,),
        in_specs=[col_spec(rows + HALO, i * H, TOGETHER) for i in range(3)]
        + [col_spec(KW, 0, TOGETHER), col_spec(KW, H, TOGETHER), col_spec(KW, 2 * H, TOGETHER)]
        + [full_spec((rows, HD)), full_spec((rows + HALO, 1)), full_spec((chunks, CHUNK))]
        + [pl.BlockSpec(memory_space=pl.ANY) for _ in after],
        out_specs=[
            col_spec(rows, 0, TOGETHER),
            col_spec(rows, 0, TOGETHER),
            head_spec((rows, CHUNK), TOGETHER),
            head_spec((rows, 2 * HD), TOGETHER),
            head_spec((rows, HD), TOGETHER),
            head_spec((rows, 2 * HD), TOGETHER),
            head_spec((HD, 2 * HD), TOGETHER),
        ],
        out_shape=[
            sds((rows, D), bf16),
            sds((rows, D), bf16),
            sds((H, rows, CHUNK), bf16),
            sds((H, rows, 2 * HD), bf16),
            sds((H, rows, HD), bf16),
            sds((H, rows, 2 * HD), bf16),
            sds((H, HD, 2 * HD), bf16),
        ],
        scratch_shapes=[pltpu.VMEM((TOGETHER, rows + HALO, HD), f32)],
        compiler_params=params(),
        cost_estimate=cost(14.5, rows),
        name="delta_local",
    )(*([projected] * 3 + [taps] * 3 + [logits, dcol, drow]), *after)


def fwd_read_kernel(qn_ref, kn_ref, wu_ref, dcol_ref, drow_ref, r_ref, o_ref):
    rows = qn_ref.shape[0]
    row, col = tri_index()
    chunks = range(rows // CHUNK)
    ats = [pl.ds(c * CHUNK, CHUNK) for c in chunks]
    marks = [chunk_marks(dcol_ref, c) for c in chunks]
    keeps = [(marks[c][0] == drow_ref[pl.ds(c, 1), :]) & (col <= row) for c in chunks]
    items = [(h, c) for h in range(qn_ref.shape[1] // HD) for c in chunks]
    lanes = [pl.ds(h * HD, HD) for h, _ in items]
    parts = [dot_nt(qn_ref[ats[c], lane], kn_ref[ats[c], lane]) for lane, (h, c) in zip(lanes, items)]
    parts = [jnp.where(keeps[c], part, 0.0).astype(bf16) for part, (h, c) in zip(parts, items)]
    ws = [(wu_ref[h, ats[c], :HD].astype(f32) * marks[c][1]).astype(bf16) for h, c in items]
    both = [
        dot_nn(part, jnp.concatenate([w, wu_ref[h, ats[c], HD:]], axis=1)) for part, w, (h, c) in zip(parts, ws, items)
    ]
    for lane, b, (h, c) in zip(lanes, both, items):
        r_ref[ats[c], lane] = (qn_ref[ats[c], lane].astype(f32) * marks[c][1] - b[:, :HD]).astype(bf16)
        o_ref[ats[c], lane] = b[:, HD:]


def fwd_read(qn, kn, wu, dcol, drow):
    rows = qn.shape[0]
    chunks = rows // CHUNK
    sds = jax.ShapeDtypeStruct
    return pl.pallas_call(
        fwd_read_kernel,
        grid=(H // TOGETHER,),
        in_specs=[col_spec(rows, 0, TOGETHER), col_spec(rows, 0, TOGETHER), head_spec((rows, 2 * HD), TOGETHER), full_spec((rows + HALO, 1)), full_spec((chunks, CHUNK))],
        out_specs=[col_spec(rows, 0, TOGETHER), col_spec(rows, 0, TOGETHER)],
        out_shape=[sds((rows, D), bf16), sds((rows, D), f32)],
        compiler_params=params(),
        cost_estimate=cost(3.2, rows),
        name="delta_read",
    )(qn, kn, wu, dcol, drow)


def fwd_state_kernel(moves, paired, place_ref, *refs):
    ins, (state_ref, out_ref, head_ref) = refs[: moves + 5], refs[-3:]
    *near_refs, far_ref, pre_ref, r_ref, o_ref, gain_ref = ins
    rows = r_ref.shape[0]
    heads = range(r_ref.shape[1] // HD)
    states = [far_ref[h].astype(f32) for h in heads]
    if paired:
        states = [jnp.where(place_ref[0] >= 2, state, 0.0) for state in states]
    for near_ref in reversed(near_refs):
        moved = [dot_nn(near_ref[h, :, :HD], states[h]) + near_ref[h, :, HD:].astype(f32) for h in heads]
        states = [jnp.where(place_ref[0] % 2 == 1, m, s) if paired else m for m, s in zip(moved, states)]
    lows = [state.astype(bf16) for state in states]
    items = [(h, c) for h in heads for c in range(rows // CHUNK)]
    ats = [pl.ds(c * CHUNK, CHUNK) for _, c in items]
    lanes = [pl.ds(h * HD, HD) for h, _ in items]
    nows = [dot_nn(pre_ref[h, at, :HD], lows[h]) for at, (h, c) in zip(ats, items)]
    nows = [(now + pre_ref[h, at, HD:].astype(f32)).astype(bf16) for now, at, (h, c) in zip(nows, ats, items)]
    outs = [dot_nn(r_ref[at, lane], now) for at, lane, now in zip(ats, lanes, nows)]
    for out, now, at, lane, (h, c) in zip(outs, nows, ats, lanes, items):
        state_ref[h, at, :] = now
        o = o_ref[at, lane] + out
        out_ref[at, lane] = o
        scale = lax.rsqrt(jnp.mean(o * o, axis=-1, keepdims=True) + EPS_NORM)
        head_ref[at, lane] = (o * scale * gain_ref[...]).astype(bf16)


def fwd_state(place, paired, nears, far, pre, r, o, gain, after):
    rows = r.shape[0]
    sds = jax.ShapeDtypeStruct
    return pl.pallas_call(
        partial(fwd_state_kernel, len(nears), paired),
        grid=(H // TOGETHER,),
        in_specs=[
            pl.BlockSpec(memory_space=pltpu.SMEM),
            *[head_spec((HD, 2 * HD), TOGETHER) for _ in nears],
            head_spec((HD, HD), TOGETHER),
            head_spec((rows, 2 * HD), TOGETHER),
            col_spec(rows, 0, TOGETHER),
            col_spec(rows, 0, TOGETHER),
            full_spec((1, HD)),
            *[pl.BlockSpec(memory_space=pl.ANY) for _ in after],
        ],
        out_specs=[head_spec((rows, HD), TOGETHER), col_spec(rows, 0, TOGETHER), col_spec(rows, 0, TOGETHER)],
        out_shape=[sds((H, rows, HD), bf16), sds((rows, D), f32), sds((rows, D), bf16)],
        compiler_params=params(),
        cost_estimate=cost(4.3, rows),
        name="delta_state",
    )(place, *nears, far, pre, r, o, gain, *after)


def bwd_local_kernel(dhead_ref, o_ref, r_ref, gain_ref, step_ref, dcol_ref, *refs):
    do_ref, dgain_ref, total_ref = refs[-3:]
    rows = o_ref.shape[0]
    chunks = rows // CHUNK

    @pl.when(pl.program_id(0) == 0)
    def _():
        dgain_ref[...] = jnp.zeros_like(dgain_ref)

    heads = range(o_ref.shape[1] // HD)
    ats = [pl.ds(c * CHUNK, CHUNK) for c in range(chunks)]
    marks = [chunk_marks(dcol_ref, c)[3] for c in range(chunks)]
    dos = []
    for h in heads:
        lanes = pl.ds(h * HD, HD)
        o = o_ref[:, lanes]
        dy = dhead_ref[:, lanes].astype(f32)
        scale = lax.rsqrt(jnp.mean(o * o, axis=-1, keepdims=True) + EPS_NORM)
        x = o * scale
        dgain_ref[...] += jnp.sum(dy * x, axis=0, keepdims=True)
        dx = dy * gain_ref[...]
        do = (scale * (dx - x * jnp.mean(dx * x, axis=-1, keepdims=True))).astype(bf16)
        do_ref[:, lanes] = do
        dos.append(do)
    gives = [
        [dot_tn(r_ref[ats[c], pl.ds(h * HD, HD)], dos[h][c * CHUNK : (c + 1) * CHUNK]) for c in range(chunks)] for h in heads
    ]
    states = [gives[h][chunks - 1] for h in heads]
    for c in reversed(range(chunks - 1)):
        gone = [dot_tn(step_ref[h, ats[c], :], states[h]) for h in heads]
        states = [marks[c] * states[h] - gone[h] + gives[h][c] for h in heads]
    for h in heads:
        total_ref[h] = states[h].astype(bf16)


def bwd_local(dhead, o, r, gain, step, dcol, after):
    rows = o.shape[0]
    sds = jax.ShapeDtypeStruct
    return pl.pallas_call(
        bwd_local_kernel,
        grid=(H // TOGETHER,),
        in_specs=[col_spec(rows, 0, TOGETHER), col_spec(rows, 0, TOGETHER), col_spec(rows, 0, TOGETHER), full_spec((1, HD)), head_spec((rows, HD), TOGETHER), full_spec((rows + HALO, 1))]
        + [pl.BlockSpec(memory_space=pl.ANY) for _ in after],
        out_specs=[col_spec(rows, 0, TOGETHER), full_spec((1, HD)), head_spec((HD, HD), TOGETHER)],
        out_shape=[sds((rows, D), bf16), sds((1, HD), f32), sds((H, HD, HD), bf16)],
        compiler_params=params(),
        cost_estimate=cost(3.8, rows),
        name="delta_back_local",
    )(dhead, o, r, gain, step, dcol, *after)


def bwd_main_kernel(moves, paired, place_ref, *refs):
    later, refs = refs[: 2 * moves + 1], refs[2 * moves + 1 :]
    ins, outs = refs[:15], refs[-12:]
    bwd_main_body(place_ref if paired else None, later, *ins, *outs)


def bwd_main_body(
    place_ref, later, q_ref, k_ref, v_ref, tq_ref, tk_ref, tv_ref, lg_ref, dcol_ref, drow_ref,
    tinv_ref, wu_ref, step_ref, state_ref, r_ref, do_ref,
    dproj_ref, rq_ref, rk_ref, rv_ref, cq_ref, ck_ref, cv_ref, dl_ref, ext, grad, held, sems,
):
    group = pl.program_id(0)
    rows = q_ref.shape[0] - HALO
    chunks = range(rows // CHUNK)
    heads = range(q_ref.shape[1] // HD)
    masks = conv_masks(dcol_ref, rows)
    row, col = tri_index()
    cut = lambda x, c: x[c * CHUNK : (c + 1) * CHUNK]

    def filtered(x, taps, h, which):
        s = conv_sum(x, taps, masks, ext.at[which + 3 * h], h)
        gate = sigmoid(s)
        return low(s * gate), gate * (1.0 + s * (1.0 - gate))

    queries, slope_q, scale_q, qns = [], [], [], []
    keys, slope_k, scale_k, kns = [], [], [], []
    values, slope_v, betas, kbs = [], [], [], []
    for h in heads:
        query, slope = filtered(q_ref, tq_ref, h, 0)
        queries.append(query)
        slope_q.append(slope)
        scale_q.append(unit_scale(query))
        qns.append((query * scale_q[h] * HD**-0.5).astype(bf16))
        key, slope = filtered(k_ref, tk_ref, h, 1)
        slope_k.append(slope)
        scale_k.append(unit_scale(key))
        kns.append(key * scale_k[h])
        value, slope = filtered(v_ref, tv_ref, h, 2)
        values.append(value)
        slope_v.append(slope)
        betas.append(sigmoid(head_column(lg_ref[...].astype(f32), group * len(heads) + h)))
        kbs.append((betas[h] * kns[h]).astype(bf16))

    moves = len(later) // 2
    marks = [chunk_marks(dcol_ref, c) for c in chunks]
    ats = [pl.ds(c * CHUNK, CHUNK) for c in chunks]
    items = [(h, c) for h in heads for c in chunks]
    lanes = [pl.ds(h * HD, HD) for h in heads]
    dss = [later[-1][h].astype(f32) for h in heads]
    if place_ref is not None:
        dss = [jnp.where(place_ref[0] < 2, ds, 0.0) for ds in dss]
    for i in reversed(range(moves)):
        moved = [dot_tn(later[i][h], dss[h]) + later[moves + i][h].astype(f32) for h in heads]
        dss = [m if place_ref is None else jnp.where(place_ref[0] % 2 == 0, m, ds) for m, ds in zip(moved, dss)]
    gives = [dot_tn(r_ref[ats[c], lanes[h]], do_ref[ats[c], lanes[h]]) for h, c in items]
    leaving = {}
    for c in reversed(chunks):
        for h in heads:
            leaving[h, c] = dss[h].astype(bf16)
        if c:
            gone = [dot_tn(step_ref[h, ats[c], :], leaving[h, c]) for h in heads]
            dss = [marks[c][3] * dss[h] - gone[h] + gives[h * len(chunks) + c] for h in heads]

    each = range(len(items))
    carries = [marks[c][1] for _, c in items]
    tails = [marks[c][2] for _, c in items]
    sames = [marks[c][0] == drow_ref[pl.ds(c, 1), :] for c in chunks]
    uptos = [sames[c] & (col <= row) for _, c in items]
    belows = [sames[c] & (col < row) for _, c in items]
    q_cs = [cut(qns[h], c) for h, c in items]
    k_cs = [cut(kns[h], c).astype(bf16) for h, c in items]
    kb_cs = [cut(kbs[h], c) for h, c in items]
    dos = [do_ref[ats[c], lanes[h]] for h, c in items]
    wus = [wu_ref[h, ats[c], :] for h, c in items]
    states = [state_ref[h, ats[c], :] for h, c in items]
    leave = [leaving[item] for item in items]
    parts = [dot_nt(q_cs[i], k_cs[i]) for i in each]
    reads = [dot_nn(wus[i][:, :HD], states[i]) for i in each]
    kds = [dot_nn(k_cs[i], leave[i]) for i in each]
    parts = [jnp.where(uptos[i], parts[i], 0.0).astype(bf16) for i in each]
    deltas = [(wus[i][:, HD:].astype(f32) - carries[i] * reads[i]).astype(bf16) for i in each]
    pds = [dot_tn(parts[i], dos[i]) for i in each]
    dparts = [dot_nt(dos[i], deltas[i]) for i in each]
    dkfs = [dot_nt(deltas[i], leave[i]) for i in each]
    dds = [pds[i] + tails[i] * kds[i] for i in each]
    throughs = [dot_nt(jnp.concatenate([dos[i], dds[i].astype(bf16)], axis=0), states[i]) for i in each]
    inner = [
        jnp.concatenate([(-(carries[i] * throughs[i][CHUNK:])).astype(bf16), dds[i].astype(bf16)], axis=1) for i in each
    ]
    dwus = [dot_tn(tinv_ref[h, ats[c], :], x) for x, (h, c) in zip(inner, items)]
    dlows = [dot_nt(dwus[i], wus[i]) for i in each]
    pairs = [
        jnp.concatenate(
            [jnp.where(uptos[i], dparts[i], 0.0).astype(bf16), jnp.where(belows[i], -dlows[i], 0.0).astype(bf16)], axis=0
        )
        for i in each
    ]
    ontos = [dot_nn(pairs[i], k_cs[i]) for i in each]
    backs = [dot_tn(pairs[i], jnp.concatenate([q_cs[i], kb_cs[i]], axis=0)) for i in each]
    b_cs = [cut(betas[h], c) for h, c in items]
    dqs = [carries[i] * throughs[i][:CHUNK] + ontos[i][:CHUNK] for i in each]
    dkbs = [dwus[i][:, :HD] + ontos[i][CHUNK:] for i in each]
    dks = [backs[i] + tails[i] * dkfs[i] + b_cs[i] * dkbs[i] for i in each]
    dvs = [b_cs[i] * dwus[i][:, HD:] for i in each]
    dbs = [
        jnp.sum(dkbs[i] * cut(kns[h], c) + dwus[i][:, HD:] * cut(values[h], c), axis=1, keepdims=True)
        for i, (h, c) in zip(each, items)
    ]

    @pl.when(group == 0)
    def _():
        dl_ref[...] = jnp.zeros_like(dl_ref)

    slot = lax.rem(group, 2)
    width = len(heads) * HD

    def sent(step, which):
        start = pl.multiple_of(which * D + step * width, 128)
        return pltpu.make_async_copy(
            held.at[lax.rem(step, 2), which], dproj_ref.at[:, pl.ds(start, width)], sems.at[lax.rem(step, 2), which]
        )

    @pl.when(group >= 2)
    def _():
        for which in range(3):
            sent(group - 2, which).wait()

    for i in range(KW - 1):
        grad[i, pl.ds(0, HALO), :] = jnp.zeros((HALO, HD), f32)
        grad[i, pl.ds(HALO + rows, 8), :] = jnp.zeros((8, HD), f32)

    def conv_back(dfilt, slope, taps_ref, rim_ref, dtap_ref, h, which):
        ds_ = low(dfilt) * slope
        lane = lanes[h]
        x = ext.at[which + 3 * h]
        dtap_ref[pl.ds(KW - 1, 1), lane] = jnp.sum(ds_ * x[pl.ds(HALO, rows), :], axis=0, keepdims=True)
        total = ds_ * taps_ref[pl.ds(KW - 1, 1), lane]
        rim = jnp.zeros((HALO, HD), f32)
        for i in range(KW - 1):
            masked = ds_ * masks[i]
            grad[i, pl.ds(HALO, rows), :] = masked
            place_i = pl.ds(HALO - KW + 1 + i, rows)
            dtap_ref[pl.ds(i, 1), lane] = jnp.sum(masked * x[place_i, :], axis=0, keepdims=True)
            tap = taps_ref[pl.ds(i, 1), lane]
            total = total + tap * grad[i, pl.ds(HALO + KW - 1 - i, rows), :]
            rim = rim + tap * grad[i, pl.ds(KW - 1 - i, HALO), :]
        rim_ref[:, lane] = rim.astype(bf16)
        held[slot, which, :, lane] = total.astype(bf16)

    lane_index = lax.broadcasted_iota(jnp.int32, (rows, HD), 1)
    for h in heads:
        join = lambda parts: jnp.concatenate(parts[h * len(chunks) : (h + 1) * len(chunks)], axis=0)
        dqn = join(dqs) * HD**-0.5
        unit = queries[h] * scale_q[h]
        dquery = scale_q[h] * (dqn - unit * jnp.sum(dqn * unit, axis=-1, keepdims=True))
        dkn = join(dks)
        dkeys = scale_k[h] * (dkn - kns[h] * jnp.sum(dkn * kns[h], axis=-1, keepdims=True))
        dlogit = join(dbs) * betas[h] * (1.0 - betas[h])
        dl_ref[...] = jnp.where(
            lane_index == group * len(heads) + h, dlogit, dl_ref[...].astype(f32)
        ).astype(bf16)
        conv_back(dquery, slope_q[h], tq_ref, rq_ref, cq_ref, h, 0)
        conv_back(dkeys, slope_k[h], tk_ref, rk_ref, ck_ref, h, 1)
        conv_back(join(dvs), slope_v[h], tv_ref, rv_ref, cv_ref, h, 2)
    for which in range(3):
        sent(group, which).start()

    @pl.when(group == pl.num_programs(0) - 1)
    def _():
        for which in range(3):
            sent(group - 1, which).wait()
            sent(group, which).wait()


def bwd_main(place, paired, moves, gives, projected, taps, logits, dcol, drow, tinv, wu, step, state, r, do, after):
    rows = projected.shape[0] - HALO
    chunks = rows // CHUNK
    sds = jax.ShapeDtypeStruct
    return pl.pallas_call(
        partial(bwd_main_kernel, len(moves), paired),
        grid=(H // TOGETHER_BACK,),
        in_specs=[pl.BlockSpec(memory_space=pltpu.SMEM)]
        + [head_spec((HD, HD), TOGETHER_BACK) for _ in (*moves, *gives)]
        + [col_spec(rows + HALO, i * H, TOGETHER_BACK) for i in range(3)]
        + [col_spec(KW, 0, TOGETHER_BACK), col_spec(KW, H, TOGETHER_BACK), col_spec(KW, 2 * H, TOGETHER_BACK)]
        + [full_spec((rows, HD)), full_spec((rows + HALO, 1)), full_spec((chunks, CHUNK))]
        + [head_spec((rows, CHUNK), TOGETHER_BACK), head_spec((rows, 2 * HD), TOGETHER_BACK), head_spec((rows, HD), TOGETHER_BACK), head_spec((rows, HD), TOGETHER_BACK)]
        + [col_spec(rows, 0, TOGETHER_BACK), col_spec(rows, 0, TOGETHER_BACK)]
        + [pl.BlockSpec(memory_space=pl.ANY) for _ in after],
        out_specs=[pl.BlockSpec(memory_space=pl.ANY)] + [col_spec(HALO, 0, TOGETHER_BACK)] * 3 + [col_spec(KW, 0, TOGETHER_BACK)] * 3 + [full_spec((rows, HD))],
        out_shape=[sds((rows, 3 * D), bf16)] + [sds((HALO, D), bf16)] * 3 + [sds((KW, D), f32)] * 3 + [sds((rows, HD), bf16)],
        scratch_shapes=[
            pltpu.VMEM((3 * TOGETHER_BACK, rows + HALO, HD), f32),
            pltpu.VMEM((KW - 1, rows + HALO + 8, HD), f32),
            pltpu.VMEM((2, 3, rows, TOGETHER_BACK * HD), bf16),
            pltpu.SemaphoreType.DMA((2, 3)),
        ],
        compiler_params=params(),
        cost_estimate=cost(24, rows),
        name="delta_back",
    )(place, *moves, *gives, *([projected] * 3 + [taps] * 3), logits, dcol, drow, tinv, wu, step, state, r, do, *after)


def pair_forward_kernel(place_ref, own_ref, other_ref, out_ref):
    late = place_ref[0] % 2 == 1
    for h in range(H):
        own, partner = own_ref[h].astype(f32), other_ref[h].astype(f32)
        first, second = jnp.where(late, partner, own), jnp.where(late, own, partner)
        out_ref[h] = (dot_nn(second[:, :HD], first[:, HD:]) + second[:, HD:]).astype(bf16)


def pair_backward_kernel(place_ref, own_a_ref, other_a_ref, own_ref, other_ref, out_ref):
    late = place_ref[0] % 2 == 1
    for h in range(H):
        own, partner = own_ref[h].astype(f32), other_ref[h].astype(f32)
        first, second = jnp.where(late, partner, own), jnp.where(late, own, partner)
        passed = jnp.where(late, other_a_ref[h, :, :HD].astype(f32), own_a_ref[h, :, :HD].astype(f32))
        out_ref[h] = (first + dot_tn(passed, second)).astype(bf16)


def pair_state(kernel, place, *arrays, after=()):
    count = len(arrays) + 1
    return pl.pallas_call(
        lambda *refs: kernel(*refs[:count], refs[-1]),
        in_specs=[pl.BlockSpec(memory_space=pltpu.SMEM)]
        + [pl.BlockSpec(memory_space=pltpu.VMEM)] * len(arrays)
        + [pl.BlockSpec(memory_space=pl.ANY)] * len(after),
        out_specs=pl.BlockSpec(memory_space=pltpu.VMEM),
        out_shape=jax.ShapeDtypeStruct((H, HD, HD), bf16),
        cost_estimate=cost(3, 512),
        name="pair_state",
        compiler_params=pltpu.CompilerParams(vmem_limit_bytes=VMEM_LIMIT),
    )(place, *arrays, *after)


def branch_kernel(x_ref, weight_ref, stream_ref, valid_ref, gain_ref, out_ref, normed_ref, sums_ref, total, *, last):
    step = pl.program_id(0)

    @pl.when(step == 0)
    def _():
        total[...] = jnp.zeros_like(total)

    total[...] += dot_nn(x_ref[...], weight_ref[...])

    @pl.when(step == pl.num_programs(0) - 1)
    def _():
        branch = total[...]
        stream = stream_ref[...] + branch
        out_ref[...] = stream
        sums_ref[pl.ds(0, 1), :] = jnp.sum(branch * branch * valid_ref[...], axis=0, keepdims=True)
        square = stream * stream
        sums_ref[pl.ds(1, 1), :] = jnp.sum(square * valid_ref[...], axis=0, keepdims=True)
        if last:
            normed_ref[...] = stream.astype(bf16)
        else:
            scale = lax.rsqrt(jnp.mean(square, axis=-1, keepdims=True) + EPS_NORM)
            normed_ref[...] = (stream * scale * gain_ref[...]).astype(bf16)


def branch(x, weight, stream, valid, gain, last, after, steps):
    rows, depth = x.shape
    sds = jax.ShapeDtypeStruct
    return pl.pallas_call(
        lambda *refs: branch_kernel(*refs[:5], *refs[-4:], last=last),
        grid=(steps,),
        in_specs=[
            pl.BlockSpec((rows, depth // steps), lambda j: (0, j)),
            pl.BlockSpec((depth // steps, D), lambda j: (j, 0)),
            full_spec((rows, D)),
            full_spec((rows, 1)),
            full_spec((1, D)),
        ]
        + [pl.BlockSpec(memory_space=pl.ANY) for _ in after],
        out_specs=[full_spec((rows, D)), full_spec((rows, D)), full_spec((2, D))],
        out_shape=[sds((rows, D), f32), sds((rows, D), bf16), sds((2, D), f32)],
        scratch_shapes=[pltpu.VMEM((rows, D), f32)],
        compiler_params=params(),
        cost_estimate=cost(5, rows),
        name="branch",
    )(x, weight, stream, valid, gain, *after)


def act_back_kernel(g_ref, down_ref, both_ref, out_ref):
    dact = dot_nt(g_ref[...], down_ref[...])
    gate, up = both_ref[0].astype(f32), both_ref[1].astype(f32)
    part = sigmoid(gate)
    silu = gate * part
    out_ref[0] = (dact * up * (part + silu * (1.0 - part))).astype(bf16)
    out_ref[1] = (dact * silu).astype(bf16)


def gated_back(g, down, both, after, steps=11):
    rows, half = g.shape[0], down.shape[0]
    size = half // steps
    block = pl.BlockSpec((2, rows, size), lambda j: (0, 0, j))
    return pl.pallas_call(
        lambda *refs: act_back_kernel(*refs[:3], refs[-1]),
        grid=(steps,),
        in_specs=[full_spec(g.shape), pl.BlockSpec((size, D), lambda j: (j, 0)), block]
        + [pl.BlockSpec(memory_space=pl.ANY) for _ in after],
        out_specs=block,
        out_shape=jax.ShapeDtypeStruct((2, rows, half), bf16),
        compiler_params=params(),
        cost_estimate=cost(8, rows),
        name="gated_back",
    )(g, down, both, *after)


def norm_back_kernel(d_ref, weight_ref, extra_ref, extra_weight_ref, stream_ref, g_ref, gain_ref, out_ref, low_ref, dgain_ref, total):
    step = pl.program_id(0)

    @pl.when(step == 0)
    def _():
        if extra_ref is None:
            total[...] = jnp.zeros_like(total)
        else:
            total[...] = dot_nt(extra_ref[...], extra_weight_ref[...])

    block = d_ref[0] if len(d_ref.shape) == 3 else d_ref[...]
    total[...] += dot_nt(block, weight_ref[...])

    @pl.when(step == pl.num_programs(0) - 1)
    def _():
        dn = total[...]
        stream = stream_ref[...]
        scale = lax.rsqrt(jnp.mean(stream * stream, axis=-1, keepdims=True) + EPS_NORM)
        x = stream * scale
        dgain_ref[...] = jnp.sum(dn * x, axis=0, keepdims=True)
        dx = dn * gain_ref[...]
        g = g_ref[...] + scale * (dx - x * jnp.mean(dx * x, axis=-1, keepdims=True))
        out_ref[...] = g
        low_ref[...] = g.astype(bf16)


def norm_back(d, weight, extra, stream, g, gain, after):
    rows = stream.shape[0]
    steps = 4
    size = weight.shape[1] // steps
    sds = jax.ShapeDtypeStruct
    if d.ndim == 3:
        d_spec = pl.BlockSpec((1, rows, size), lambda k: (k // 2, 0, k % 2))
    else:
        d_spec = pl.BlockSpec((rows, size), lambda k: (0, k))
    count = 5 + len(extra)

    def kernel(*refs):
        ins, outs = refs[:count], refs[-4:]
        more = ins[2 : 2 + len(extra)] if extra else (None, None)
        norm_back_kernel(*ins[:2], *more, *ins[2 + len(extra) :], *outs)

    return pl.pallas_call(
        kernel,
        grid=(steps,),
        in_specs=[d_spec, pl.BlockSpec((D, size), lambda k: (0, k))]
        + [full_spec(array.shape) for array in extra]
        + [full_spec((rows, D)), full_spec((rows, D)), full_spec((1, D))]
        + [pl.BlockSpec(memory_space=pl.ANY) for _ in after],
        out_specs=[full_spec((rows, D)), full_spec((rows, D)), full_spec((1, D))],
        out_shape=[sds((rows, D), f32), sds((rows, D), bf16), sds((1, D), f32)],
        scratch_shapes=[pltpu.VMEM((rows, D), f32)],
        compiler_params=params(),
        cost_estimate=cost(9, rows),
        name="norm_back",
    )(d, weight, *extra, stream, g, gain, *after)


def other(block, axis, mask):
    return lax.ppermute(block, axis, [(i, i ^ mask) for i in range(lax.axis_size(axis))])


def sum_over(block, axis):
    mask = 1
    while mask < lax.axis_size(axis):
        block = block + other(block, axis, mask)
        mask *= 2
    return block


ANY = pl.BlockSpec(memory_space=pl.ANY)
SMEM = pl.BlockSpec(memory_space=pltpu.SMEM)
VMEM = pl.BlockSpec(memory_space=pltpu.VMEM)


def run_copies(pairs, sems):
    copies = [pltpu.make_async_copy(src, dst, sems.at[i]) for i, (src, dst) in enumerate(pairs)]
    for copy in copies:
        copy.start()
    for copy in copies:
        copy.wait()


def aligned(index, size):
    return pl.ds(pl.multiple_of(index * size, 128), size)


def offsets(sizes):
    return [sum(sizes[:i]) for i in range(len(sizes))]


def pack_kernel(place_ref, *refs, plan):
    count = sum(len(sizes) for _, sizes in plan)
    ins, outs, sems = list(refs[:count]), refs[-len(plan) - 1 : -1], refs[-1]
    quarter = place_ref[0]
    pairs = []
    for (layer, sizes), out_ref in zip(plan, outs):
        for at, size in zip(offsets(sizes), sizes):
            pairs.append((ins.pop(0).at[layer, :, aligned(quarter, size)], out_ref.at[:, pl.ds(at, size)]))
    run_copies(pairs, sems)


def pack(place, groups, after):
    plan = [(layer, [weight.shape[2] // 4 for weight in weights]) for weights, layer in groups]
    weights = [weight for group, _ in groups for weight in group]
    return pl.pallas_call(
        partial(pack_kernel, plan=plan),
        in_specs=[SMEM] + [ANY] * (len(weights) + len(after)),
        out_specs=[VMEM] * len(groups),
        out_shape=[jax.ShapeDtypeStruct((128, sum(sizes)), bf16) for _, sizes in plan],
        scratch_shapes=[pltpu.SemaphoreType.DMA((len(weights),))],
        cost_estimate=cost(2 * len(groups), 512),
        name="pack_quarters",
        compiler_params=pltpu.CompilerParams(vmem_limit_bytes=VMEM_LIMIT),
    )(place, *weights, *after)


def arrivals(place_ref, pieces, weights, sizes, sems):
    seq, core = place_ref[0], place_ref[1]
    chips = weights[0].shape[0]
    copies = {0: [], 1: [], 2: [], 3: []}
    at = 0
    for own, (h, x, y, a, b) in ((core, pieces[:5]), (1 - core, pieces[5:])):
        for piece, mask, row in ((h, 0, 0), (x, 1, 0), (y, 2, 0), (a, 3, 0), (b, 3, chips // 2)):
            here = pl.ds(row, piece.shape[0])
            for weight, start, size in zip(weights, offsets(sizes), sizes):
                copies[mask].append(
                    pltpu.make_async_copy(
                        piece.at[:, :, pl.ds(start, size)], weight.at[here, own, :, aligned(seq ^ mask, size)], sems.at[at]
                    )
                )
                at += 1
    return copies


def columns_of(weight, quarter, size):
    block = weight[:, :, :, aligned(quarter, size)]
    return block.reshape(-1, size)


def project_kernel(place_ref, tail_ref, gain_ref, normed_ref, beta_ref, *refs, sizes):
    pieces, (out_ref, logits_ref, *full_refs) = refs[:10], refs[-9:-5]
    weight, more, low_tail, sems_in, sems_out = refs[-5:]
    copies = arrivals(place_ref, pieces, (weight, more), sizes, sems_in)
    for mask in (0, 1, 2, 3):
        for copy in copies[mask]:
            copy.start()
    tail = tail_ref[...]
    scale = lax.rsqrt(jnp.mean(tail * tail, axis=-1, keepdims=True) + EPS_NORM)
    low_tail[...] = (tail * scale * gain_ref[...]).astype(bf16)
    logits_ref[...] = dot_nn(normed_ref[...], beta_ref[...]).astype(bf16)
    sent = []
    for mask in (0, 1, 2, 3):
        for copy in copies[mask]:
            copy.wait()
        quarter = place_ref[0] ^ mask
        columns = aligned(quarter, sizes[0])
        sent.append(
            pltpu.make_async_copy(
                weight.at[:, :, :, columns], full_refs[0].at[:, :, :, columns], sems_out.at[mask]
            )
        )
        sent[-1].start()
        block = columns_of(weight, quarter, sizes[0])
        out_ref[pl.ds(0, HALO), columns] = dot_nn(low_tail[...], block).astype(bf16)
        out_ref[pl.ds(HALO, normed_ref.shape[0]), columns] = dot_nn(normed_ref[...], block).astype(bf16)
    sent.append(pltpu.make_async_copy(more, full_refs[1], sems_out.at[4]))
    sent[-1].start()
    for copy in sent:
        copy.wait()


def project(place, tail, gain, normed, beta, pieces, sizes, after):
    rows = normed.shape[0]
    chips = pieces[0].shape[0] // 128
    pieces = [piece.reshape(-1, 128, piece.shape[1]) for piece in pieces]
    sds = jax.ShapeDtypeStruct
    shapes = [(chips, 2, 128, 4 * size) for size in sizes]
    out, logits, first, second = pl.pallas_call(
        partial(project_kernel, sizes=sizes),
        in_specs=[SMEM] + [VMEM] * 4 + [ANY] * (len(pieces) + len(after)),
        out_specs=[VMEM, VMEM, ANY, ANY],
        out_shape=[sds((rows + HALO, 4 * sizes[0]), bf16), sds((rows, beta.shape[1]), bf16)]
        + [sds(shape, bf16) for shape in shapes],
        scratch_shapes=[pltpu.VMEM(shape, bf16) for shape in shapes]
        + [pltpu.VMEM((HALO, D), bf16), pltpu.SemaphoreType.DMA((20,)), pltpu.SemaphoreType.DMA((5,))],
        compiler_params=pltpu.CompilerParams(vmem_limit_bytes=VMEM_LIMIT),
        cost_estimate=cost(10, rows),
        name="project",
    )(place, tail, gain, normed, beta, *pieces, *after)
    return out, logits, first.reshape(D, -1), second.reshape(D, -1)


def gated_kernel(place_ref, x_ref, *refs, size):
    pieces, (act_ref, both_ref, full_ref) = refs[:10], refs[-9:-6]
    weight, act, both, sems_in, sems_out, sems_act = refs[-6:]
    copies = arrivals(place_ref, pieces, (weight,), (size,), sems_in)
    order = (0, 2, 1, 3)
    for mask in order:
        for copy in copies[mask]:
            copy.start()
    sent = []
    for turn in (0, 1):
        for mask in order[2 * turn : 2 * turn + 2]:
            for copy in copies[mask]:
                copy.wait()
            columns = aligned(place_ref[0] ^ mask, size)
            sent.append(
                pltpu.make_async_copy(weight.at[:, :, :, columns], full_ref.at[:, :, :, columns], sems_out.at[mask])
            )
            sent[-1].start()
        half = lax.rem(place_ref[0] ^ turn, 2)
        gate_block = dot_nn(x_ref[...], columns_of(weight, half, size))
        up_block = dot_nn(x_ref[...], columns_of(weight, half + 2, size))
        act[turn] = (gate_block * sigmoid(gate_block) * up_block).astype(bf16)
        both[turn, 0] = gate_block.astype(bf16)
        both[turn, 1] = up_block.astype(bf16)
        columns = aligned(half, size)
        sent.append(pltpu.make_async_copy(act.at[turn], act_ref.at[:, columns], sems_act.at[2 * turn]))
        sent.append(pltpu.make_async_copy(both.at[turn], both_ref.at[:, :, columns], sems_act.at[2 * turn + 1]))
        for copy in sent[-2:]:
            copy.start()
    for copy in sent:
        copy.wait()


def gated(place, x, pieces, size, after):
    rows = x.shape[0]
    chips = pieces[0].shape[0] // 128
    pieces = [piece.reshape(-1, 128, piece.shape[1]) for piece in pieces]
    sds = jax.ShapeDtypeStruct
    act, both, full = pl.pallas_call(
        partial(gated_kernel, size=size),
        in_specs=[SMEM, VMEM] + [ANY] * (len(pieces) + len(after)),
        out_specs=[ANY] * 3,
        out_shape=[sds((rows, 2 * size), bf16), sds((2, rows, 2 * size), bf16), sds((chips, 2, 128, 4 * size), bf16)],
        scratch_shapes=[
            pltpu.VMEM((chips, 2, 128, 4 * size), bf16),
            pltpu.VMEM((2, rows, size), bf16),
            pltpu.VMEM((2, 2, rows, size), bf16),
            pltpu.SemaphoreType.DMA((10,)),
            pltpu.SemaphoreType.DMA((4,)),
            pltpu.SemaphoreType.DMA((4,)),
        ],
        compiler_params=pltpu.CompilerParams(vmem_limit_bytes=VMEM_LIMIT),
        cost_estimate=cost(15, rows),
        name="gated",
    )(place, x, *pieces, *after)
    return act, both, full.reshape(D, -1)


def gate(array, after):
    return pl.pallas_call(
        lambda *refs: None,
        in_specs=[ANY] * (1 + len(after)),
        out_specs=ANY,
        out_shape=jax.ShapeDtypeStruct(array.shape, array.dtype),
        input_output_aliases={0: 0},
        cost_estimate=cost(0.5, 512),
        name="gate",
        compiler_params=pltpu.CompilerParams(vmem_limit_bytes=VMEM_LIMIT),
    )(array, *after)


def relay_kernel(x_ref, y_ref, *refs):
    a_ref, b_ref, _, _, sems = refs[-5:]
    half = a_ref.shape[0]
    run_copies([(x_ref.at[pl.ds(0, half)], a_ref), (y_ref.at[pl.ds(half, half)], b_ref)], sems)


def relay(over_x, over_y, after):
    half = jax.ShapeDtypeStruct((over_x.shape[0] // 2, over_x.shape[1]), over_x.dtype)
    whole = jax.ShapeDtypeStruct(over_x.shape, over_x.dtype)
    a, b, over_x, over_y = pl.pallas_call(
        relay_kernel,
        in_specs=[ANY] * (2 + len(after)),
        out_specs=[VMEM] * 2 + [ANY] * 2,
        out_shape=[half] * 2 + [whole] * 2,
        input_output_aliases={0: 2, 1: 3},
        scratch_shapes=[pltpu.SemaphoreType.DMA((2,))],
        cost_estimate=cost(2.5, 512),
        name="relay",
        compiler_params=pltpu.CompilerParams(vmem_limit_bytes=VMEM_LIMIT),
    )(over_x, over_y, *after)
    return (a, b), (over_x, over_y)


def core_groups():
    return [list(range(core, lax.axis_size("fsdp"), 2)) for core in range(2)]


def gather_chips(packed):
    return lax.all_gather(packed, "fsdp", axis=0, axis_index_groups=core_groups(), tiled=True)


def scatter_chips(total):
    return lax.psum_scatter(total, "fsdp", scatter_dimension=0, axis_index_groups=core_groups(), tiled=True)


def first_round(block):
    return other(block, "seq", 1), other(block, "seq", 2)


def second_round(passed):
    return other(passed[0], "seq", 2), other(passed[1], "seq", 1)


def interleaved(ref, core):
    blocks = ref.shape[1] // 256
    return jnp.concatenate([ref[:, aligned(2 * z + core, 128)] for z in range(blocks)], axis=1)


def grad_pieces_kernel(place_ref, *refs, count):
    ins, (o0_ref, o1_ref, o2_ref, oa_ref, ob_ref), scratch = refs[: 4 * count], refs[-6 - count : -1 - count], refs[-1 - count :]
    lefts, rights, turned, total = ins[: 2 * count], ins[2 * count :], scratch[:count], scratch[count]
    step = pl.program_id(0)
    tokens = lefts[0].shape[0]

    @pl.when(step == 0)
    def _():
        for i in range(2 * count):
            turned[i // 2][:, pl.ds((i % 2) * tokens, tokens)] = interleaved(lefts[i], place_ref[1]).T

    start = 0
    for i in range(count):
        a_ref, b_ref = rights[2 * i : 2 * i + 2]
        size = a_ref.shape[-1]
        a, b = [ref[0] if len(ref.shape) == 3 else ref[...] for ref in (a_ref, b_ref)]
        total[:, pl.ds(start, size)] = (
            dot_nn(turned[i][:, pl.ds(0, tokens)], a) + dot_nn(turned[i][:, pl.ds(tokens, tokens)], b)
        ).astype(bf16)
        start += size
    half = total.shape[0] // 2
    for i, out in enumerate((o0_ref, o1_ref, o2_ref)):

        @pl.when(step == i)
        def _(out=out):
            out[...] = total[...]

    @pl.when(step == 3)
    def _():
        oa_ref[...] = total[pl.ds(0, half), :]
        ob_ref[...] = total[pl.ds(half, half), :]


def grad_pieces(place, pairs, after):
    lefts = [left for pair in pairs for left in pair[0]]
    rights = [right for pair in pairs for right in pair[1]]
    tokens, rows = lefts[0].shape[0], lefts[0].shape[1] // 2
    sizes = [right.size // tokens // 4 for right in rights]
    width = sum(sizes[::2])
    whole = lambda array: pl.BlockSpec(array.shape, lambda j, place_ref: (0, 0))

    def quarter(right, size):
        if right.ndim == 2:
            return pl.BlockSpec((tokens, size), lambda j, place_ref: (0, place_ref[0] ^ j))
        return pl.BlockSpec(
            (1, tokens, size), lambda j, place_ref: ((place_ref[0] ^ j) // 2, 0, lax.rem(place_ref[0] ^ j, 2))
        )

    shapes = [(rows, width)] * 3 + [(rows // 2, width)] * 2
    return pl.pallas_call(
        partial(grad_pieces_kernel, count=len(pairs)),
        grid_spec=pltpu.PrefetchScalarGridSpec(
            num_scalar_prefetch=1,
            grid=(4,),
            in_specs=[whole(left) for left in lefts] + [quarter(right, size) for right, size in zip(rights, sizes)] + [ANY] * len(after),
            out_specs=[pl.BlockSpec(shape, lambda j, place_ref: (0, 0)) for shape in shapes],
            scratch_shapes=[pltpu.VMEM((rows, 2 * tokens), bf16) for _ in pairs] + [pltpu.VMEM((rows, width), bf16)],
        ),
        out_shape=[jax.ShapeDtypeStruct(shape, bf16) for shape in shapes],
        compiler_params=pltpu.CompilerParams(vmem_limit_bytes=VMEM_LIMIT),
        cost_estimate=cost(12, 512),
        name="grad_pieces",
    )(place, *lefts, *rights, *after)


def settle_kernel(place_ref, *refs, sizes):
    pieces, outs = refs[:5], refs[-len(sizes) :]
    rows = pieces[0].shape[0]
    masks = ((0, 0, rows), (1, 0, rows), (2, 0, rows), (3, 0, rows // 2), (3, rows // 2, rows // 2))
    for piece, (mask, at, count) in zip(pieces, masks):
        for out_ref, start, size in zip(outs, offsets(sizes), sizes):
            out_ref[0, pl.ds(at, count), aligned(place_ref[0] ^ mask, size)] = piece[:, pl.ds(start, size)].astype(f32)


def settle(place, pieces, sizes, layer, so_far):
    rows = pieces[0].shape[0]
    whole = lambda array: pl.BlockSpec(array.shape, lambda i: (0, 0))
    return pl.pallas_call(
        partial(settle_kernel, sizes=sizes),
        grid=(1,),
        in_specs=[SMEM] + [whole(piece) for piece in pieces] + [ANY] * len(so_far),
        out_specs=[pl.BlockSpec((1, rows, 4 * size), lambda i: (layer, 0, 0)) for size in sizes],
        out_shape=[jax.ShapeDtypeStruct((LAYERS, rows, 4 * size), f32) for size in sizes],
        input_output_aliases={6 + i: i for i in range(len(so_far))},
        compiler_params=pltpu.CompilerParams(vmem_limit_bytes=VMEM_LIMIT),
        cost_estimate=cost(3, 512),
        name="settle_gradient",
    )(place, *pieces, *so_far)


def merge_kernel(x_ref, y_ref, a_ref, b_ref, *refs):
    ox_ref, oy_ref = refs[-2:]
    ox_ref[...] = (x_ref[...].astype(f32) + b_ref[...].astype(f32)).astype(bf16)
    oy_ref[...] = (y_ref[...].astype(f32) + a_ref[...].astype(f32)).astype(bf16)


def merge(over_x, over_y, diag_a, diag_b, after):
    half, width = diag_a.shape
    rows = half // 4
    lower = pl.BlockSpec((rows, width), lambda i: (i, 0))
    upper = pl.BlockSpec((rows, width), lambda i: (i + 4, 0))
    whole = jax.ShapeDtypeStruct(over_x.shape, bf16)
    return pl.pallas_call(
        merge_kernel,
        grid=(4,),
        in_specs=[upper, lower, lower, lower] + [ANY] * len(after),
        out_specs=[upper, lower],
        out_shape=[whole, whole],
        input_output_aliases={0: 0, 1: 1},
        compiler_params=pltpu.CompilerParams(vmem_limit_bytes=VMEM_LIMIT),
        cost_estimate=cost(3.5, 512),
        name="merge",
    )(over_x, over_y, diag_a, diag_b, *after)


def total_kernel(own_ref, x_ref, y_ref, *refs):
    refs[-1][...] = (own_ref[...].astype(f32) + x_ref[...].astype(f32) + y_ref[...].astype(f32)).astype(bf16)


def total_of(own, from_x, from_y, after):
    rows, width = own.shape
    block = pl.BlockSpec((rows // 4, width), lambda i: (i, 0))
    return pl.pallas_call(
        total_kernel,
        grid=(4,),
        in_specs=[block] * 3 + [ANY] * len(after),
        out_specs=block,
        out_shape=jax.ShapeDtypeStruct(own.shape, bf16),
        compiler_params=pltpu.CompilerParams(vmem_limit_bytes=VMEM_LIMIT),
        cost_estimate=cost(4, 512),
        name="total",
    )(own, from_x, from_y, *after)


def gather_start(scattered, after):
    block = gate(scattered, after) if after else scattered
    return block, first_round(block)


def gather_settle(place, block, over, sizes, layer, so_far, after):
    passed, over = relay(*over, after)
    pieces = [block, *over, *second_round(passed)]
    return settle(place, pieces, sizes, layer, so_far), passed


def small_kernel(*refs):
    ins, out_ref = refs[:-1], refs[-1]
    at = 0
    out_ref[...] = jnp.zeros_like(out_ref)
    for ref in ins:
        for start in range(0, ref.shape[1], D):
            size = min(D, ref.shape[1] - start)
            out_ref[pl.ds(at, ref.shape[0]), pl.ds(0, size)] = ref[:, pl.ds(start, size)]
            at += ref.shape[0]


def small_rows(arrays):
    counts = [array.shape[0] * -(-array.shape[1] // D) for array in arrays]
    packed = pl.pallas_call(
        small_kernel,
        in_specs=[VMEM] * len(arrays),
        out_specs=VMEM,
        out_shape=jax.ShapeDtypeStruct((-(-sum(counts) // 8) * 8, D), f32),
        cost_estimate=cost(2, 512),
        name="small_rows",
        compiler_params=pltpu.CompilerParams(vmem_limit_bytes=VMEM_LIMIT),
    )(*arrays)
    return packed, offsets(counts)


def small_part(packed, start, shape):
    parts = -(-shape[1] // D)
    rows = [packed[start + i * shape[0] : start + (i + 1) * shape[0], : min(D, shape[1])] for i in range(parts)]
    return jnp.concatenate(rows, axis=1)


epsilon_norm = EPS_NORM


def shifted(block, axis, distance):
    devices = range(lax.axis_size(axis))
    route = [(i - distance, i) for i in devices if i - distance in devices]
    return lax.ppermute(block, axis, route)


def root_norm(values, gain):
    return (
        values * lax.rsqrt(jnp.mean(values * values, axis=-1, keepdims=True) + epsilon_norm) * gain
    )


def swiglu_act(gate_up):
    half_width = gate_up.shape[1] // 2
    return jax.nn.silu(gate_up[:, :half_width]) * gate_up[:, half_width:]


def contract_last(left, right):
    return lax.dot_general(
        left, right, (((1,), (1,)), ((), ())), preferred_element_type=jnp.float32
    )


def contract_first(left, right):
    return lax.dot_general(
        left, right, (((0,), (0,)), ((), ())), preferred_element_type=jnp.float32
    )


def fetch_rows(weights):
    return lax.all_gather(weights, "fsdp", axis=0, tiled=True)


def reduce_rows(left, right):
    return lax.psum_scatter(
        contract_first(left, right).astype(jnp.bfloat16), "fsdp", scatter_dimension=0, tiled=True
    )


def documents(segments, rows):
    doc_pad = jnp.concatenate([jnp.full((HALO,), -1, jnp.int32), segments])
    dcol = lax.dynamic_slice_in_dim(doc_pad, lax.axis_index("seq") * rows, rows + HALO)
    return dcol[:, None], dcol[HALO:].reshape(rows // CHUNK, CHUNK)


def on_device(
    tokens,
    segments,
    valid_mask,
    norm_gains,
    head_gain,
    conv_weight,
    beta_weight,
    qkv_weight,
    out_weight,
    gate_up_weight,
    down_weight,
    cotangent,
):
    rows = tokens.shape[1]
    pieces = lax.axis_size("seq")
    dcol, drow = documents(segments[0], rows)
    place = jnp.stack([lax.axis_index("seq"), lax.axis_index("fsdp") % 2]).astype(jnp.int32)
    valid_rows = valid_mask[0].astype(jnp.float32)
    stream = tokens[0].astype(jnp.float32)
    square_sums = []
    stored = []
    for at in range(LAYERS):
        qkv_full = fetch_rows(qkv_weight[at])
        out_full = fetch_rows(out_weight[at])
        gate_up_full = fetch_rows(gate_up_weight[at])
        down_full = fetch_rows(down_weight[at])
        square_sums.append(jnp.sum(jnp.sum(stream * stream, axis=1) * valid_rows))
        normed_one, pull_one = jax.vjp(root_norm, stream, norm_gains[at, 0])
        normed_one = normed_one.astype(jnp.bfloat16)
        projected = jnp.dot(normed_one, qkv_full, preferred_element_type=jnp.float32).astype(bf16)
        logits = jnp.dot(normed_one, beta_weight[at], preferred_element_type=jnp.float32).astype(bf16)
        logits = jnp.pad(logits, ((0, 0), (0, HD - H)))
        projected = jnp.concatenate([shifted(projected[rows - HALO :], "seq", 1), projected], axis=0)
        qn, kn, tinv, wu, step, pre, total = fwd_local(
            projected, conv_weight[at], logits, dcol, drow, []
        )
        nears = [shifted(total, "seq", d) for d in range(1, pieces - 1)]
        far = shifted(total[:, :, HD:], "seq", pieces - 1)
        moves = [shifted(total[:, :, :HD], "seq", -d) for d in range(1, pieces - 1)]
        reads, local_out = fwd_read(qn, kn, wu, dcol, drow)
        state, mixed, attended = fwd_state(
            place, False, nears, far, pre, reads, local_out, head_gain[at][None], []
        )
        branch = jnp.dot(attended, out_full, preferred_element_type=jnp.float32)
        square_sums.append(jnp.sum(jnp.sum(branch * branch, axis=1) * valid_rows))
        stream = stream + branch
        normed_two, pull_two = jax.vjp(root_norm, stream, norm_gains[at, 1])
        normed_two = normed_two.astype(jnp.bfloat16)
        gate_up = jnp.dot(normed_two, gate_up_full, preferred_element_type=jnp.float32)
        activated, pull_act = jax.vjp(swiglu_act, gate_up)
        activated = activated.astype(jnp.bfloat16)
        branch = jnp.dot(activated, down_full, preferred_element_type=jnp.float32)
        square_sums.append(jnp.sum(jnp.sum(branch * branch, axis=1) * valid_rows))
        stream = stream + branch
        stored.append(
            (
                qkv_full, out_full, gate_up_full, down_full, pull_one, normed_one, attended, pull_two, normed_two,
                pull_act, activated, moves, mixed,
                (projected, conv_weight[at], logits, dcol, drow, tinv, wu, step, state, reads),
            )
        )
    stream_grad = cotangent[0].astype(jnp.float32) * valid_rows[:, None]
    gain_list = []
    head_list = []
    filter_list = []
    beta_list = []
    weight_list = []
    for at in reversed(range(LAYERS)):
        (
            qkv_full, out_full, gate_up_full, down_full, pull_one, normed_one, attended, pull_two, normed_two,
            pull_act, activated, moves, mixed, kept,
        ) = stored[at]
        step, reads = kept[7], kept[9]
        branch_low = stream_grad.astype(jnp.bfloat16)
        grad_down = reduce_rows(activated, branch_low)
        (grad_gate_up,) = pull_act(contract_last(branch_low, down_full))
        grad_gate_up = grad_gate_up.astype(jnp.bfloat16)
        grad_gate = reduce_rows(normed_two, grad_gate_up)
        grad_state, gain_two = pull_two(contract_last(grad_gate_up, gate_up_full))
        stream_grad = stream_grad + grad_state
        branch_low = stream_grad.astype(jnp.bfloat16)
        grad_out = reduce_rows(attended, branch_low)
        grad_heads = contract_last(branch_low, out_full).astype(jnp.bfloat16)
        grad_mixed, gain_head, total = bwd_local(
            grad_heads, mixed, reads, head_gain[at][None], step, dcol, []
        )
        gives = [shifted(total, "seq", -d) for d in range(1, pieces)]
        grad_proj, *parts, grad_logits = bwd_main(place, False, moves, gives, *kept, grad_mixed, [])
        grad_logits = grad_logits[:, :H]
        rim = shifted(jnp.concatenate(parts[:3], axis=1), "seq", -1)
        grad_filter = jnp.concatenate(parts[3:6], axis=1)
        grad_proj = grad_proj.at[rows - HALO :].add(rim)
        grad_qkv = reduce_rows(normed_one, grad_proj)
        grad_beta = contract_first(normed_one, grad_logits)
        grad_normed = contract_last(grad_proj, qkv_full) + contract_last(grad_logits, beta_weight[at])
        grad_state, gain_one = pull_one(grad_normed)
        stream_grad = stream_grad + grad_state
        weight_list.append(
            [lax.psum(grad, "seq").astype(f32) for grad in (grad_qkv, grad_out, grad_gate, grad_down)]
        )
        gain_list.append(jnp.stack([gain_one, gain_two]))
        head_list.append(gain_head[0])
        filter_list.append(grad_filter)
        beta_list.append(grad_beta)
    stats_sum, valid_count, gains_sum, head_sum, filter_sum, beta_sum = lax.psum(
        (
            jnp.stack(square_sums),
            jnp.sum(valid_rows),
            jnp.stack(gain_list[::-1]),
            jnp.stack(head_list[::-1]),
            jnp.stack(filter_list[::-1]),
            jnp.stack(beta_list[::-1]),
        ),
        ("seq", "fsdp"),
    )
    rms_stats = jnp.sqrt(stats_sum / (jnp.maximum(valid_count, 1.0) * D)).reshape(LAYERS, 3)
    return (
        stream.astype(jnp.bfloat16)[None],
        stream_grad[None],
        gains_sum,
        head_sum,
        filter_sum,
        beta_sum,
        *[jnp.stack(pair[::-1]) for pair in zip(*weight_list)],
        rms_stats,
    )


def on_device_axes(
    tokens,
    segments,
    valid_mask,
    norm_gains,
    head_gain,
    conv_weight,
    beta_weight,
    qkv_weight,
    out_weight,
    gate_up_weight,
    down_weight,
    cotangent,
):
    rows = tokens.shape[1]
    dcol, drow = documents(segments[0], rows)
    place = jnp.stack([lax.axis_index("seq"), lax.axis_index("fsdp") % 2]).astype(jnp.int32)
    valid_rows = valid_mask[0].astype(f32)
    near = lambda array: (array, other(array, "fsdp", 1))
    size_qkv, size_out, size_gate = [weight.shape[2] // 4 for weight in (qkv_weight, out_weight, gate_up_weight)]
    sizes_one, sizes_two = (size_qkv, size_out), (size_gate,)
    groups = []
    for at in range(LAYERS):
        groups += [((qkv_weight, out_weight), at), ((gate_up_weight,), at)]
    packs = pack(place, groups[:1], [])
    packs += pack(place, groups[1:], packs)
    blocks, downs = [], []
    for at in range(LAYERS):
        blocks += [gather_chips(packed) for packed in packs[2 * at : 2 * at + 2]]
        downs.append(lax.all_gather(down_weight[at], "fsdp", axis=0, tiled=True))

    def launch(block, after):
        block = gate(block, after) if after else block
        return block, first_round(block)

    def finish(block, over, after):
        near_block = other(block, "fsdp", 1)
        passed, over = relay(*over, [near_block, *after])
        near_over = [other(piece, "fsdp", 1) for piece in over]
        return [block, *over], [near_block, *near_over], second_round(passed), passed

    def complete(came, after):
        own, near_own, passed, _ = came
        passed = [gate(piece, after) if after else piece for piece in passed]
        return [*own, *passed, *near_own, *[other(piece, "fsdp", 1) for piece in passed]]

    stream = tokens[0].astype(f32)
    tail = shifted(tokens[0, rows - HALO :], "seq", 1).astype(f32)
    valid = valid_rows[:, None]
    betas = jnp.pad(beta_weight, ((0, 0), (0, 0), (0, HD - H)))
    gains = lambda at, which: norm_gains[at, which][None]
    square_sums = [jnp.sum(stream * stream * valid, axis=0)[None]]
    normed = root_norm(stream, gains(0, 0)).astype(bf16)
    ready = [tail, betas, normed, dcol, drow, valid, stream, *square_sums]
    parts_one = complete(finish(*launch(blocks[0], []), ready), [])
    coming = launch(blocks[1], parts_one[-2:])
    stored = []
    for at in range(LAYERS):
        normed_one = near(normed)
        projected, logits, qkv_full, out_full = project(
            place, tail, gains(at, 0), normed, betas[at], parts_one, sizes_one, []
        )
        qn, kn, tinv, wu, step, pre, total = fwd_local(
            projected, conv_weight[at], logits, dcol, drow, normed_one[1:]
        )
        partner = other(total, "seq", 1)
        reads, local_out = fwd_read(qn, kn, wu, dcol, drow)
        pair = pair_state(pair_forward_kernel, place, total, partner, after=[reads])
        far = other(pair, "seq", 2)
        came = finish(*coming, [far])
        state, mixed, attended = fwd_state(
            place, True, [partner], far, pre, reads, local_out, head_gain[at][None], [*came[1], *came[3]]
        )
        parts_two = complete(came, [attended])
        attended = near(attended)
        after_mix, normed, sums = branch(attended[0], out_full, stream, valid, gains(at, 1), False, [], 1)
        normed_two = near(normed)
        more = at + 1 < LAYERS
        if more:
            coming = launch(blocks[2 * at + 2], parts_two[3:5])
        activated, both, gate_up_full = gated(place, normed, parts_two, size_gate, attended[1:])
        passed = []
        if more:
            came = finish(*coming, [activated, *normed_two])
            passed = came[3]
        new_stream, normed, more_sums = branch(
            activated, downs[at], after_mix, valid, gains((at + 1) % LAYERS, 0), not more, passed, 2
        )
        if more:
            parts_one = complete(came, [new_stream])
            tail = shifted(new_stream[rows - HALO :], "seq", 1)
            coming = launch(blocks[2 * at + 3], [*parts_one[-2:], tail])
        square_sums += [sums[:1], more_sums[:1], more_sums[1:]]
        stored.append(
            (
                qkv_full, out_full, gate_up_full, downs[at], stream, normed_one, attended, after_mix,
                normed_two, both, activated, (total, partner), mixed,
                new_stream, (projected, conv_weight[at], logits, dcol, drow, tinv, wu, step, state, reads),
            )
        )
        stream = new_stream
    result = normed
    g = cotangent[0].astype(f32) * valid
    g_low = g.astype(bf16)
    small = []
    waiting = []
    result_qkv, result_out, result_gate = [], [], []
    for at in reversed(range(LAYERS)):
        (
            qkv_full, out_full, gate_up_full, down_full, stream, normed_one, attended, after_mix,
            normed_two, both, activated, states, mixed, leaving, kept,
        ) = stored[at]
        step, reads = kept[7], kept[9]
        started = []
        if waiting:
            grad_down = contract_first(gate(activated, [scattered, waiting[0]]), g_low).astype(bf16)
            own, over_x, over_y, diag_a, diag_b = waiting
            over_x, over_y = merge(over_x, over_y, diag_a, diag_b, [grad_down])
            above = (own, other(over_x, "seq", 1), other(over_y, "seq", 2))
            block, over = gather_start(scattered, [over_x])
            started = [block]
        else:
            grad_down = contract_first(activated, g_low).astype(bf16)
        grad_gate_up = gated_back(g_low, down_full, both, [over_x] if waiting else [grad_down], 2)
        grad_down = lax.psum_scatter(grad_down, "fsdp", scatter_dimension=0, tiled=True)
        grad_gate_up = near(grad_gate_up)
        g, g_low, gain_two = norm_back(
            grad_gate_up[0], gate_up_full, (), after_mix, g, gains(at, 1), started
        )
        branch_low = near(g_low)
        pairs_one = [(normed_two, grad_gate_up)]
        out_pair = (attended, branch_low)
        ready = [gain_two]
        if waiting:
            pairs_one.append(out_pair)
            reduced = total_of(*above, [gain_two])
            above = scatter_chips(reduced)
            ready += [reduced]
        own, over_x, over_y, diag_a, diag_b = grad_pieces(place, pairs_one, ready)
        diag_a, diag_b = other(diag_a, "seq", 1), other(diag_b, "seq", 2)
        done = [own]
        if waiting:
            result_gate, passed = gather_settle(place, block, over, (size_gate,), at + 1, [], [own])
            done += passed
        grad_heads = contract_last(branch_low[0], out_full).astype(bf16)
        grad_mixed, gain_head, total = bwd_local(
            grad_heads, mixed, reads, head_gain[at][None], step, dcol, done
        )
        partner = other(total, "seq", 1)
        fillers = result_gate if waiting else [leaving]
        pair = pair_state(pair_backward_kernel, place, *states, total, partner, after=fillers)
        gives = [partner, other(pair, "seq", 2)]
        over_x, over_y = merge(over_x, over_y, diag_a, diag_b, [gives[1]])
        from_x, from_y = other(over_x, "seq", 1), other(over_y, "seq", 2)
        grad_proj, *parts, grad_logits = bwd_main(
            place, True, states[1:], gives, *kept, grad_mixed,
            [over_x, *branch_low[1:], *([above] if waiting else [])],
        )
        rim = shifted(jnp.concatenate(parts[:3], axis=1), "seq", -1)
        reduced = total_of(own, from_x, from_y, [grad_proj, grad_down])
        scattered = scatter_chips(reduced)
        grad_proj = near(gate(grad_proj, [reduced]).at[rows - HALO :].add(rim))
        grad_beta = contract_first(grad_logits[:, :H], normed_one[0])
        g, g_low, gain_one = norm_back(
            grad_proj[0], qkv_full, (grad_logits, betas[at]), stream, g, gains(at, 0), [reduced]
        )
        pairs_two = [(normed_one, grad_proj)]
        started = [gain_one]
        small += [gain_one, gain_two, gain_head, *parts[3:6], grad_beta]
        if waiting:
            grad_down = gate(grad_down, [reduced])
            grad_down = grad_down + gate(other(grad_down, "seq", 1), [gain_one])
            down_above = down_above + gate(other(gate(down_above, [reduced]), "seq", 2), [gain_one])
            above_far = other(down_above, "seq", 1)
            block, over = gather_start(above, [reduced])
            small += [*square_sums[: 3 * LAYERS], jnp.broadcast_to(jnp.sum(valid_rows), (1, D))]
            packed, starts = small_rows(small)
            started += [grad_down, down_above, packed]
            packed_near = other(packed, "fsdp", 1)
            down_far = other(grad_down, "seq", 2)
        else:
            pairs_two.append(out_pair)
            down_above = grad_down
        own, over_x, over_y, diag_a, diag_b = grad_pieces(place, pairs_two, started)
        if waiting:
            settled, _ = gather_settle(place, block, over, (size_qkv, size_out), at + 1, [], [own])
            result_qkv, result_out = settled
        waiting = own, over_x, over_y, other(diag_a, "seq", 1), other(diag_b, "seq", 2)
    own, over_x, over_y, diag_a, diag_b = waiting
    packed = packed + gate(packed_near, [own])
    packed = packed + other(packed, "fsdp", 2)
    downs = [grad_down + gate(down_far, [own]), down_above + gate(above_far, [own])]
    over_x, over_y = merge(over_x, over_y, diag_a, diag_b, [packed, *downs])
    from_x, from_y = other(over_x, "seq", 1), other(over_y, "seq", 2)
    packed = packed + other(gate(packed, [over_x]), "fsdp", 4)
    reduced = total_of(own, from_x, from_y, [packed])
    last = scatter_chips(reduced)
    packed = sum_over(gate(packed, [reduced]), "seq")
    block, over = gather_start(scattered, [reduced])
    (result_gate, result_out), _ = gather_settle(
        place, block, over, (size_gate, size_out), 0, [*result_gate, result_out], []
    )
    block, over = gather_start(last, [packed, result_gate])
    (result_qkv,), _ = gather_settle(place, block, over, (size_qkv,), 0, [result_qkv], [])
    summed = [small_part(packed, start, array.shape) for start, array in zip(starts, small)]
    of_layer = lambda at: summed[7 * (LAYERS - 1 - at) : 7 * (LAYERS - at)]
    by_layer = lambda pick: jnp.stack([pick(of_layer(at)) for at in range(LAYERS)])
    stats = jnp.concatenate(summed[7 * LAYERS : -1], axis=0)
    count = summed[-1][0, 0]
    rms_stats = jnp.sqrt(jnp.sum(stats, axis=1) / (jnp.maximum(count, 1.0) * D)).reshape(LAYERS, 3)
    return (
        result[None],
        g[None],
        by_layer(lambda arrays: jnp.concatenate(arrays[:2], axis=0)),
        by_layer(lambda arrays: arrays[2][0]),
        by_layer(lambda arrays: jnp.concatenate(arrays[3:6], axis=1)),
        by_layer(lambda arrays: arrays[6].T),
        result_qkv,
        result_out,
        result_gate,
        jnp.stack(downs).astype(f32),
        rms_stats,
    )


def solution(mesh):
    axes = mesh.shape["seq"] == 4 and mesh.shape["fsdp"] == 8
    return jax.shard_map(
        on_device_axes if axes else on_device,
        mesh=mesh,
        in_specs=(
            P("fsdp", "seq", None),
            P("fsdp", None),
            P("fsdp", "seq"),
            P(),
            P(),
            P(),
            P(),
            P(None, "fsdp", None),
            P(None, "fsdp", None),
            P(None, "fsdp", None),
            P(None, "fsdp", None),
            P("fsdp", "seq", None),
        ),
        out_specs=(
            P("fsdp", "seq", None),
            P("fsdp", "seq", None),
            P(),
            P(),
            P(),
            P(),
            P(None, "fsdp", None),
            P(None, "fsdp", None),
            P(None, "fsdp", None),
            P(None, "fsdp", None),
            P(),
        ),
        check_vma=False,
    )
```

```python
from functools import partial
import jax
import jax.numpy as jnp
from jax import lax
from jax.experimental import pallas as pl
from jax.experimental.pallas import tpu as pltpu
from jax.sharding import PartitionSpec as P

D = 1024
H = 8
HD = 128
KW = 4
LAYERS = 2
CHUNK = 128
TOGETHER = 4
TOGETHER_BACK = 2
HALO = 16
f32 = jnp.float32
bf16 = jnp.bfloat16
EPS_NORM = 1e-05
EPS_UNIT = 1e-06
VMEM_LIMIT = 60 * 1024 * 1024


def dot_nn(a, b):
    return lax.dot_general(a.astype(bf16), b.astype(bf16), (((1,), (0,)), ((), ())), preferred_element_type=f32)


def dot_nt(a, b):
    return lax.dot_general(a.astype(bf16), b.astype(bf16), (((1,), (1,)), ((), ())), preferred_element_type=f32)


def dot_tn(a, b):
    return lax.dot_general(a.astype(bf16), b.astype(bf16), (((0,), (0,)), ((), ())), preferred_element_type=f32)


def sigmoid(x):
    return 1.0 / (1.0 + jnp.exp(-x))


def conv_masks(dcol_ref, rows):
    here = dcol_ref[pl.ds(HALO, rows), :]
    return [
        jnp.broadcast_to((dcol_ref[pl.ds(HALO - KW + 1 + i, rows), :] == here).astype(f32), (rows, HD))
        for i in range(KW - 1)
    ]


def conv_sum(x_ref, taps_ref, masks, ext, h):
    rows = x_ref.shape[0] - HALO
    lanes = pl.ds(h * HD, HD)
    ext[...] = x_ref[:, lanes].astype(f32)
    total = taps_ref[pl.ds(KW - 1, 1), lanes] * ext[pl.ds(HALO, rows), :]
    for i in range(KW - 1):
        total = total + taps_ref[pl.ds(i, 1), lanes] * ext[pl.ds(HALO - KW + 1 + i, rows), :] * masks[i]
    return total


def low(x):
    return x.astype(bf16).astype(f32)


def unit_scale(x):
    return lax.rsqrt(jnp.sum(x * x, axis=-1, keepdims=True) + EPS_UNIT)


def head_column(table, head):
    lane = lax.broadcasted_iota(jnp.int32, table.shape, 1)
    return jnp.sum(jnp.where(lane == head, table, 0.0), axis=1, keepdims=True)


def chunk_marks(dcol_ref, c):
    at = HALO + c * CHUNK
    docs = dcol_ref[pl.ds(at, CHUNK), :]
    prior = dcol_ref[pl.ds(at - 1, 1), :]
    last = dcol_ref[pl.ds(at + CHUNK - 1, 1), :]
    carry = (docs == prior).astype(f32)
    tail = (docs == last).astype(f32)
    carry_last = (last == prior).astype(f32)
    return docs, carry, tail, carry_last


def tri_index():
    row = lax.broadcasted_iota(jnp.int32, (CHUNK, CHUNK), 0)
    col = lax.broadcasted_iota(jnp.int32, (CHUNK, CHUNK), 1)
    return row, col


def inverses(systems, differ):
    row, col = tri_index()
    eye = (row == col).astype(f32)
    found = [eye - jnp.where(differ == 1, low_part, 0.0) for low_part in systems]
    step = 2
    while step < CHUNK:
        side = (differ >= step) & (differ < 2 * step)
        lows = [x.astype(bf16) for x in found]
        inner = [dot_nn(jnp.where(side, s, 0.0), x) for s, x in zip(systems, lows)]
        outer = [dot_nn(x, y) for x, y in zip(lows, inner)]
        found = [x - y for x, y in zip(found, outer)]
        step *= 2
    return found


def fwd_local_kernel(
    q_ref, k_ref, v_ref, tq_ref, tk_ref, tv_ref, lg_ref, dcol_ref, drow_ref, *refs,
):
    qn_ref, kn_ref, tinv_ref, wu_ref, gain_ref, pre_ref, total_ref, ext = refs[-8:]
    group = pl.program_id(0)
    rows = q_ref.shape[0] - HALO
    chunks = rows // CHUNK
    masks = conv_masks(dcol_ref, rows)
    heads = range(q_ref.shape[1] // HD)

    def filtered(x, taps, h):
        s = conv_sum(x, taps, masks, ext.at[h], h)
        return low(s * sigmoid(s))

    queries = [filtered(q_ref, tq_ref, h) for h in heads]
    keys = [filtered(k_ref, tk_ref, h) for h in heads]
    values = [filtered(v_ref, tv_ref, h) for h in heads]
    kns, kbs, vbs = [], [], []
    for h in heads:
        lanes = pl.ds(h * HD, HD)
        qn_ref[:, lanes] = (queries[h] * (unit_scale(queries[h]) * HD**-0.5)).astype(bf16)
        kn = keys[h] * unit_scale(keys[h])
        kn_ref[:, lanes] = kn.astype(bf16)
        beta = sigmoid(head_column(lg_ref[...].astype(f32), group * len(heads) + h))
        kns.append(kn.astype(bf16))
        kbs.append((beta * kn).astype(bf16))
        vbs.append((beta * values[h]).astype(bf16))
    row, col = tri_index()
    differ = row ^ col
    marks = [chunk_marks(dcol_ref, c) for c in range(chunks)]
    cut = lambda x, c: x[c * CHUNK : (c + 1) * CHUNK]
    items = [(h, c) for h in heads for c in range(chunks)]
    keeps = [(marks[c][0] == drow_ref[pl.ds(c, 1), :]) & (col < row) for c in range(chunks)]
    systems = [dot_nt(cut(kbs[h], c), cut(kns[h], c)) for h, c in items]
    systems = [jnp.where(keeps[c], s, 0.0) for s, (h, c) in zip(systems, items)]
    found = [x.astype(bf16) for x in inverses(systems, differ)]
    both = [
        dot_nn(x, jnp.concatenate([cut(kbs[h], c), cut(vbs[h], c)], axis=1)) for x, (h, c) in zip(found, items)
    ]
    tails = [(cut(kns[h], c).astype(f32) * marks[c][2]).astype(bf16) for h, c in items]
    moved = [
        jnp.concatenate([(b[:, :HD] * marks[c][1]).astype(bf16), b[:, HD:].astype(bf16)], axis=1)
        for b, (h, c) in zip(both, items)
    ]
    steps = [dot_tn(t, m) for t, m in zip(tails, moved)]
    for i, (h, c) in enumerate(items):
        at = pl.ds(c * CHUNK, CHUNK)
        tinv_ref[h, at, :] = found[i]
        wu_ref[h, at, :] = both[i].astype(bf16)
        gain_ref[h, at, :] = steps[i][:, :HD].astype(bf16)
    eye = (row == col).astype(f32)
    states = [jnp.concatenate([eye, jnp.zeros_like(eye)], axis=1) for _ in heads]
    for c in range(chunks):
        lows = [state.astype(bf16) for state in states]
        for h in heads:
            pre_ref[h, pl.ds(c * CHUNK, CHUNK), :] = lows[h]
        gone = [dot_nn(steps[h * chunks + c][:, :HD], lows[h]) for h in heads]
        states = [
            marks[c][3] * states[h]
            - gone[h]
            + jnp.concatenate([jnp.zeros_like(eye), steps[h * chunks + c][:, HD:]], axis=1)
            for h in heads
        ]
    for h in heads:
        total_ref[h] = states[h].astype(bf16)


def col_spec(rows, base, count=1):
    return pl.BlockSpec((rows, count * HD), lambda h: (0, base // count + h))


def full_spec(shape):
    return pl.BlockSpec(shape, lambda h: (0,) * len(shape))


def head_spec(shape, count=1):
    return pl.BlockSpec((count,) + shape, lambda h: (h,) + (0,) * len(shape))


def params():
    return pltpu.CompilerParams(vmem_limit_bytes=VMEM_LIMIT, dimension_semantics=("arbitrary",))


def cost(micros, rows):
    return pl.CostEstimate(flops=0, bytes_accessed=int(micros * 3.69e6 * rows / 512), transcendentals=0)


def fwd_local(projected, taps, logits, dcol, drow, after):
    rows = projected.shape[0] - HALO
    chunks = rows // CHUNK
    sds = jax.ShapeDtypeStruct
    return pl.pallas_call(
        fwd_local_kernel,
        grid=(H // TOGETHER,),
        in_specs=[col_spec(rows + HALO, i * H, TOGETHER) for i in range(3)]
        + [col_spec(KW, 0, TOGETHER), col_spec(KW, H, TOGETHER), col_spec(KW, 2 * H, TOGETHER)]
        + [full_spec((rows, HD)), full_spec((rows + HALO, 1)), full_spec((chunks, CHUNK))]
        + [pl.BlockSpec(memory_space=pl.ANY) for _ in after],
        out_specs=[
            col_spec(rows, 0, TOGETHER),
            col_spec(rows, 0, TOGETHER),
            head_spec((rows, CHUNK), TOGETHER),
            head_spec((rows, 2 * HD), TOGETHER),
            head_spec((rows, HD), TOGETHER),
            head_spec((rows, 2 * HD), TOGETHER),
            head_spec((HD, 2 * HD), TOGETHER),
        ],
        out_shape=[
            sds((rows, D), bf16),
            sds((rows, D), bf16),
            sds((H, rows, CHUNK), bf16),
            sds((H, rows, 2 * HD), bf16),
            sds((H, rows, HD), bf16),
            sds((H, rows, 2 * HD), bf16),
            sds((H, HD, 2 * HD), bf16),
        ],
        scratch_shapes=[pltpu.VMEM((TOGETHER, rows + HALO, HD), f32)],
        compiler_params=params(),
        cost_estimate=cost(14.5, rows),
        name="delta_local",
    )(*([projected] * 3 + [taps] * 3 + [logits, dcol, drow]), *after)


def fwd_read_kernel(qn_ref, kn_ref, wu_ref, dcol_ref, drow_ref, r_ref, o_ref):
    rows = qn_ref.shape[0]
    row, col = tri_index()
    chunks = range(rows // CHUNK)
    ats = [pl.ds(c * CHUNK, CHUNK) for c in chunks]
    marks = [chunk_marks(dcol_ref, c) for c in chunks]
    keeps = [(marks[c][0] == drow_ref[pl.ds(c, 1), :]) & (col <= row) for c in chunks]
    items = [(h, c) for h in range(qn_ref.shape[1] // HD) for c in chunks]
    lanes = [pl.ds(h * HD, HD) for h, _ in items]
    parts = [dot_nt(qn_ref[ats[c], lane], kn_ref[ats[c], lane]) for lane, (h, c) in zip(lanes, items)]
    parts = [jnp.where(keeps[c], part, 0.0).astype(bf16) for part, (h, c) in zip(parts, items)]
    ws = [(wu_ref[h, ats[c], :HD].astype(f32) * marks[c][1]).astype(bf16) for h, c in items]
    both = [
        dot_nn(part, jnp.concatenate([w, wu_ref[h, ats[c], HD:]], axis=1)) for part, w, (h, c) in zip(parts, ws, items)
    ]
    for lane, b, (h, c) in zip(lanes, both, items):
        r_ref[ats[c], lane] = (qn_ref[ats[c], lane].astype(f32) * marks[c][1] - b[:, :HD]).astype(bf16)
        o_ref[ats[c], lane] = b[:, HD:]


def fwd_read(qn, kn, wu, dcol, drow):
    rows = qn.shape[0]
    chunks = rows // CHUNK
    sds = jax.ShapeDtypeStruct
    return pl.pallas_call(
        fwd_read_kernel,
        grid=(H // TOGETHER,),
        in_specs=[col_spec(rows, 0, TOGETHER), col_spec(rows, 0, TOGETHER), head_spec((rows, 2 * HD), TOGETHER), full_spec((rows + HALO, 1)), full_spec((chunks, CHUNK))],
        out_specs=[col_spec(rows, 0, TOGETHER), col_spec(rows, 0, TOGETHER)],
        out_shape=[sds((rows, D), bf16), sds((rows, D), f32)],
        compiler_params=params(),
        cost_estimate=cost(3.2, rows),
        name="delta_read",
    )(qn, kn, wu, dcol, drow)


def fwd_state_kernel(moves, paired, place_ref, *refs):
    ins, (state_ref, out_ref, head_ref) = refs[: moves + 5], refs[-3:]
    *near_refs, far_ref, pre_ref, r_ref, o_ref, gain_ref = ins
    rows = r_ref.shape[0]
    heads = range(r_ref.shape[1] // HD)
    states = [far_ref[h].astype(f32) for h in heads]
    if paired:
        states = [jnp.where(place_ref[0] >= 2, state, 0.0) for state in states]
    for near_ref in reversed(near_refs):
        moved = [dot_nn(near_ref[h, :, :HD], states[h]) + near_ref[h, :, HD:].astype(f32) for h in heads]
        states = [jnp.where(place_ref[0] % 2 == 1, m, s) if paired else m for m, s in zip(moved, states)]
    lows = [state.astype(bf16) for state in states]
    items = [(h, c) for h in heads for c in range(rows // CHUNK)]
    ats = [pl.ds(c * CHUNK, CHUNK) for _, c in items]
    lanes = [pl.ds(h * HD, HD) for h, _ in items]
    nows = [dot_nn(pre_ref[h, at, :HD], lows[h]) for at, (h, c) in zip(ats, items)]
    nows = [(now + pre_ref[h, at, HD:].astype(f32)).astype(bf16) for now, at, (h, c) in zip(nows, ats, items)]
    outs = [dot_nn(r_ref[at, lane], now) for at, lane, now in zip(ats, lanes, nows)]
    for out, now, at, lane, (h, c) in zip(outs, nows, ats, lanes, items):
        state_ref[h, at, :] = now
        o = o_ref[at, lane] + out
        out_ref[at, lane] = o
        scale = lax.rsqrt(jnp.mean(o * o, axis=-1, keepdims=True) + EPS_NORM)
        head_ref[at, lane] = (o * scale * gain_ref[...]).astype(bf16)


def fwd_state(place, paired, nears, far, pre, r, o, gain, after):
    rows = r.shape[0]
    sds = jax.ShapeDtypeStruct
    return pl.pallas_call(
        partial(fwd_state_kernel, len(nears), paired),
        grid=(H // TOGETHER,),
        in_specs=[
            pl.BlockSpec(memory_space=pltpu.SMEM),
            *[head_spec((HD, 2 * HD), TOGETHER) for _ in nears],
            head_spec((HD, HD), TOGETHER),
            head_spec((rows, 2 * HD), TOGETHER),
            col_spec(rows, 0, TOGETHER),
            col_spec(rows, 0, TOGETHER),
            full_spec((1, HD)),
            *[pl.BlockSpec(memory_space=pl.ANY) for _ in after],
        ],
        out_specs=[head_spec((rows, HD), TOGETHER), col_spec(rows, 0, TOGETHER), col_spec(rows, 0, TOGETHER)],
        out_shape=[sds((H, rows, HD), bf16), sds((rows, D), f32), sds((rows, D), bf16)],
        compiler_params=params(),
        cost_estimate=cost(4.3, rows),
        name="delta_state",
    )(place, *nears, far, pre, r, o, gain, *after)


def bwd_local_kernel(dhead_ref, o_ref, r_ref, gain_ref, step_ref, dcol_ref, *refs):
    do_ref, dgain_ref, total_ref = refs[-3:]
    rows = o_ref.shape[0]
    chunks = rows // CHUNK

    @pl.when(pl.program_id(0) == 0)
    def _():
        dgain_ref[...] = jnp.zeros_like(dgain_ref)

    heads = range(o_ref.shape[1] // HD)
    ats = [pl.ds(c * CHUNK, CHUNK) for c in range(chunks)]
    marks = [chunk_marks(dcol_ref, c)[3] for c in range(chunks)]
    dos = []
    for h in heads:
        lanes = pl.ds(h * HD, HD)
        o = o_ref[:, lanes]
        dy = dhead_ref[:, lanes].astype(f32)
        scale = lax.rsqrt(jnp.mean(o * o, axis=-1, keepdims=True) + EPS_NORM)
        x = o * scale
        dgain_ref[...] += jnp.sum(dy * x, axis=0, keepdims=True)
        dx = dy * gain_ref[...]
        do = (scale * (dx - x * jnp.mean(dx * x, axis=-1, keepdims=True))).astype(bf16)
        do_ref[:, lanes] = do
        dos.append(do)
    gives = [
        [dot_tn(r_ref[ats[c], pl.ds(h * HD, HD)], dos[h][c * CHUNK : (c + 1) * CHUNK]) for c in range(chunks)] for h in heads
    ]
    states = [gives[h][chunks - 1] for h in heads]
    for c in reversed(range(chunks - 1)):
        gone = [dot_tn(step_ref[h, ats[c], :], states[h]) for h in heads]
        states = [marks[c] * states[h] - gone[h] + gives[h][c] for h in heads]
    for h in heads:
        total_ref[h] = states[h].astype(bf16)


def bwd_local(dhead, o, r, gain, step, dcol, after):
    rows = o.shape[0]
    sds = jax.ShapeDtypeStruct
    return pl.pallas_call(
        bwd_local_kernel,
        grid=(H // TOGETHER,),
        in_specs=[col_spec(rows, 0, TOGETHER), col_spec(rows, 0, TOGETHER), col_spec(rows, 0, TOGETHER), full_spec((1, HD)), head_spec((rows, HD), TOGETHER), full_spec((rows + HALO, 1))]
        + [pl.BlockSpec(memory_space=pl.ANY) for _ in after],
        out_specs=[col_spec(rows, 0, TOGETHER), full_spec((1, HD)), head_spec((HD, HD), TOGETHER)],
        out_shape=[sds((rows, D), bf16), sds((1, HD), f32), sds((H, HD, HD), bf16)],
        compiler_params=params(),
        cost_estimate=cost(3.8, rows),
        name="delta_back_local",
    )(dhead, o, r, gain, step, dcol, *after)


def bwd_main_kernel(moves, paired, place_ref, *refs):
    later, refs = refs[: 2 * moves + 1], refs[2 * moves + 1 :]
    ins, outs = refs[:15], refs[-12:]
    bwd_main_body(place_ref if paired else None, later, *ins, *outs)


def bwd_main_body(
    place_ref, later, q_ref, k_ref, v_ref, tq_ref, tk_ref, tv_ref, lg_ref, dcol_ref, drow_ref,
    tinv_ref, wu_ref, step_ref, state_ref, r_ref, do_ref,
    dproj_ref, rq_ref, rk_ref, rv_ref, cq_ref, ck_ref, cv_ref, dl_ref, ext, grad, held, sems,
):
    group = pl.program_id(0)
    rows = q_ref.shape[0] - HALO
    chunks = range(rows // CHUNK)
    heads = range(q_ref.shape[1] // HD)
    masks = conv_masks(dcol_ref, rows)
    row, col = tri_index()
    cut = lambda x, c: x[c * CHUNK : (c + 1) * CHUNK]

    def filtered(x, taps, h, which):
        s = conv_sum(x, taps, masks, ext.at[which + 3 * h], h)
        gate = sigmoid(s)
        return low(s * gate), gate * (1.0 + s * (1.0 - gate))

    queries, slope_q, scale_q, qns = [], [], [], []
    keys, slope_k, scale_k, kns = [], [], [], []
    values, slope_v, betas, kbs = [], [], [], []
    for h in heads:
        query, slope = filtered(q_ref, tq_ref, h, 0)
        queries.append(query)
        slope_q.append(slope)
        scale_q.append(unit_scale(query))
        qns.append((query * scale_q[h] * HD**-0.5).astype(bf16))
        key, slope = filtered(k_ref, tk_ref, h, 1)
        slope_k.append(slope)
        scale_k.append(unit_scale(key))
        kns.append(key * scale_k[h])
        value, slope = filtered(v_ref, tv_ref, h, 2)
        values.append(value)
        slope_v.append(slope)
        betas.append(sigmoid(head_column(lg_ref[...].astype(f32), group * len(heads) + h)))
        kbs.append((betas[h] * kns[h]).astype(bf16))

    moves = len(later) // 2
    marks = [chunk_marks(dcol_ref, c) for c in chunks]
    ats = [pl.ds(c * CHUNK, CHUNK) for c in chunks]
    items = [(h, c) for h in heads for c in chunks]
    lanes = [pl.ds(h * HD, HD) for h in heads]
    dss = [later[-1][h].astype(f32) for h in heads]
    if place_ref is not None:
        dss = [jnp.where(place_ref[0] < 2, ds, 0.0) for ds in dss]
    for i in reversed(range(moves)):
        moved = [dot_tn(later[i][h], dss[h]) + later[moves + i][h].astype(f32) for h in heads]
        dss = [m if place_ref is None else jnp.where(place_ref[0] % 2 == 0, m, ds) for m, ds in zip(moved, dss)]
    gives = [dot_tn(r_ref[ats[c], lanes[h]], do_ref[ats[c], lanes[h]]) for h, c in items]
    leaving = {}
    for c in reversed(chunks):
        for h in heads:
            leaving[h, c] = dss[h].astype(bf16)
        if c:
            gone = [dot_tn(step_ref[h, ats[c], :], leaving[h, c]) for h in heads]
            dss = [marks[c][3] * dss[h] - gone[h] + gives[h * len(chunks) + c] for h in heads]

    each = range(len(items))
    carries = [marks[c][1] for _, c in items]
    tails = [marks[c][2] for _, c in items]
    sames = [marks[c][0] == drow_ref[pl.ds(c, 1), :] for c in chunks]
    uptos = [sames[c] & (col <= row) for _, c in items]
    belows = [sames[c] & (col < row) for _, c in items]
    q_cs = [cut(qns[h], c) for h, c in items]
    k_cs = [cut(kns[h], c).astype(bf16) for h, c in items]
    kb_cs = [cut(kbs[h], c) for h, c in items]
    dos = [do_ref[ats[c], lanes[h]] for h, c in items]
    wus = [wu_ref[h, ats[c], :] for h, c in items]
    states = [state_ref[h, ats[c], :] for h, c in items]
    leave = [leaving[item] for item in items]
    parts = [dot_nt(q_cs[i], k_cs[i]) for i in each]
    reads = [dot_nn(wus[i][:, :HD], states[i]) for i in each]
    kds = [dot_nn(k_cs[i], leave[i]) for i in each]
    parts = [jnp.where(uptos[i], parts[i], 0.0).astype(bf16) for i in each]
    deltas = [(wus[i][:, HD:].astype(f32) - carries[i] * reads[i]).astype(bf16) for i in each]
    pds = [dot_tn(parts[i], dos[i]) for i in each]
    dparts = [dot_nt(dos[i], deltas[i]) for i in each]
    dkfs = [dot_nt(deltas[i], leave[i]) for i in each]
    dds = [pds[i] + tails[i] * kds[i] for i in each]
    throughs = [dot_nt(jnp.concatenate([dos[i], dds[i].astype(bf16)], axis=0), states[i]) for i in each]
    inner = [
        jnp.concatenate([(-(carries[i] * throughs[i][CHUNK:])).astype(bf16), dds[i].astype(bf16)], axis=1) for i in each
    ]
    dwus = [dot_tn(tinv_ref[h, ats[c], :], x) for x, (h, c) in zip(inner, items)]
    dlows = [dot_nt(dwus[i], wus[i]) for i in each]
    pairs = [
        jnp.concatenate(
            [jnp.where(uptos[i], dparts[i], 0.0).astype(bf16), jnp.where(belows[i], -dlows[i], 0.0).astype(bf16)], axis=0
        )
        for i in each
    ]
    ontos = [dot_nn(pairs[i], k_cs[i]) for i in each]
    backs = [dot_tn(pairs[i], jnp.concatenate([q_cs[i], kb_cs[i]], axis=0)) for i in each]
    b_cs = [cut(betas[h], c) for h, c in items]
    dqs = [carries[i] * throughs[i][:CHUNK] + ontos[i][:CHUNK] for i in each]
    dkbs = [dwus[i][:, :HD] + ontos[i][CHUNK:] for i in each]
    dks = [backs[i] + tails[i] * dkfs[i] + b_cs[i] * dkbs[i] for i in each]
    dvs = [b_cs[i] * dwus[i][:, HD:] for i in each]
    dbs = [
        jnp.sum(dkbs[i] * cut(kns[h], c) + dwus[i][:, HD:] * cut(values[h], c), axis=1, keepdims=True)
        for i, (h, c) in zip(each, items)
    ]

    @pl.when(group == 0)
    def _():
        dl_ref[...] = jnp.zeros_like(dl_ref)

    slot = lax.rem(group, 2)
    width = len(heads) * HD

    def sent(step, which):
        start = pl.multiple_of(which * D + step * width, 128)
        return pltpu.make_async_copy(
            held.at[lax.rem(step, 2), which], dproj_ref.at[:, pl.ds(start, width)], sems.at[lax.rem(step, 2), which]
        )

    @pl.when(group >= 2)
    def _():
        for which in range(3):
            sent(group - 2, which).wait()

    for i in range(KW - 1):
        grad[i, pl.ds(0, HALO), :] = jnp.zeros((HALO, HD), f32)
        grad[i, pl.ds(HALO + rows, 8), :] = jnp.zeros((8, HD), f32)

    def conv_back(dfilt, slope, taps_ref, rim_ref, dtap_ref, h, which):
        ds_ = low(dfilt) * slope
        lane = lanes[h]
        x = ext.at[which + 3 * h]
        dtap_ref[pl.ds(KW - 1, 1), lane] = jnp.sum(ds_ * x[pl.ds(HALO, rows), :], axis=0, keepdims=True)
        total = ds_ * taps_ref[pl.ds(KW - 1, 1), lane]
        rim = jnp.zeros((HALO, HD), f32)
        for i in range(KW - 1):
            masked = ds_ * masks[i]
            grad[i, pl.ds(HALO, rows), :] = masked
            place_i = pl.ds(HALO - KW + 1 + i, rows)
            dtap_ref[pl.ds(i, 1), lane] = jnp.sum(masked * x[place_i, :], axis=0, keepdims=True)
            tap = taps_ref[pl.ds(i, 1), lane]
            total = total + tap * grad[i, pl.ds(HALO + KW - 1 - i, rows), :]
            rim = rim + tap * grad[i, pl.ds(KW - 1 - i, HALO), :]
        rim_ref[:, lane] = rim.astype(bf16)
        held[slot, which, :, lane] = total.astype(bf16)

    lane_index = lax.broadcasted_iota(jnp.int32, (rows, HD), 1)
    for h in heads:
        join = lambda parts: jnp.concatenate(parts[h * len(chunks) : (h + 1) * len(chunks)], axis=0)
        dqn = join(dqs) * HD**-0.5
        unit = queries[h] * scale_q[h]
        dquery = scale_q[h] * (dqn - unit * jnp.sum(dqn * unit, axis=-1, keepdims=True))
        dkn = join(dks)
        dkeys = scale_k[h] * (dkn - kns[h] * jnp.sum(dkn * kns[h], axis=-1, keepdims=True))
        dlogit = join(dbs) * betas[h] * (1.0 - betas[h])
        dl_ref[...] = jnp.where(
            lane_index == group * len(heads) + h, dlogit, dl_ref[...].astype(f32)
        ).astype(bf16)
        conv_back(dquery, slope_q[h], tq_ref, rq_ref, cq_ref, h, 0)
        conv_back(dkeys, slope_k[h], tk_ref, rk_ref, ck_ref, h, 1)
        conv_back(join(dvs), slope_v[h], tv_ref, rv_ref, cv_ref, h, 2)
    for which in range(3):
        sent(group, which).start()

    @pl.when(group == pl.num_programs(0) - 1)
    def _():
        for which in range(3):
            sent(group - 1, which).wait()
            sent(group, which).wait()


def bwd_main(place, paired, moves, gives, projected, taps, logits, dcol, drow, tinv, wu, step, state, r, do, after):
    rows = projected.shape[0] - HALO
    chunks = rows // CHUNK
    sds = jax.ShapeDtypeStruct
    return pl.pallas_call(
        partial(bwd_main_kernel, len(moves), paired),
        grid=(H // TOGETHER_BACK,),
        in_specs=[pl.BlockSpec(memory_space=pltpu.SMEM)]
        + [head_spec((HD, HD), TOGETHER_BACK) for _ in (*moves, *gives)]
        + [col_spec(rows + HALO, i * H, TOGETHER_BACK) for i in range(3)]
        + [col_spec(KW, 0, TOGETHER_BACK), col_spec(KW, H, TOGETHER_BACK), col_spec(KW, 2 * H, TOGETHER_BACK)]
        + [full_spec((rows, HD)), full_spec((rows + HALO, 1)), full_spec((chunks, CHUNK))]
        + [head_spec((rows, CHUNK), TOGETHER_BACK), head_spec((rows, 2 * HD), TOGETHER_BACK), head_spec((rows, HD), TOGETHER_BACK), head_spec((rows, HD), TOGETHER_BACK)]
        + [col_spec(rows, 0, TOGETHER_BACK), col_spec(rows, 0, TOGETHER_BACK)]
        + [pl.BlockSpec(memory_space=pl.ANY) for _ in after],
        out_specs=[pl.BlockSpec(memory_space=pl.ANY)] + [col_spec(HALO, 0, TOGETHER_BACK)] * 3 + [col_spec(KW, 0, TOGETHER_BACK)] * 3 + [full_spec((rows, HD))],
        out_shape=[sds((rows, 3 * D), bf16)] + [sds((HALO, D), bf16)] * 3 + [sds((KW, D), f32)] * 3 + [sds((rows, HD), bf16)],
        scratch_shapes=[
            pltpu.VMEM((3 * TOGETHER_BACK, rows + HALO, HD), f32),
            pltpu.VMEM((KW - 1, rows + HALO + 8, HD), f32),
            pltpu.VMEM((2, 3, rows, TOGETHER_BACK * HD), bf16),
            pltpu.SemaphoreType.DMA((2, 3)),
        ],
        compiler_params=params(),
        cost_estimate=cost(24, rows),
        name="delta_back",
    )(place, *moves, *gives, *([projected] * 3 + [taps] * 3), logits, dcol, drow, tinv, wu, step, state, r, do, *after)


def pair_forward_kernel(place_ref, own_ref, other_ref, out_ref):
    late = place_ref[0] % 2 == 1
    for h in range(H):
        own, partner = own_ref[h].astype(f32), other_ref[h].astype(f32)
        first, second = jnp.where(late, partner, own), jnp.where(late, own, partner)
        out_ref[h] = (dot_nn(second[:, :HD], first[:, HD:]) + second[:, HD:]).astype(bf16)


def pair_backward_kernel(place_ref, own_a_ref, other_a_ref, own_ref, other_ref, out_ref):
    late = place_ref[0] % 2 == 1
    for h in range(H):
        own, partner = own_ref[h].astype(f32), other_ref[h].astype(f32)
        first, second = jnp.where(late, partner, own), jnp.where(late, own, partner)
        passed = jnp.where(late, other_a_ref[h, :, :HD].astype(f32), own_a_ref[h, :, :HD].astype(f32))
        out_ref[h] = (first + dot_tn(passed, second)).astype(bf16)


def pair_state(kernel, place, *arrays, after=()):
    count = len(arrays) + 1
    return pl.pallas_call(
        lambda *refs: kernel(*refs[:count], refs[-1]),
        in_specs=[pl.BlockSpec(memory_space=pltpu.SMEM)]
        + [pl.BlockSpec(memory_space=pltpu.VMEM)] * len(arrays)
        + [pl.BlockSpec(memory_space=pl.ANY)] * len(after),
        out_specs=pl.BlockSpec(memory_space=pltpu.VMEM),
        out_shape=jax.ShapeDtypeStruct((H, HD, HD), bf16),
        cost_estimate=cost(3, 512),
        name="pair_state",
        compiler_params=pltpu.CompilerParams(vmem_limit_bytes=VMEM_LIMIT),
    )(place, *arrays, *after)


def branch_kernel(x_ref, weight_ref, stream_ref, valid_ref, gain_ref, out_ref, normed_ref, sums_ref, total, *, last):
    step = pl.program_id(0)

    @pl.when(step == 0)
    def _():
        total[...] = jnp.zeros_like(total)

    total[...] += dot_nn(x_ref[...], weight_ref[...])

    @pl.when(step == pl.num_programs(0) - 1)
    def _():
        branch = total[...]
        stream = stream_ref[...] + branch
        out_ref[...] = stream
        sums_ref[pl.ds(0, 1), :] = jnp.sum(branch * branch * valid_ref[...], axis=0, keepdims=True)
        square = stream * stream
        sums_ref[pl.ds(1, 1), :] = jnp.sum(square * valid_ref[...], axis=0, keepdims=True)
        if last:
            normed_ref[...] = stream.astype(bf16)
        else:
            scale = lax.rsqrt(jnp.mean(square, axis=-1, keepdims=True) + EPS_NORM)
            normed_ref[...] = (stream * scale * gain_ref[...]).astype(bf16)


def branch(x, weight, stream, valid, gain, last, after, steps):
    rows, depth = x.shape
    sds = jax.ShapeDtypeStruct
    return pl.pallas_call(
        lambda *refs: branch_kernel(*refs[:5], *refs[-4:], last=last),
        grid=(steps,),
        in_specs=[
            pl.BlockSpec((rows, depth // steps), lambda j: (0, j)),
            pl.BlockSpec((depth // steps, D), lambda j: (j, 0)),
            full_spec((rows, D)),
            full_spec((rows, 1)),
            full_spec((1, D)),
        ]
        + [pl.BlockSpec(memory_space=pl.ANY) for _ in after],
        out_specs=[full_spec((rows, D)), full_spec((rows, D)), full_spec((2, D))],
        out_shape=[sds((rows, D), f32), sds((rows, D), bf16), sds((2, D), f32)],
        scratch_shapes=[pltpu.VMEM((rows, D), f32)],
        compiler_params=params(),
        cost_estimate=cost(5, rows),
        name="branch",
    )(x, weight, stream, valid, gain, *after)


def act_back_kernel(g_ref, down_ref, both_ref, out_ref):
    dact = dot_nt(g_ref[...], down_ref[...])
    gate, up = both_ref[0].astype(f32), both_ref[1].astype(f32)
    part = sigmoid(gate)
    silu = gate * part
    out_ref[0] = (dact * up * (part + silu * (1.0 - part))).astype(bf16)
    out_ref[1] = (dact * silu).astype(bf16)


def gated_back(g, down, both, after, steps=11):
    rows, half = g.shape[0], down.shape[0]
    size = half // steps
    block = pl.BlockSpec((2, rows, size), lambda j: (0, 0, j))
    return pl.pallas_call(
        lambda *refs: act_back_kernel(*refs[:3], refs[-1]),
        grid=(steps,),
        in_specs=[full_spec(g.shape), pl.BlockSpec((size, D), lambda j: (j, 0)), block]
        + [pl.BlockSpec(memory_space=pl.ANY) for _ in after],
        out_specs=block,
        out_shape=jax.ShapeDtypeStruct((2, rows, half), bf16),
        compiler_params=params(),
        cost_estimate=cost(8, rows),
        name="gated_back",
    )(g, down, both, *after)


def norm_back_kernel(d_ref, weight_ref, extra_ref, extra_weight_ref, stream_ref, g_ref, gain_ref, out_ref, low_ref, dgain_ref, total):
    step = pl.program_id(0)

    @pl.when(step == 0)
    def _():
        if extra_ref is None:
            total[...] = jnp.zeros_like(total)
        else:
            total[...] = dot_nt(extra_ref[...], extra_weight_ref[...])

    block = d_ref[0] if len(d_ref.shape) == 3 else d_ref[...]
    total[...] += dot_nt(block, weight_ref[...])

    @pl.when(step == pl.num_programs(0) - 1)
    def _():
        dn = total[...]
        stream = stream_ref[...]
        scale = lax.rsqrt(jnp.mean(stream * stream, axis=-1, keepdims=True) + EPS_NORM)
        x = stream * scale
        dgain_ref[...] = jnp.sum(dn * x, axis=0, keepdims=True)
        dx = dn * gain_ref[...]
        g = g_ref[...] + scale * (dx - x * jnp.mean(dx * x, axis=-1, keepdims=True))
        out_ref[...] = g
        low_ref[...] = g.astype(bf16)


def norm_back(d, weight, extra, stream, g, gain, after):
    rows = stream.shape[0]
    steps = 4
    size = weight.shape[1] // steps
    sds = jax.ShapeDtypeStruct
    if d.ndim == 3:
        d_spec = pl.BlockSpec((1, rows, size), lambda k: (k // 2, 0, k % 2))
    else:
        d_spec = pl.BlockSpec((rows, size), lambda k: (0, k))
    count = 5 + len(extra)

    def kernel(*refs):
        ins, outs = refs[:count], refs[-4:]
        more = ins[2 : 2 + len(extra)] if extra else (None, None)
        norm_back_kernel(*ins[:2], *more, *ins[2 + len(extra) :], *outs)

    return pl.pallas_call(
        kernel,
        grid=(steps,),
        in_specs=[d_spec, pl.BlockSpec((D, size), lambda k: (0, k))]
        + [full_spec(array.shape) for array in extra]
        + [full_spec((rows, D)), full_spec((rows, D)), full_spec((1, D))]
        + [pl.BlockSpec(memory_space=pl.ANY) for _ in after],
        out_specs=[full_spec((rows, D)), full_spec((rows, D)), full_spec((1, D))],
        out_shape=[sds((rows, D), f32), sds((rows, D), bf16), sds((1, D), f32)],
        scratch_shapes=[pltpu.VMEM((rows, D), f32)],
        compiler_params=params(),
        cost_estimate=cost(9, rows),
        name="norm_back",
    )(d, weight, *extra, stream, g, gain, *after)


def other(block, axis, mask):
    return lax.ppermute(block, axis, [(i, i ^ mask) for i in range(lax.axis_size(axis))])


def sum_over(block, axis):
    mask = 1
    while mask < lax.axis_size(axis):
        block = block + other(block, axis, mask)
        mask *= 2
    return block


ANY = pl.BlockSpec(memory_space=pl.ANY)
SMEM = pl.BlockSpec(memory_space=pltpu.SMEM)
VMEM = pl.BlockSpec(memory_space=pltpu.VMEM)


def run_copies(pairs, sems):
    copies = [pltpu.make_async_copy(src, dst, sems.at[i]) for i, (src, dst) in enumerate(pairs)]
    for copy in copies:
        copy.start()
    for copy in copies:
        copy.wait()


def aligned(index, size):
    return pl.ds(pl.multiple_of(index * size, 128), size)


def offsets(sizes):
    return [sum(sizes[:i]) for i in range(len(sizes))]


def pack_kernel(place_ref, *refs, plan):
    count = sum(len(sizes) for _, sizes in plan)
    ins, outs, sems = list(refs[:count]), refs[-len(plan) - 1 : -1], refs[-1]
    quarter = place_ref[0]
    pairs = []
    for (layer, sizes), out_ref in zip(plan, outs):
        for at, size in zip(offsets(sizes), sizes):
            pairs.append((ins.pop(0).at[layer, :, aligned(quarter, size)], out_ref.at[:, pl.ds(at, size)]))
    run_copies(pairs, sems)


def pack(place, groups, after):
    plan = [(layer, [weight.shape[2] // 4 for weight in weights]) for weights, layer in groups]
    weights = [weight for group, _ in groups for weight in group]
    return pl.pallas_call(
        partial(pack_kernel, plan=plan),
        in_specs=[SMEM] + [ANY] * (len(weights) + len(after)),
        out_specs=[VMEM] * len(groups),
        out_shape=[jax.ShapeDtypeStruct((128, sum(sizes)), bf16) for _, sizes in plan],
        scratch_shapes=[pltpu.SemaphoreType.DMA((len(weights),))],
        cost_estimate=cost(2 * len(groups), 512),
        name="pack_quarters",
        compiler_params=pltpu.CompilerParams(vmem_limit_bytes=VMEM_LIMIT),
    )(place, *weights, *after)


def arrivals(place_ref, pieces, weights, sizes, sems):
    seq, core = place_ref[0], place_ref[1]
    chips = weights[0].shape[0]
    copies = {0: [], 1: [], 2: [], 3: []}
    at = 0
    for own, (h, x, y, a, b) in ((core, pieces[:5]), (1 - core, pieces[5:])):
        for piece, mask, row in ((h, 0, 0), (x, 1, 0), (y, 2, 0), (a, 3, 0), (b, 3, chips // 2)):
            here = pl.ds(row, piece.shape[0])
            for weight, start, size in zip(weights, offsets(sizes), sizes):
                copies[mask].append(
                    pltpu.make_async_copy(
                        piece.at[:, :, pl.ds(start, size)], weight.at[here, own, :, aligned(seq ^ mask, size)], sems.at[at]
                    )
                )
                at += 1
    return copies


def columns_of(weight, quarter, size):
    block = weight[:, :, :, aligned(quarter, size)]
    return block.reshape(-1, size)


def project_kernel(place_ref, tail_ref, gain_ref, normed_ref, beta_ref, *refs, sizes):
    pieces, (out_ref, logits_ref, *full_refs) = refs[:10], refs[-9:-5]
    weight, more, low_tail, sems_in, sems_out = refs[-5:]
    copies = arrivals(place_ref, pieces, (weight, more), sizes, sems_in)
    for mask in (0, 1, 2, 3):
        for copy in copies[mask]:
            copy.start()
    tail = tail_ref[...]
    scale = lax.rsqrt(jnp.mean(tail * tail, axis=-1, keepdims=True) + EPS_NORM)
    low_tail[...] = (tail * scale * gain_ref[...]).astype(bf16)
    logits_ref[...] = dot_nn(normed_ref[...], beta_ref[...]).astype(bf16)
    sent = []
    for mask in (0, 1, 2, 3):
        for copy in copies[mask]:
            copy.wait()
        quarter = place_ref[0] ^ mask
        columns = aligned(quarter, sizes[0])
        sent.append(
            pltpu.make_async_copy(
                weight.at[:, :, :, columns], full_refs[0].at[:, :, :, columns], sems_out.at[mask]
            )
        )
        sent[-1].start()
        block = columns_of(weight, quarter, sizes[0])
        out_ref[pl.ds(0, HALO), columns] = dot_nn(low_tail[...], block).astype(bf16)
        out_ref[pl.ds(HALO, normed_ref.shape[0]), columns] = dot_nn(normed_ref[...], block).astype(bf16)
    sent.append(pltpu.make_async_copy(more, full_refs[1], sems_out.at[4]))
    sent[-1].start()
    for copy in sent:
        copy.wait()


def project(place, tail, gain, normed, beta, pieces, sizes, after):
    rows = normed.shape[0]
    chips = pieces[0].shape[0] // 128
    pieces = [piece.reshape(-1, 128, piece.shape[1]) for piece in pieces]
    sds = jax.ShapeDtypeStruct
    shapes = [(chips, 2, 128, 4 * size) for size in sizes]
    out, logits, first, second = pl.pallas_call(
        partial(project_kernel, sizes=sizes),
        in_specs=[SMEM] + [VMEM] * 4 + [ANY] * (len(pieces) + len(after)),
        out_specs=[VMEM, VMEM, ANY, ANY],
        out_shape=[sds((rows + HALO, 4 * sizes[0]), bf16), sds((rows, beta.shape[1]), bf16)]
        + [sds(shape, bf16) for shape in shapes],
        scratch_shapes=[pltpu.VMEM(shape, bf16) for shape in shapes]
        + [pltpu.VMEM((HALO, D), bf16), pltpu.SemaphoreType.DMA((20,)), pltpu.SemaphoreType.DMA((5,))],
        compiler_params=pltpu.CompilerParams(vmem_limit_bytes=VMEM_LIMIT),
        cost_estimate=cost(10, rows),
        name="project",
    )(place, tail, gain, normed, beta, *pieces, *after)
    return out, logits, first.reshape(D, -1), second.reshape(D, -1)


def gated_kernel(place_ref, x_ref, *refs, size):
    pieces, (act_ref, both_ref, full_ref) = refs[:10], refs[-9:-6]
    weight, act, both, sems_in, sems_out, sems_act = refs[-6:]
    copies = arrivals(place_ref, pieces, (weight,), (size,), sems_in)
    order = (0, 2, 1, 3)
    for mask in order:
        for copy in copies[mask]:
            copy.start()
    sent = []
    for turn in (0, 1):
        for mask in order[2 * turn : 2 * turn + 2]:
            for copy in copies[mask]:
                copy.wait()
            columns = aligned(place_ref[0] ^ mask, size)
            sent.append(
                pltpu.make_async_copy(weight.at[:, :, :, columns], full_ref.at[:, :, :, columns], sems_out.at[mask])
            )
            sent[-1].start()
        half = lax.rem(place_ref[0] ^ turn, 2)
        gate_block = dot_nn(x_ref[...], columns_of(weight, half, size))
        up_block = dot_nn(x_ref[...], columns_of(weight, half + 2, size))
        act[turn] = (gate_block * sigmoid(gate_block) * up_block).astype(bf16)
        both[turn, 0] = gate_block.astype(bf16)
        both[turn, 1] = up_block.astype(bf16)
        columns = aligned(half, size)
        sent.append(pltpu.make_async_copy(act.at[turn], act_ref.at[:, columns], sems_act.at[2 * turn]))
        sent.append(pltpu.make_async_copy(both.at[turn], both_ref.at[:, :, columns], sems_act.at[2 * turn + 1]))
        for copy in sent[-2:]:
            copy.start()
    for copy in sent:
        copy.wait()


def gated(place, x, pieces, size, after):
    rows = x.shape[0]
    chips = pieces[0].shape[0] // 128
    pieces = [piece.reshape(-1, 128, piece.shape[1]) for piece in pieces]
    sds = jax.ShapeDtypeStruct
    act, both, full = pl.pallas_call(
        partial(gated_kernel, size=size),
        in_specs=[SMEM, VMEM] + [ANY] * (len(pieces) + len(after)),
        out_specs=[ANY] * 3,
        out_shape=[sds((rows, 2 * size), bf16), sds((2, rows, 2 * size), bf16), sds((chips, 2, 128, 4 * size), bf16)],
        scratch_shapes=[
            pltpu.VMEM((chips, 2, 128, 4 * size), bf16),
            pltpu.VMEM((2, rows, size), bf16),
            pltpu.VMEM((2, 2, rows, size), bf16),
            pltpu.SemaphoreType.DMA((10,)),
            pltpu.SemaphoreType.DMA((4,)),
            pltpu.SemaphoreType.DMA((4,)),
        ],
        compiler_params=pltpu.CompilerParams(vmem_limit_bytes=VMEM_LIMIT),
        cost_estimate=cost(15, rows),
        name="gated",
    )(place, x, *pieces, *after)
    return act, both, full.reshape(D, -1)


def gate(array, after):
    return pl.pallas_call(
        lambda *refs: None,
        in_specs=[ANY] * (1 + len(after)),
        out_specs=ANY,
        out_shape=jax.ShapeDtypeStruct(array.shape, array.dtype),
        input_output_aliases={0: 0},
        cost_estimate=cost(0.5, 512),
        name="gate",
        compiler_params=pltpu.CompilerParams(vmem_limit_bytes=VMEM_LIMIT),
    )(array, *after)


def relay_kernel(x_ref, y_ref, *refs):
    a_ref, b_ref, _, _, sems = refs[-5:]
    half = a_ref.shape[0]
    run_copies([(x_ref.at[pl.ds(0, half)], a_ref), (y_ref.at[pl.ds(half, half)], b_ref)], sems)


def relay(over_x, over_y, after):
    half = jax.ShapeDtypeStruct((over_x.shape[0] // 2, over_x.shape[1]), over_x.dtype)
    whole = jax.ShapeDtypeStruct(over_x.shape, over_x.dtype)
    a, b, over_x, over_y = pl.pallas_call(
        relay_kernel,
        in_specs=[ANY] * (2 + len(after)),
        out_specs=[VMEM] * 2 + [ANY] * 2,
        out_shape=[half] * 2 + [whole] * 2,
        input_output_aliases={0: 2, 1: 3},
        scratch_shapes=[pltpu.SemaphoreType.DMA((2,))],
        cost_estimate=cost(2.5, 512),
        name="relay",
        compiler_params=pltpu.CompilerParams(vmem_limit_bytes=VMEM_LIMIT),
    )(over_x, over_y, *after)
    return (a, b), (over_x, over_y)


def core_groups():
    return [list(range(core, lax.axis_size("fsdp"), 2)) for core in range(2)]


def gather_chips(packed):
    return lax.all_gather(packed, "fsdp", axis=0, axis_index_groups=core_groups(), tiled=True)


def scatter_chips(total):
    return lax.psum_scatter(total, "fsdp", scatter_dimension=0, axis_index_groups=core_groups(), tiled=True)


def first_round(block):
    return other(block, "seq", 1), other(block, "seq", 2)


def second_round(passed):
    return other(passed[0], "seq", 2), other(passed[1], "seq", 1)


def interleaved(ref, core):
    blocks = ref.shape[1] // 256
    return jnp.concatenate([ref[:, aligned(2 * z + core, 128)] for z in range(blocks)], axis=1)


def grad_pieces_kernel(place_ref, *refs, count):
    ins, (o0_ref, o1_ref, o2_ref, oa_ref, ob_ref), scratch = refs[: 4 * count], refs[-6 - count : -1 - count], refs[-1 - count :]
    lefts, rights, turned, total = ins[: 2 * count], ins[2 * count :], scratch[:count], scratch[count]
    step = pl.program_id(0)
    tokens = lefts[0].shape[0]

    @pl.when(step == 0)
    def _():
        for i in range(2 * count):
            turned[i // 2][:, pl.ds((i % 2) * tokens, tokens)] = interleaved(lefts[i], place_ref[1]).T

    start = 0
    for i in range(count):
        a_ref, b_ref = rights[2 * i : 2 * i + 2]
        size = a_ref.shape[-1]
        a, b = [ref[0] if len(ref.shape) == 3 else ref[...] for ref in (a_ref, b_ref)]
        total[:, pl.ds(start, size)] = (
            dot_nn(turned[i][:, pl.ds(0, tokens)], a) + dot_nn(turned[i][:, pl.ds(tokens, tokens)], b)
        ).astype(bf16)
        start += size
    half = total.shape[0] // 2
    for i, out in enumerate((o0_ref, o1_ref, o2_ref)):

        @pl.when(step == i)
        def _(out=out):
            out[...] = total[...]

    @pl.when(step == 3)
    def _():
        oa_ref[...] = total[pl.ds(0, half), :]
        ob_ref[...] = total[pl.ds(half, half), :]


def grad_pieces(place, pairs, after):
    lefts = [left for pair in pairs for left in pair[0]]
    rights = [right for pair in pairs for right in pair[1]]
    tokens, rows = lefts[0].shape[0], lefts[0].shape[1] // 2
    sizes = [right.size // tokens // 4 for right in rights]
    width = sum(sizes[::2])
    whole = lambda array: pl.BlockSpec(array.shape, lambda j, place_ref: (0, 0))

    def quarter(right, size):
        if right.ndim == 2:
            return pl.BlockSpec((tokens, size), lambda j, place_ref: (0, place_ref[0] ^ j))
        return pl.BlockSpec(
            (1, tokens, size), lambda j, place_ref: ((place_ref[0] ^ j) // 2, 0, lax.rem(place_ref[0] ^ j, 2))
        )

    shapes = [(rows, width)] * 3 + [(rows // 2, width)] * 2
    return pl.pallas_call(
        partial(grad_pieces_kernel, count=len(pairs)),
        grid_spec=pltpu.PrefetchScalarGridSpec(
            num_scalar_prefetch=1,
            grid=(4,),
            in_specs=[whole(left) for left in lefts] + [quarter(right, size) for right, size in zip(rights, sizes)] + [ANY] * len(after),
            out_specs=[pl.BlockSpec(shape, lambda j, place_ref: (0, 0)) for shape in shapes],
            scratch_shapes=[pltpu.VMEM((rows, 2 * tokens), bf16) for _ in pairs] + [pltpu.VMEM((rows, width), bf16)],
        ),
        out_shape=[jax.ShapeDtypeStruct(shape, bf16) for shape in shapes],
        compiler_params=pltpu.CompilerParams(vmem_limit_bytes=VMEM_LIMIT),
        cost_estimate=cost(12, 512),
        name="grad_pieces",
    )(place, *lefts, *rights, *after)


def settle_kernel(place_ref, *refs, sizes):
    pieces, outs = refs[:5], refs[-len(sizes) :]
    rows = pieces[0].shape[0]
    masks = ((0, 0, rows), (1, 0, rows), (2, 0, rows), (3, 0, rows // 2), (3, rows // 2, rows // 2))
    for piece, (mask, at, count) in zip(pieces, masks):
        for out_ref, start, size in zip(outs, offsets(sizes), sizes):
            out_ref[0, pl.ds(at, count), aligned(place_ref[0] ^ mask, size)] = piece[:, pl.ds(start, size)].astype(f32)


def settle(place, pieces, sizes, layer, so_far):
    rows = pieces[0].shape[0]
    whole = lambda array: pl.BlockSpec(array.shape, lambda i: (0, 0))
    return pl.pallas_call(
        partial(settle_kernel, sizes=sizes),
        grid=(1,),
        in_specs=[SMEM] + [whole(piece) for piece in pieces] + [ANY] * len(so_far),
        out_specs=[pl.BlockSpec((1, rows, 4 * size), lambda i: (layer, 0, 0)) for size in sizes],
        out_shape=[jax.ShapeDtypeStruct((LAYERS, rows, 4 * size), f32) for size in sizes],
        input_output_aliases={6 + i: i for i in range(len(so_far))},
        compiler_params=pltpu.CompilerParams(vmem_limit_bytes=VMEM_LIMIT),
        cost_estimate=cost(3, 512),
        name="settle_gradient",
    )(place, *pieces, *so_far)


def merge_kernel(x_ref, y_ref, a_ref, b_ref, *refs):
    ox_ref, oy_ref = refs[-2:]
    ox_ref[...] = (x_ref[...].astype(f32) + b_ref[...].astype(f32)).astype(bf16)
    oy_ref[...] = (y_ref[...].astype(f32) + a_ref[...].astype(f32)).astype(bf16)


def merge(over_x, over_y, diag_a, diag_b, after):
    half, width = diag_a.shape
    rows = half // 4
    lower = pl.BlockSpec((rows, width), lambda i: (i, 0))
    upper = pl.BlockSpec((rows, width), lambda i: (i + 4, 0))
    whole = jax.ShapeDtypeStruct(over_x.shape, bf16)
    return pl.pallas_call(
        merge_kernel,
        grid=(4,),
        in_specs=[upper, lower, lower, lower] + [ANY] * len(after),
        out_specs=[upper, lower],
        out_shape=[whole, whole],
        input_output_aliases={0: 0, 1: 1},
        compiler_params=pltpu.CompilerParams(vmem_limit_bytes=VMEM_LIMIT),
        cost_estimate=cost(3.5, 512),
        name="merge",
    )(over_x, over_y, diag_a, diag_b, *after)


def total_kernel(own_ref, x_ref, y_ref, *refs):
    refs[-1][...] = (own_ref[...].astype(f32) + x_ref[...].astype(f32) + y_ref[...].astype(f32)).astype(bf16)


def total_of(own, from_x, from_y, after):
    rows, width = own.shape
    block = pl.BlockSpec((rows // 4, width), lambda i: (i, 0))
    return pl.pallas_call(
        total_kernel,
        grid=(4,),
        in_specs=[block] * 3 + [ANY] * len(after),
        out_specs=block,
        out_shape=jax.ShapeDtypeStruct(own.shape, bf16),
        compiler_params=pltpu.CompilerParams(vmem_limit_bytes=VMEM_LIMIT),
        cost_estimate=cost(4, 512),
        name="total",
    )(own, from_x, from_y, *after)


def gather_start(scattered, after):
    block = gate(scattered, after) if after else scattered
    return block, first_round(block)


def gather_settle(place, block, over, sizes, layer, so_far, after):
    passed, over = relay(*over, after)
    pieces = [block, *over, *second_round(passed)]
    return settle(place, pieces, sizes, layer, so_far), passed


def small_kernel(*refs):
    ins, out_ref = refs[:-1], refs[-1]
    at = 0
    out_ref[...] = jnp.zeros_like(out_ref)
    for ref in ins:
        for start in range(0, ref.shape[1], D):
            size = min(D, ref.shape[1] - start)
            out_ref[pl.ds(at, ref.shape[0]), pl.ds(0, size)] = ref[:, pl.ds(start, size)]
            at += ref.shape[0]


def small_rows(arrays):
    counts = [array.shape[0] * -(-array.shape[1] // D) for array in arrays]
    packed = pl.pallas_call(
        small_kernel,
        in_specs=[VMEM] * len(arrays),
        out_specs=VMEM,
        out_shape=jax.ShapeDtypeStruct((-(-sum(counts) // 8) * 8, D), f32),
        cost_estimate=cost(2, 512),
        name="small_rows",
        compiler_params=pltpu.CompilerParams(vmem_limit_bytes=VMEM_LIMIT),
    )(*arrays)
    return packed, offsets(counts)


def small_part(packed, start, shape):
    parts = -(-shape[1] // D)
    rows = [packed[start + i * shape[0] : start + (i + 1) * shape[0], : min(D, shape[1])] for i in range(parts)]
    return jnp.concatenate(rows, axis=1)


epsilon_norm = EPS_NORM


def shifted(block, axis, distance):
    devices = range(lax.axis_size(axis))
    route = [(i - distance, i) for i in devices if i - distance in devices]
    return lax.ppermute(block, axis, route)


def root_norm(values, gain):
    return (
        values * lax.rsqrt(jnp.mean(values * values, axis=-1, keepdims=True) + epsilon_norm) * gain
    )


def swiglu_act(gate_up):
    half_width = gate_up.shape[1] // 2
    return jax.nn.silu(gate_up[:, :half_width]) * gate_up[:, half_width:]


def contract_last(left, right):
    return lax.dot_general(
        left, right, (((1,), (1,)), ((), ())), preferred_element_type=jnp.float32
    )


def contract_first(left, right):
    return lax.dot_general(
        left, right, (((0,), (0,)), ((), ())), preferred_element_type=jnp.float32
    )


def fetch_rows(weights):
    return lax.all_gather(weights, "fsdp", axis=0, tiled=True)


def reduce_rows(left, right):
    return lax.psum_scatter(
        contract_first(left, right).astype(jnp.bfloat16), "fsdp", scatter_dimension=0, tiled=True
    )


def documents(segments, rows):
    doc_pad = jnp.concatenate([jnp.full((HALO,), -1, jnp.int32), segments])
    dcol = lax.dynamic_slice_in_dim(doc_pad, lax.axis_index("seq") * rows, rows + HALO)
    return dcol[:, None], dcol[HALO:].reshape(rows // CHUNK, CHUNK)


def on_device(
    tokens,
    segments,
    valid_mask,
    norm_gains,
    head_gain,
    conv_weight,
    beta_weight,
    qkv_weight,
    out_weight,
    gate_up_weight,
    down_weight,
    cotangent,
):
    rows = tokens.shape[1]
    pieces = lax.axis_size("seq")
    dcol, drow = documents(segments[0], rows)
    place = jnp.stack([lax.axis_index("seq"), lax.axis_index("fsdp") % 2]).astype(jnp.int32)
    valid_rows = valid_mask[0].astype(jnp.float32)
    stream = tokens[0].astype(jnp.float32)
    square_sums = []
    stored = []
    for at in range(LAYERS):
        qkv_full = fetch_rows(qkv_weight[at])
        out_full = fetch_rows(out_weight[at])
        gate_up_full = fetch_rows(gate_up_weight[at])
        down_full = fetch_rows(down_weight[at])
        square_sums.append(jnp.sum(jnp.sum(stream * stream, axis=1) * valid_rows))
        normed_one, pull_one = jax.vjp(root_norm, stream, norm_gains[at, 0])
        normed_one = normed_one.astype(jnp.bfloat16)
        projected = jnp.dot(normed_one, qkv_full, preferred_element_type=jnp.float32).astype(bf16)
        logits = jnp.dot(normed_one, beta_weight[at], preferred_element_type=jnp.float32).astype(bf16)
        logits = jnp.pad(logits, ((0, 0), (0, HD - H)))
        projected = jnp.concatenate([shifted(projected[rows - HALO :], "seq", 1), projected], axis=0)
        qn, kn, tinv, wu, step, pre, total = fwd_local(
            projected, conv_weight[at], logits, dcol, drow, []
        )
        nears = [shifted(total, "seq", d) for d in range(1, pieces - 1)]
        far = shifted(total[:, :, HD:], "seq", pieces - 1)
        moves = [shifted(total[:, :, :HD], "seq", -d) for d in range(1, pieces - 1)]
        reads, local_out = fwd_read(qn, kn, wu, dcol, drow)
        state, mixed, attended = fwd_state(
            place, False, nears, far, pre, reads, local_out, head_gain[at][None], []
        )
        branch = jnp.dot(attended, out_full, preferred_element_type=jnp.float32)
        square_sums.append(jnp.sum(jnp.sum(branch * branch, axis=1) * valid_rows))
        stream = stream + branch
        normed_two, pull_two = jax.vjp(root_norm, stream, norm_gains[at, 1])
        normed_two = normed_two.astype(jnp.bfloat16)
        gate_up = jnp.dot(normed_two, gate_up_full, preferred_element_type=jnp.float32)
        activated, pull_act = jax.vjp(swiglu_act, gate_up)
        activated = activated.astype(jnp.bfloat16)
        branch = jnp.dot(activated, down_full, preferred_element_type=jnp.float32)
        square_sums.append(jnp.sum(jnp.sum(branch * branch, axis=1) * valid_rows))
        stream = stream + branch
        stored.append(
            (
                qkv_full, out_full, gate_up_full, down_full, pull_one, normed_one, attended, pull_two, normed_two,
                pull_act, activated, moves, mixed,
                (projected, conv_weight[at], logits, dcol, drow, tinv, wu, step, state, reads),
            )
        )
    stream_grad = cotangent[0].astype(jnp.float32) * valid_rows[:, None]
    gain_list = []
    head_list = []
    filter_list = []
    beta_list = []
    weight_list = []
    for at in reversed(range(LAYERS)):
        (
            qkv_full, out_full, gate_up_full, down_full, pull_one, normed_one, attended, pull_two, normed_two,
            pull_act, activated, moves, mixed, kept,
        ) = stored[at]
        step, reads = kept[7], kept[9]
        branch_low = stream_grad.astype(jnp.bfloat16)
        grad_down = reduce_rows(activated, branch_low)
        (grad_gate_up,) = pull_act(contract_last(branch_low, down_full))
        grad_gate_up = grad_gate_up.astype(jnp.bfloat16)
        grad_gate = reduce_rows(normed_two, grad_gate_up)
        grad_state, gain_two = pull_two(contract_last(grad_gate_up, gate_up_full))
        stream_grad = stream_grad + grad_state
        branch_low = stream_grad.astype(jnp.bfloat16)
        grad_out = reduce_rows(attended, branch_low)
        grad_heads = contract_last(branch_low, out_full).astype(jnp.bfloat16)
        grad_mixed, gain_head, total = bwd_local(
            grad_heads, mixed, reads, head_gain[at][None], step, dcol, []
        )
        gives = [shifted(total, "seq", -d) for d in range(1, pieces)]
        grad_proj, *parts, grad_logits = bwd_main(place, False, moves, gives, *kept, grad_mixed, [])
        grad_logits = grad_logits[:, :H]
        rim = shifted(jnp.concatenate(parts[:3], axis=1), "seq", -1)
        grad_filter = jnp.concatenate(parts[3:6], axis=1)
        grad_proj = grad_proj.at[rows - HALO :].add(rim)
        grad_qkv = reduce_rows(normed_one, grad_proj)
        grad_beta = contract_first(normed_one, grad_logits)
        grad_normed = contract_last(grad_proj, qkv_full) + contract_last(grad_logits, beta_weight[at])
        grad_state, gain_one = pull_one(grad_normed)
        stream_grad = stream_grad + grad_state
        weight_list.append(
            [lax.psum(grad, "seq").astype(f32) for grad in (grad_qkv, grad_out, grad_gate, grad_down)]
        )
        gain_list.append(jnp.stack([gain_one, gain_two]))
        head_list.append(gain_head[0])
        filter_list.append(grad_filter)
        beta_list.append(grad_beta)
    stats_sum, valid_count, gains_sum, head_sum, filter_sum, beta_sum = lax.psum(
        (
            jnp.stack(square_sums),
            jnp.sum(valid_rows),
            jnp.stack(gain_list[::-1]),
            jnp.stack(head_list[::-1]),
            jnp.stack(filter_list[::-1]),
            jnp.stack(beta_list[::-1]),
        ),
        ("seq", "fsdp"),
    )
    rms_stats = jnp.sqrt(stats_sum / (jnp.maximum(valid_count, 1.0) * D)).reshape(LAYERS, 3)
    return (
        stream.astype(jnp.bfloat16)[None],
        stream_grad[None],
        gains_sum,
        head_sum,
        filter_sum,
        beta_sum,
        *[jnp.stack(pair[::-1]) for pair in zip(*weight_list)],
        rms_stats,
    )


def on_device_axes(
    tokens,
    segments,
    valid_mask,
    norm_gains,
    head_gain,
    conv_weight,
    beta_weight,
    qkv_weight,
    out_weight,
    gate_up_weight,
    down_weight,
    cotangent,
):
    rows = tokens.shape[1]
    dcol, drow = documents(segments[0], rows)
    place = jnp.stack([lax.axis_index("seq"), lax.axis_index("fsdp") % 2]).astype(jnp.int32)
    valid_rows = valid_mask[0].astype(f32)
    near = lambda array: (array, other(array, "fsdp", 1))
    size_qkv, size_out, size_gate = [weight.shape[2] // 4 for weight in (qkv_weight, out_weight, gate_up_weight)]
    sizes_one, sizes_two = (size_qkv, size_out), (size_gate,)
    groups = []
    for at in range(LAYERS):
        groups += [((qkv_weight, out_weight), at), ((gate_up_weight,), at)]
    packs = pack(place, groups[:1], [])
    packs += pack(place, groups[1:], packs)
    blocks, downs = [], []
    for at in range(LAYERS):
        blocks += [gather_chips(packed) for packed in packs[2 * at : 2 * at + 2]]
        downs.append(lax.all_gather(down_weight[at], "fsdp", axis=0, tiled=True))

    def launch(block, after):
        block = gate(block, after) if after else block
        return block, first_round(block)

    def finish(block, over, after):
        near_block = other(block, "fsdp", 1)
        passed, over = relay(*over, [near_block, *after])
        near_over = [other(piece, "fsdp", 1) for piece in over]
        return [block, *over], [near_block, *near_over], second_round(passed), passed

    def complete(came, after):
        own, near_own, passed, _ = came
        passed = [gate(piece, after) if after else piece for piece in passed]
        return [*own, *passed, *near_own, *[other(piece, "fsdp", 1) for piece in passed]]

    stream = tokens[0].astype(f32)
    tail = shifted(tokens[0, rows - HALO :], "seq", 1).astype(f32)
    valid = valid_rows[:, None]
    betas = jnp.pad(beta_weight, ((0, 0), (0, 0), (0, HD - H)))
    gains = lambda at, which: norm_gains[at, which][None]
    square_sums = [jnp.sum(stream * stream * valid, axis=0)[None]]
    normed = root_norm(stream, gains(0, 0)).astype(bf16)
    ready = [tail, betas, normed, dcol, drow, valid, stream, *square_sums]
    parts_one = complete(finish(*launch(blocks[0], []), ready), [])
    coming = launch(blocks[1], parts_one[-2:])
    stored = []
    for at in range(LAYERS):
        normed_one = near(normed)
        projected, logits, qkv_full, out_full = project(
            place, tail, gains(at, 0), normed, betas[at], parts_one, sizes_one, []
        )
        qn, kn, tinv, wu, step, pre, total = fwd_local(
            projected, conv_weight[at], logits, dcol, drow, normed_one[1:]
        )
        partner = other(total, "seq", 1)
        reads, local_out = fwd_read(qn, kn, wu, dcol, drow)
        came = finish(*coming, [reads])
        pair = pair_state(pair_forward_kernel, place, total, partner, after=came[3])
        far = other(pair, "seq", 2)
        state, mixed, attended = fwd_state(
            place, True, [partner], far, pre, reads, local_out, head_gain[at][None], [*came[1], *came[3]]
        )
        parts_two = complete(came, [attended])
        attended = near(attended)
        after_mix, normed, sums = branch(attended[0], out_full, stream, valid, gains(at, 1), False, [], 1)
        normed_two = near(normed)
        more = at + 1 < LAYERS
        if more:
            coming = launch(blocks[2 * at + 2], parts_two[3:5])
        activated, both, gate_up_full = gated(place, normed, parts_two, size_gate, attended[1:])
        passed = []
        if more:
            came = finish(*coming, [activated, *normed_two])
            passed = came[3]
        new_stream, normed, more_sums = branch(
            activated, downs[at], after_mix, valid, gains((at + 1) % LAYERS, 0), not more, passed, 2
        )
        if more:
            parts_one = complete(came, [new_stream])
            tail = shifted(new_stream[rows - HALO :], "seq", 1)
            coming = launch(blocks[2 * at + 3], [*parts_one[-2:], tail])
        square_sums += [sums[:1], more_sums[:1], more_sums[1:]]
        stored.append(
            (
                qkv_full, out_full, gate_up_full, downs[at], stream, normed_one, attended, after_mix,
                normed_two, both, activated, (total, partner), mixed,
                new_stream, (projected, conv_weight[at], logits, dcol, drow, tinv, wu, step, state, reads),
            )
        )
        stream = new_stream
    result = normed
    g = cotangent[0].astype(f32) * valid
    g_low = g.astype(bf16)
    small = []
    waiting = []
    result_qkv, result_out, result_gate = [], [], []
    for at in reversed(range(LAYERS)):
        (
            qkv_full, out_full, gate_up_full, down_full, stream, normed_one, attended, after_mix,
            normed_two, both, activated, states, mixed, leaving, kept,
        ) = stored[at]
        step, reads = kept[7], kept[9]
        started = []
        if waiting:
            grad_down = contract_first(gate(activated, [scattered, waiting[0]]), g_low).astype(bf16)
            own, over_x, over_y, diag_a, diag_b = waiting
            over_x, over_y = merge(over_x, over_y, diag_a, diag_b, [grad_down])
            above = (own, other(over_x, "seq", 1), other(over_y, "seq", 2))
            block, over = gather_start(scattered, [over_x])
            started = [block]
        else:
            grad_down = contract_first(activated, g_low).astype(bf16)
        grad_gate_up = gated_back(g_low, down_full, both, [over_x] if waiting else [grad_down], 2)
        grad_down = lax.psum_scatter(grad_down, "fsdp", scatter_dimension=0, tiled=True)
        grad_gate_up = near(grad_gate_up)
        g, g_low, gain_two = norm_back(
            grad_gate_up[0], gate_up_full, (), after_mix, g, gains(at, 1), started
        )
        branch_low = near(g_low)
        pairs_one = [(normed_two, grad_gate_up)]
        out_pair = (attended, branch_low)
        ready = [gain_two]
        if waiting:
            pairs_one.append(out_pair)
            reduced = total_of(*above, [gain_two])
            above = scatter_chips(reduced)
            ready += [reduced]
        own, over_x, over_y, diag_a, diag_b = grad_pieces(place, pairs_one, ready)
        diag_a, diag_b = other(diag_a, "seq", 1), other(diag_b, "seq", 2)
        done = [own]
        if waiting:
            result_gate, passed = gather_settle(place, block, over, (size_gate,), at + 1, [], [own])
            done += passed
        grad_heads = contract_last(branch_low[0], out_full).astype(bf16)
        grad_mixed, gain_head, total = bwd_local(
            grad_heads, mixed, reads, head_gain[at][None], step, dcol, done
        )
        partner = other(total, "seq", 1)
        fillers = result_gate if waiting else [leaving]
        pair = pair_state(pair_backward_kernel, place, *states, total, partner, after=fillers)
        gives = [partner, other(pair, "seq", 2)]
        over_x, over_y = merge(over_x, over_y, diag_a, diag_b, [gives[1]])
        from_x, from_y = other(over_x, "seq", 1), other(over_y, "seq", 2)
        grad_proj, *parts, grad_logits = bwd_main(
            place, True, states[1:], gives, *kept, grad_mixed,
            [over_x, *branch_low[1:], *([above] if waiting else [])],
        )
        rim = shifted(jnp.concatenate(parts[:3], axis=1), "seq", -1)
        reduced = total_of(own, from_x, from_y, [grad_proj, grad_down])
        scattered = scatter_chips(reduced)
        grad_proj = near(gate(grad_proj, [reduced]).at[rows - HALO :].add(rim))
        grad_beta = contract_first(grad_logits[:, :H], normed_one[0])
        g, g_low, gain_one = norm_back(
            grad_proj[0], qkv_full, (grad_logits, betas[at]), stream, g, gains(at, 0), [reduced]
        )
        pairs_two = [(normed_one, grad_proj)]
        started = [gain_one]
        small += [gain_one, gain_two, gain_head, *parts[3:6], grad_beta]
        if waiting:
            grad_down = gate(grad_down, [reduced])
            grad_down = grad_down + gate(other(grad_down, "seq", 1), [gain_one])
            down_above = down_above + gate(other(gate(down_above, [reduced]), "seq", 2), [gain_one])
            above_far = other(down_above, "seq", 1)
            block, over = gather_start(above, [reduced])
            small += [*square_sums[: 3 * LAYERS], jnp.broadcast_to(jnp.sum(valid_rows), (1, D))]
            packed, starts = small_rows(small)
            started += [grad_down, down_above, packed]
            packed_near = other(packed, "fsdp", 1)
            down_far = other(grad_down, "seq", 2)
        else:
            pairs_two.append(out_pair)
            down_above = grad_down
        own, over_x, over_y, diag_a, diag_b = grad_pieces(place, pairs_two, started)
        if waiting:
            settled, _ = gather_settle(place, block, over, (size_qkv, size_out), at + 1, [], [own])
            result_qkv, result_out = settled
        waiting = own, over_x, over_y, other(diag_a, "seq", 1), other(diag_b, "seq", 2)
    own, over_x, over_y, diag_a, diag_b = waiting
    packed = packed + gate(packed_near, [own])
    packed = packed + other(packed, "fsdp", 2)
    downs = [grad_down + gate(down_far, [own]), down_above + gate(above_far, [own])]
    over_x, over_y = merge(over_x, over_y, diag_a, diag_b, [packed, *downs])
    from_x, from_y = other(over_x, "seq", 1), other(over_y, "seq", 2)
    packed = packed + other(gate(packed, [over_x]), "fsdp", 4)
    reduced = total_of(own, from_x, from_y, [packed])
    last = scatter_chips(reduced)
    packed = sum_over(gate(packed, [reduced]), "seq")
    block, over = gather_start(scattered, [reduced])
    (result_gate, result_out), _ = gather_settle(
        place, block, over, (size_gate, size_out), 0, [*result_gate, result_out], []
    )
    block, over = gather_start(last, [packed, result_gate])
    (result_qkv,), _ = gather_settle(place, block, over, (size_qkv,), 0, [result_qkv], [])
    summed = [small_part(packed, start, array.shape) for start, array in zip(starts, small)]
    of_layer = lambda at: summed[7 * (LAYERS - 1 - at) : 7 * (LAYERS - at)]
    by_layer = lambda pick: jnp.stack([pick(of_layer(at)) for at in range(LAYERS)])
    stats = jnp.concatenate(summed[7 * LAYERS : -1], axis=0)
    count = summed[-1][0, 0]
    rms_stats = jnp.sqrt(jnp.sum(stats, axis=1) / (jnp.maximum(count, 1.0) * D)).reshape(LAYERS, 3)
    return (
        result[None],
        g[None],
        by_layer(lambda arrays: jnp.concatenate(arrays[:2], axis=0)),
        by_layer(lambda arrays: arrays[2][0]),
        by_layer(lambda arrays: jnp.concatenate(arrays[3:6], axis=1)),
        by_layer(lambda arrays: arrays[6].T),
        result_qkv,
        result_out,
        result_gate,
        jnp.stack(downs).astype(f32),
        rms_stats,
    )


def solution(mesh):
    axes = mesh.shape["seq"] == 4 and mesh.shape["fsdp"] == 8
    return jax.shard_map(
        on_device_axes if axes else on_device,
        mesh=mesh,
        in_specs=(
            P("fsdp", "seq", None),
            P("fsdp", None),
            P("fsdp", "seq"),
            P(),
            P(),
            P(),
            P(),
            P(None, "fsdp", None),
            P(None, "fsdp", None),
            P(None, "fsdp", None),
            P(None, "fsdp", None),
            P("fsdp", "seq", None),
        ),
        out_specs=(
            P("fsdp", "seq", None),
            P("fsdp", "seq", None),
            P(),
            P(),
            P(),
            P(),
            P(None, "fsdp", None),
            P(None, "fsdp", None),
            P(None, "fsdp", None),
            P(None, "fsdp", None),
            P(),
        ),
        check_vma=False,
    )
```
